256 devices in a mesh: ctx: 32 (over z, x_lo, core), tp: 8 (over x_hi, y).
Axes of the slice: x: 4 (x_hi: 2, x_lo: 2; x = x_hi * 2 + x_lo), y: 4, z: 8, core: 2. Of those that a mesh axis runs over, the one named last changes fastest.
Arguments:
- projected: bfloat16 [8192, 3, 8192], P('ctx', None, 'tp'), may hold values from -6 to 6
- cotangent: bfloat16 [8192, 8192], P('ctx', 'tp')
- short_filter: float32 [7, 3, 8192], P(None, None, 'tp'), may hold values from -2 to 2
- long_filter: float32 [128, 8192], P(None, 'tp'), may hold values from -0.5 to 0.5
Outputs:
- scaled_grad: bfloat16 [8192, 3, 8192], P('ctx', None, 'tp')
- long_grad: float32 [128, 8192], P('ctx', 'tp')
- short_grad: float32 [7, 3, 8192], P(None, None, 'tp')
- grad_scale: float32 [], replicated
The draws below stay inside these ranges and needn't reach their ends.
All inputs are finite; a program needn't handle non-finite values.
Results may differ from the reference program's by a relative error of at most 0.0017.
Values may be sent and summed in bfloat16 or wider, within the bound.
A program may use at most 128 MiB of HBM per device.

```python
import math
import jax
import jax.numpy as jnp
from jax import lax

D = 8192
FILT = 128
SHORT = 7
TOKENS = 8192


def draw_cotangent(key, part):
    key = jax.random.fold_in(key, 11)
    base_key, column_key = jax.random.split(key)
    position = jnp.arange(TOKENS, dtype=jnp.float32) / TOKENS
    base = jnp.clip(jax.random.normal(base_key, (TOKENS, D), jnp.float32), -6.0, 6.0)
    rising = jnp.exp(position * math.log(10.0))
    spread = jnp.exp(jax.random.uniform(column_key, (D,), jnp.float32, 0.0, math.log(10.0)))
    factor = 0.1 / math.sqrt(TOKENS)
    return (base * rising[:, None] * spread[None, :] * factor).astype(jnp.bfloat16)


def steps_of(own_key, dims, cuts, smallest, top_value):
    gain, own = 1.0, jax.random.fold_in(own_key, 6)
    for dim, blocks in cuts:
        heights = jnp.exp(jax.random.uniform(jax.random.fold_in(own, dim), (blocks,), jnp.float32, smallest / len(cuts), top_value / len(cuts)))
        gain = gain * jnp.repeat(heights, dims[dim] // blocks).reshape([-1 if axis == dim else 1 for axis in range(len(dims))])
    return gain


def normal_values(own_key, shape, deviation, reach, cuts=(), held_as=jnp.bfloat16):
    array = jax.random.normal(own_key, shape, jnp.float32) * deviation
    if len(cuts) > 0:
        array = steps_of(own_key, shape, cuts, -0.22, 0.18) * array
    return jnp.clip(array, min=-reach, max=reach).astype(held_as)


def setup_inputs(seed: int = 0) -> dict:
    seeds = jax.random.split(jax.random.key(seed), 5)
    projected = normal_values(seeds[0], (TOKENS, 3, D), 1.0, 6.0, ((0, 32), (2, 8)))
    cotangent = draw_cotangent(jax.random.fold_in(seeds[4], 71), 0)
    short_filter = normal_values(seeds[2], (SHORT, 3, D), SHORT ** -0.5, 2.0, ((2, 8),), jnp.float32)
    long_filter = normal_values(seeds[3], (FILT, D), FILT ** -0.5, 0.5, ((1, 8),), jnp.float32)
    return dict(projected=projected, cotangent=cotangent, short_filter=short_filter, long_filter=long_filter)


EPSILON = 1e-6
FP8_RANGE = 448.0


def block_grads(inputs, gradient, short_rows, filters):
    length = inputs.shape[0]
    fft_size = 2 * length
    width = filters.shape[1]
    padded = jnp.pad(inputs, ((SHORT - 1, 0), (0, 0)))
    features = short_rows[0] * padded[SHORT - 1:SHORT - 1 + length]
    for offset in range(1, SHORT):
        features = features + short_rows[offset] * padded[SHORT - 1 - offset:SHORT - 1 - offset + length]
    query_part = features[:, :width]
    key_part = features[:, width:2 * width]
    value_part = features[:, 2 * width:]
    product = key_part * value_part
    spectrum_filter = jnp.fft.rfft(filters, n=fft_size, axis=0)
    spectrum_product = jnp.fft.rfft(product, n=fft_size, axis=0)
    filtered = jnp.fft.irfft(spectrum_product * spectrum_filter, n=fft_size, axis=0)[:length]
    d_query = gradient * filtered
    d_filtered = gradient * query_part
    spectrum_grad = jnp.fft.rfft(d_filtered, n=fft_size, axis=0)
    d_product = jnp.fft.irfft(spectrum_grad * jnp.conj(spectrum_filter), n=fft_size, axis=0)[:length]
    long_grad = jnp.fft.irfft(spectrum_grad * jnp.conj(spectrum_product), n=fft_size, axis=0)[:FILT]
    d_features = jnp.concatenate([d_query, d_product * value_part, d_product * key_part], axis=1)
    padded_grad = jnp.pad(d_features, ((0, SHORT - 1), (0, 0)))
    d_input = short_rows[0] * padded_grad[0:length]
    for offset in range(1, SHORT):
        d_input = d_input + short_rows[offset] * padded_grad[offset:offset + length]
    short_grad = jnp.stack([jnp.sum(d_features * padded[SHORT - 1 - offset:SHORT - 1 - offset + length], axis=0) for offset in range(SHORT)])
    return d_input, long_grad, short_grad


def reference(projected, cotangent, short_filter, long_filter):
    block = math.gcd(D, 256)
    count = D // block

    def slices(index):
        start = (index * block).astype(jnp.int32)
        inputs = lax.dynamic_slice_in_dim(projected, start, block, 2).astype(jnp.float32).reshape(TOKENS, 3 * block)
        gradient = lax.dynamic_slice_in_dim(cotangent, start, block, 1).astype(jnp.float32)
        short_rows = lax.dynamic_slice_in_dim(short_filter, start, block, 2).reshape(SHORT, 3 * block)
        filters = lax.dynamic_slice_in_dim(long_filter, start, block, 1)
        return block_grads(inputs, gradient, short_rows, filters)

    def first_pass(index):
        d_input, long_part, short_part = slices(index)
        return jnp.max(jnp.abs(d_input)), long_part, short_part

    indices = jnp.arange(count, dtype=jnp.int32)
    peaks, long_parts, short_parts = lax.map(first_pass, indices)
    peak = jnp.max(peaks)
    factor = FP8_RANGE / (peak + EPSILON)

    def second_pass(index):
        return (slices(index)[0] * factor).astype(jnp.bfloat16)

    scaled_parts = lax.map(second_pass, indices)
    scaled_grad = scaled_parts.reshape(count, TOKENS, 3, block).transpose(1, 2, 0, 3).reshape(TOKENS, 3, D)
    long_grad = long_parts.transpose(1, 0, 2).reshape(FILT, D)
    short_grad = short_parts.reshape(count, SHORT, 3, block).transpose(1, 2, 0, 3).reshape(SHORT, 3, D)
    grad_scale = (peak + EPSILON) / FP8_RANGE
    return (scaled_grad, long_grad, short_grad, grad_scale)
```

```python
import functools

import jax
import jax.numpy as jnp
import ml_dtypes
import numpy as np
from jax import lax
from jax.experimental import pallas as pl
from jax.experimental.pallas import tpu as pltpu
from jax.sharding import PartitionSpec as P

EPSILON = 1e-06
FP8_RANGE = 448.0
MESH = pl.DeviceIdType.MESH

HALF = 208
SIZE = 2 * HALF
EDGE = 144
NEAR = 16
GROUP = 256
TILES = GROUP // 128
SPAN = 392
CHUNK = 56
BLOCKS = HALF // 16
f32 = jnp.float32
bf16 = jnp.bfloat16


def split_np(matrix):
    high = matrix.astype(ml_dtypes.bfloat16)
    low = (matrix - high.astype(np.float64)).astype(ml_dtypes.bfloat16)
    return high, low


def joined_np(matrix):
    high, low = split_np(matrix)
    return np.concatenate([high, high, low], axis=1)


@functools.lru_cache(None)
def transforms():
    m = np.arange(HALF)[None, :]
    k = np.arange(HALF // 2)[:, None]
    even_re = np.cos(2 * np.pi * ((k * m) % HALF) / HALF)
    even_im = -np.sin(2 * np.pi * ((k * m) % HALF) / HALF)
    even_im[0] = np.cos(np.pi * m[0])
    odd_re = np.cos(2 * np.pi * (((2 * k + 1) * m) % SIZE) / SIZE)
    odd_im = -np.sin(2 * np.pi * (((2 * k + 1) * m) % SIZE) / SIZE)

    def blocks(re, im):
        return np.stack([re.reshape(BLOCKS, 8, HALF), im.reshape(BLOCKS, 8, HALF)], axis=1).reshape(HALF, HALF)

    even = blocks(even_re, even_im)
    odd = blocks(odd_re, odd_im)
    weight = np.full((HALF // 2, 1), 2.0 / SIZE)
    first = weight.copy()
    first[0] = 1.0 / SIZE
    back_even = blocks(even_re * first, even_im * first).T
    back_odd = blocks(odd_re * weight, odd_im * weight).T
    c = np.arange(128)
    core, x, z, r = c // 64, (c // 32) % 2, (c // 4) % 8, c % 4
    lag = 128 - ((z * 4 + x * 2 + core) * 4 + r)
    back_lag = np.concatenate([back_even[lag % HALF], back_odd[lag % HALF]], axis=1)
    both = np.concatenate([even, odd], axis=0)
    ahead = np.concatenate([even, -odd], axis=0)[:, 48 : 48 + EDGE]
    return (
        joined_np(even),
        joined_np(odd),
        joined_np(both[:, :128]),
        joined_np(ahead),
        joined_np(back_even),
        joined_np(back_odd),
        joined_np(back_lag),
    )


def split(value):
    high = value.astype(bf16)
    low = (value - high.astype(f32)).astype(bf16)
    return high, low


def dot(a, b):
    return lax.dot_general(a, b, (((1,), (0,)), ((), ())), preferred_element_type=f32)


def halo_kernel(x_ref, g_ref, pkv, pq, nq, ng, nkv, send, recv):
    me = lax.axis_index("ctx")
    count = lax.axis_size("ctx")
    after = lax.rem(me + 1, count)
    before = lax.rem(me + count - 1, count)
    barrier = pltpu.get_barrier_semaphore()
    for other in (after, before):
        pl.semaphore_signal(barrier, inc=1, device_id={"ctx": other}, device_id_type=MESH)
    pl.semaphore_wait(barrier, 2)
    rows = x_ref.shape[1]
    plan = (
        (x_ref.at[pl.ds(1, 2), pl.ds(rows - EDGE, EDGE)], pkv, after),
        (x_ref.at[0, pl.ds(0, EDGE)], nq, before),
        (g_ref.at[pl.ds(0, EDGE)], ng, before),
        (x_ref.at[0, pl.ds(rows - NEAR, NEAR)], pq, after),
        (x_ref.at[pl.ds(1, 2), pl.ds(0, NEAR)], nkv, before),
    )
    copies = []
    for index, (source, target, other) in enumerate(plan):
        copy = pltpu.make_async_remote_copy(
            src_ref=source,
            dst_ref=target,
            send_sem=send.at[index],
            recv_sem=recv.at[index],
            device_id={"ctx": other},
            device_id_type=MESH,
        )
        copy.start()
        copies.append(copy)
    for copy in copies:
        copy.wait()


def halos(x3, cotangent):
    chan = x3.shape[2]
    shapes = [(2, EDGE, chan), (NEAR, chan), (EDGE, chan), (EDGE, chan), (2, NEAR, chan)]
    return pl.pallas_call(
        halo_kernel,
        out_shape=[jax.ShapeDtypeStruct(s, bf16) for s in shapes],
        in_specs=[pl.BlockSpec(memory_space=pl.ANY)] * 2,
        out_specs=[pl.BlockSpec(memory_space=pl.ANY)] * 5,
        scratch_shapes=[pltpu.SemaphoreType.DMA((5,)), pltpu.SemaphoreType.DMA((5,))],
        compiler_params=pltpu.CompilerParams(collective_id=0, has_side_effects=True),
        name="halo_exchange",
    )(x3, cotangent)


def main_kernel(
    x_ref, pkv, pq, nq, ng, nkv, g_ref, sf, lf, fe, fo, fh, fa, be, bo, bl,
    din, lgrad, sgrad, peak,
    xs, gs, kf, vf, ps, ds, hi, lo, sp, sd, sx, sh, er, orr, fil, dpr, df,
):
    me = lax.axis_index("ctx")
    count = lax.axis_size("ctx")
    inner = (me > 0).astype(f32)
    outer = (me < count - 1).astype(f32)

    for t in range(TILES):
        lanes = pl.ds(128 * t, 128)
        xs[0, t, 0:NEAR] = pq[:, lanes].astype(f32) * inner
        xs[0, t, NEAR : NEAR + 256] = x_ref[0, :, lanes].astype(f32)
        xs[0, t, NEAR + 256 : SIZE] = nq[:, lanes].astype(f32)
        for s in (1, 2):
            xs[s, t, 0:EDGE] = pkv[s - 1, :, lanes].astype(f32) * inner
            xs[s, t, EDGE : EDGE + 256] = x_ref[s, :, lanes].astype(f32)
            xs[s, t, EDGE + 256 : SIZE] = nkv[s - 1, :, lanes].astype(f32)
        gs[t, 0:256] = g_ref[:, lanes].astype(f32)
        gs[t, 256 : 256 + EDGE] = ng[:, lanes].astype(f32) * outer
        ps[t, SPAN:SIZE] = jnp.zeros((SIZE - SPAN, 128), f32)
        ds[t, SPAN:SIZE] = jnp.zeros((SIZE - SPAN, 128), f32)

    for t in range(TILES):
        lanes = pl.ds(128 * t, 128)

        def features(c, _, t=t, lanes=lanes):
            base = pl.multiple_of(c * CHUNK, 8)
            parts = []
            for s in range(3):
                total = None
                for i in range(7):
                    term = xs[s, t, pl.ds(base + NEAR - i, CHUNK), :] * sf[s, i : i + 1, lanes]
                    total = term if total is None else total + term
                parts.append(total)
            own = pl.ds(base, CHUNK)
            kf[t, own, :] = parts[1]
            vf[t, own, :] = parts[2]
            ps[t, own, :] = parts[1] * parts[2]
            ds[t, own, :] = parts[0] * gs[t, own, :]
            return 0

        lax.fori_loop(0, SPAN // CHUNK, features, 0)

    def rows_of(ref, start, size):
        return jnp.concatenate([ref[t, start : start + size, :] for t in range(TILES)], axis=1)

    def put(slot, start, value):
        high, low = split(value)
        hi[slot, start : start + value.shape[0], :] = high
        lo[slot, start : start + value.shape[0], :] = low

    def taken(slot, size=HALF):
        high = hi[slot, 0:size, :]
        return jnp.concatenate([high, lo[slot, 0:size, :], high], axis=0)

    for b in range(BLOCKS):
        low_rows, high_rows = rows_of(ps, 16 * b, 16), rows_of(ps, HALF + 16 * b, 16)
        put(0, 16 * b, low_rows + high_rows)
        put(1, 16 * b, low_rows - high_rows)
        low_rows = rows_of(ds, 16 * b, 16)
        if b < 3:
            high_rows = rows_of(ds, HALF + 16 * b, 16)
            put(2, 16 * b, low_rows + high_rows)
            put(3, 16 * b, low_rows - high_rows)
        else:
            put(2, 16 * b, low_rows)
    for b in range(EDGE // 16):
        put(4, 16 * b, rows_of(ds, 256 + 16 * b, 16))
    for b in range(8):
        put(5, 16 * b, lf[16 * b : 16 * b + 16, :])
    hi[3, 48:HALF, :] = hi[2, 48:HALF, :]
    lo[3, 48:HALF, :] = lo[2, 48:HALF, :]
    sh[...] = dot(fh[...], taken(5, 128))
    sp[0:HALF] = dot(fe[...], taken(0))
    sp[HALF:SIZE] = dot(fo[...], taken(1))
    sd[0:HALF] = dot(fe[...], taken(2))
    sd[HALF:SIZE] = dot(fo[...], taken(3))
    sx[...] = sd[...] + dot(fa[...], taken(4, EDGE))

    row = lax.broadcasted_iota(jnp.int32, (8, GROUP), 0)
    for part in range(2):
        for b in range(BLOCKS):
            start = HALF * part + 16 * b

            def pair(ref, start=start):
                return ref[start : start + 8, :], ref[start + 8 : start + 16, :]

            pr, pi = pair(sp)
            hr, him = pair(sh)
            dr, di = pair(sd)
            xr, xi = pair(sx)
            special = part == 0 and b == 0

            def pack(same, cross, re, im, sign, special=special):
                if special:
                    real = re + sign * jnp.where(row == 0, 0.0, same)
                    imag = jnp.where(row == 0, same, im + cross)
                else:
                    real = re + same if sign > 0 else re - same
                    imag = im + cross
                return jnp.concatenate([real, imag], axis=0)

            put(part, 16 * b, pack(pi * him, pi * hr, pr * hr, pr * him, -1.0))
            put(2 + part, 16 * b, pack(xi * him, xi * hr, xr * hr, -(xr * him), 1.0))
            put(4 + part, 16 * b, pack(di * pi, -(di * pr), dr * pr, dr * pi, 1.0))

    high = jnp.concatenate([hi[4, 0:HALF, :], hi[5, 0:HALF, :]], axis=0)
    low = jnp.concatenate([lo[4, 0:HALF, :], lo[5, 0:HALF, :]], axis=0)
    lgrad[...] = dot(bl[...], jnp.concatenate([high, low, high], axis=0))
    er[0] = dot(be[...], taken(0))
    orr[0] = dot(bo[...], taken(1))
    er[1] = dot(be[...], taken(2))
    orr[1] = dot(bo[...], taken(3))

    for t in range(TILES):
        lanes = pl.ds(128 * t, 128)
        fil[t, 0:80, :] = er[0, 128:HALF, lanes] + orr[0, 128:HALF, lanes]
        fil[t, 80:264, :] = er[0, 0:184, lanes] - orr[0, 0:184, lanes]
        dpr[t, 0:HALF, :] = er[1, :, lanes] + orr[1, :, lanes]
        dpr[t, HALF:264, :] = er[1, 0:56, lanes] - orr[1, 0:56, lanes]
        df[0, t, 0:264, :] = gs[t, 0:264, :] * fil[t]
        df[1, t, 0:264, :] = dpr[t] * vf[t, 128:SPAN, :]
        df[2, t, 0:264, :] = dpr[t] * kf[t, 128:SPAN, :]

    top = jnp.zeros((8, 128), f32)
    for t in range(TILES):
        lanes = pl.ds(128 * t, 128)
        for s in range(3):
            shift = NEAR if s == 0 else EDGE

            def step(c, carry, s=s, t=t, lanes=lanes, shift=shift):
                top, sums = carry
                base = pl.multiple_of(c * 64, 8)
                total = None
                for i in range(7):
                    term = df[s, t, pl.ds(base + i, 64), :] * sf[s, i : i + 1, lanes]
                    total = term if total is None else total + term
                din[s, pl.ds(base, 64), lanes] = total
                top = jnp.maximum(top, jnp.max(jnp.abs(total).reshape(8, 8, 128), axis=0))
                own = df[s, t, pl.ds(base, 64), :]
                new = []
                for i in range(7):
                    term = own * xs[s, t, pl.ds(base + shift - i, 64), :]
                    new.append(sums[i] + jnp.sum(term.reshape(8, 8, 128), axis=0))
                return top, tuple(new)

            zero = jnp.zeros((8, 128), f32)
            top, sums = lax.fori_loop(0, 4, step, (top, (zero,) * 7))
            sgrad[s, :, lanes] = jnp.concatenate(
                [jnp.sum(v, axis=0, keepdims=True) for v in sums] + [jnp.zeros((1, 128), f32)], axis=0
            )

    @pl.when(pl.program_id(0) == 0)
    def _():
        peak[...] = top

    @pl.when(pl.program_id(0) > 0)
    def _():
        peak[...] = jnp.maximum(peak[...], top)


def main(x3, halo, cotangent, sf, lf):
    _, rows, chan = x3.shape
    consts = [jnp.asarray(c) for c in transforms()]

    def block(*lead):
        n = len(lead)
        return pl.BlockSpec((*lead, GROUP), lambda i: (0,) * n + (i,))

    whole = [pl.BlockSpec(c.shape, lambda i: (0, 0), pipeline_mode=pl.Buffered(1)) for c in consts]
    return pl.pallas_call(
        main_kernel,
        grid=(chan // GROUP,),
        out_shape=[
            jax.ShapeDtypeStruct((3, rows, chan), f32),
            jax.ShapeDtypeStruct((128, chan), f32),
            jax.ShapeDtypeStruct((3, 8, chan), f32),
            jax.ShapeDtypeStruct((8, 128), f32),
        ],
        in_specs=[
            block(3, rows),
            block(2, EDGE),
            block(NEAR),
            block(EDGE),
            block(EDGE),
            block(2, NEAR),
            block(rows),
            block(3, 7),
            block(128),
            *whole,
        ],
        out_specs=[block(3, rows), block(128), block(3, 8), pl.BlockSpec((8, 128), lambda i: (0, 0))],
        scratch_shapes=[
            pltpu.VMEM((3, TILES, SIZE, 128), f32),
            pltpu.VMEM((TILES, 256 + EDGE, 128), f32),
            pltpu.VMEM((TILES, SPAN, 128), f32),
            pltpu.VMEM((TILES, SPAN, 128), f32),
            pltpu.VMEM((TILES, SIZE, 128), f32),
            pltpu.VMEM((TILES, SIZE, 128), f32),
            pltpu.VMEM((6, HALF, GROUP), bf16),
            pltpu.VMEM((6, HALF, GROUP), bf16),
            pltpu.VMEM((SIZE, GROUP), f32),
            pltpu.VMEM((SIZE, GROUP), f32),
            pltpu.VMEM((SIZE, GROUP), f32),
            pltpu.VMEM((SIZE, GROUP), f32),
            pltpu.VMEM((2, HALF, GROUP), f32),
            pltpu.VMEM((2, HALF, GROUP), f32),
            pltpu.VMEM((TILES, 264, 128), f32),
            pltpu.VMEM((TILES, 264, 128), f32),
            pltpu.VMEM((3, TILES, 272, 128), f32),
        ],
        compiler_params=pltpu.CompilerParams(vmem_limit_bytes=48 * 1024 * 1024),
        name="gradients",
    )(x3, *halo, cotangent, sf, lf, *consts)


def sum_kernel(
    lg_ref, sg_ref, pk_ref, lout, sout, pout,
    lbuf1, lbuf2, zsrc, zbuf, sacc, sbuf1, sbuf2, szbuf, sfin, pbuf1, pbuf2, pbuf3, pone, ptwo,
    send, recv,
):
    c = lax.axis_index("ctx")
    tp = lax.axis_index("tp")
    core = lax.rem(c, 2)
    x = lax.rem(c // 2, 2)
    z = c // 4

    def at(zz, xx, cc):
        return {"ctx": zz * 4 + xx * 2 + cc}

    pair = at(z, x, 1 - core)
    cross = at(z, 1 - x, core)
    diagonal = at(z, 1 - x, 1 - core)
    rings = [at(lax.rem(z + n, 8), x, core) for n in range(1, 8)]
    columns = [{"tp": lax.rem(tp + n, 8)} for n in range(1, 8)]
    barrier = pltpu.get_barrier_semaphore()
    for other in [pair, cross, diagonal, *rings, *columns]:
        pl.semaphore_signal(barrier, inc=1, device_id=other, device_id_type=MESH)
    pl.semaphore_wait(barrier, 17)

    def remote(slot, source, target, other):
        copy = pltpu.make_async_remote_copy(
            src_ref=source,
            dst_ref=target,
            send_sem=send.at[slot],
            recv_sem=recv.at[slot],
            device_id=other,
            device_id_type=MESH,
        )
        copy.start()
        return copy

    tops = [remote(10 + n, pk_ref, pbuf1.at[n], columns[n]) for n in range(7)]
    one = remote(0, lg_ref.at[pl.ds(pl.multiple_of((1 - core) * 64, 64), 64)], lbuf1, pair)
    two = remote(1, sg_ref.at[:, pl.ds(pl.multiple_of((1 - core) * 512, 512), 512)], sbuf1, pair)
    for copy in tops:
        copy.wait()
    top = pk_ref[...]
    for n in range(7):
        top = jnp.maximum(top, pbuf1[n])
    pone[...] = top
    one.wait()
    two.wait()
    lbuf1[...] += lg_ref[pl.ds(pl.multiple_of(core * 64, 64), 64), :]
    sacc[...] = sbuf1[...] + sg_ref[:, pl.ds(pl.multiple_of(core * 512, 512), 512)]

    tops = [remote(20 + n, pone, pbuf2.at[n], rings[n]) for n in range(7)]
    one = remote(2, lbuf1.at[pl.ds(pl.multiple_of((1 - x) * 32, 32), 32)], lbuf2, cross)
    two = remote(3, sacc.at[:, pl.ds(pl.multiple_of((1 - x) * 256, 256), 256)], sbuf2, cross)
    for copy in tops:
        copy.wait()
    for n in range(7):
        top = jnp.maximum(top, pbuf2[n])
    ptwo[...] = top
    tops = [remote(30 + n, ptwo, pbuf3.at[n], other) for n, other in enumerate((pair, cross, diagonal))]
    one.wait()
    two.wait()
    total = lbuf2[...] + lbuf1[pl.ds(pl.multiple_of(x * 32, 32), 32), :]
    for n in range(8):
        zsrc[n] = total[4 * n : 4 * n + 4, :]
    mine = sbuf2[...] + sacc[:, pl.ds(pl.multiple_of(x * 256, 256), 256)]
    sfin[:, pl.ds(pl.multiple_of(x * 256, 256), 256)] = mine

    longs = [remote(40 + n, zsrc.at[lax.rem(z + n + 1, 8)], zbuf.at[n], rings[n]) for n in range(7)]
    half = sfin.at[:, pl.ds(pl.multiple_of(x * 256, 256), 256)]
    shorts = [remote(50 + n, half, szbuf.at[n], rings[n]) for n in range(7)]
    for copy in tops:
        copy.wait()
    for n in range(3):
        top = jnp.maximum(top, pbuf3[n])
    pout[...] = top
    for copy in shorts:
        copy.wait()
    for n in range(7):
        mine += szbuf[n]
    spot = pl.multiple_of(core * 512, 512) + pl.multiple_of(x * 256, 256)
    sout[:, pl.ds(pl.multiple_of(spot, 256), 256)] = mine
    quarter = sout.at[:, pl.ds(pl.multiple_of(spot, 256), 256)]
    lasts = [remote(60 + n, quarter, quarter, other) for n, other in enumerate((pair, cross, diagonal))]
    for copy in longs:
        copy.wait()
    whole = zsrc[z]
    for n in range(7):
        whole += zbuf[n]
    lout[...] = whole
    for copy in lasts:
        copy.wait()


def sums(lgrad, sgrad, peak):
    chan = lgrad.shape[1]
    vmem = pl.BlockSpec(memory_space=pltpu.VMEM)
    return pl.pallas_call(
        sum_kernel,
        out_shape=[
            jax.ShapeDtypeStruct((4, chan), f32),
            jax.ShapeDtypeStruct((24, chan), f32),
            jax.ShapeDtypeStruct((8, 128), f32),
        ],
        in_specs=[vmem] * 3,
        out_specs=[vmem] * 3,
        scratch_shapes=[
            pltpu.VMEM((64, chan), f32),
            pltpu.VMEM((32, chan), f32),
            pltpu.VMEM((8, 4, chan), f32),
            pltpu.VMEM((7, 4, chan), f32),
            pltpu.VMEM((24, chan // 2), f32),
            pltpu.VMEM((24, chan // 2), f32),
            pltpu.VMEM((24, chan // 4), f32),
            pltpu.VMEM((7, 24, chan // 4), f32),
            pltpu.VMEM((24, chan // 2), f32),
            pltpu.VMEM((7, 8, 128), f32),
            pltpu.VMEM((7, 8, 128), f32),
            pltpu.VMEM((3, 8, 128), f32),
            pltpu.VMEM((8, 128), f32),
            pltpu.VMEM((8, 128), f32),
            pltpu.SemaphoreType.DMA((64,)),
            pltpu.SemaphoreType.DMA((64,)),
        ],
        compiler_params=pltpu.CompilerParams(
            collective_id=1, has_side_effects=True, vmem_limit_bytes=16 * 1024 * 1024
        ),
        name="gradient_sums",
    )(lgrad, sgrad, peak)


def scale_kernel(din, peak, out, scale):
    top = jnp.max(peak[...]) + EPSILON
    out[...] = (din[...] * (FP8_RANGE / top)).astype(bf16)
    scale[0, 0] = top / FP8_RANGE


def scaled(din, peak):
    _, rows, chan = din.shape
    return pl.pallas_call(
        scale_kernel,
        grid=(4,),
        out_shape=[jax.ShapeDtypeStruct((3, rows, chan), bf16), jax.ShapeDtypeStruct((1, 1), f32)],
        in_specs=[
            pl.BlockSpec((3, rows // 4, chan), lambda i: (0, i, 0)),
            pl.BlockSpec((8, 128), lambda i: (0, 0)),
        ],
        out_specs=[
            pl.BlockSpec((3, rows // 4, chan), lambda i: (0, i, 0)),
            pl.BlockSpec((1, 1), lambda i: (0, 0), memory_space=pltpu.SMEM),
        ],
        compiler_params=pltpu.CompilerParams(vmem_limit_bytes=32 * 1024 * 1024),
        name="scaling",
    )(din, peak)


def body(projected, cotangent, short_filter, long_filter):
    chan = projected.shape[2]
    x3 = projected.transpose(1, 0, 2)
    sf = short_filter.transpose(1, 0, 2)
    halo = halos(x3, cotangent)
    din, lgrad, sgrad, peak = main(x3, halo, cotangent, sf, long_filter)
    long_grad, short_all, top = sums(lgrad, sgrad.reshape(24, chan), peak)
    out, scale = scaled(din, top)
    short_grad = short_all.reshape(3, 8, chan)[:, :7].transpose(1, 0, 2)
    return out.transpose(1, 0, 2), long_grad, short_grad, scale.reshape(())


def solution(mesh):
    placed = (P("ctx", None, "tp"), P("ctx", "tp"), P(None, None, "tp"), P(None, "tp"))
    return jax.shard_map(
        body,
        mesh=mesh,
        in_specs=placed,
        out_specs=(P("ctx", None, "tp"), P("ctx", "tp"), P(None, None, "tp"), P()),
        check_vma=False,
    )
```

```python
import functools

import jax
import jax.numpy as jnp
import ml_dtypes
import numpy as np
from jax import lax
from jax.experimental import pallas as pl
from jax.experimental.pallas import tpu as pltpu
from jax.sharding import PartitionSpec as P

EPSILON = 1e-06
FP8_RANGE = 448.0
MESH = pl.DeviceIdType.MESH

HALF = 208
SIZE = 2 * HALF
EDGE = 144
NEAR = 16
GROUP = 256
TILES = GROUP // 128
SPAN = 392
CHUNK = 56
BLOCKS = HALF // 16
f32 = jnp.float32
bf16 = jnp.bfloat16


def split_np(matrix):
    high = matrix.astype(ml_dtypes.bfloat16)
    low = (matrix - high.astype(np.float64)).astype(ml_dtypes.bfloat16)
    return high, low


def joined_np(matrix):
    high, low = split_np(matrix)
    return np.concatenate([high, high, low], axis=1)


@functools.lru_cache(None)
def transforms():
    m = np.arange(HALF)[None, :]
    k = np.arange(HALF // 2)[:, None]
    even_re = np.cos(2 * np.pi * ((k * m) % HALF) / HALF)
    even_im = -np.sin(2 * np.pi * ((k * m) % HALF) / HALF)
    even_im[0] = np.cos(np.pi * m[0])
    odd_re = np.cos(2 * np.pi * (((2 * k + 1) * m) % SIZE) / SIZE)
    odd_im = -np.sin(2 * np.pi * (((2 * k + 1) * m) % SIZE) / SIZE)

    def blocks(re, im):
        return np.stack([re.reshape(BLOCKS, 8, HALF), im.reshape(BLOCKS, 8, HALF)], axis=1).reshape(HALF, HALF)

    even = blocks(even_re, even_im)
    odd = blocks(odd_re, odd_im)
    weight = np.full((HALF // 2, 1), 2.0 / SIZE)
    first = weight.copy()
    first[0] = 1.0 / SIZE
    back_even = blocks(even_re * first, even_im * first).T
    back_odd = blocks(odd_re * weight, odd_im * weight).T
    c = np.arange(128)
    core, x, z, r = c // 64, (c // 32) % 2, (c // 4) % 8, c % 4
    lag = 128 - ((z * 4 + x * 2 + core) * 4 + r)
    back_lag = np.concatenate([back_even[lag % HALF], back_odd[lag % HALF]], axis=1)
    both = np.concatenate([even, odd], axis=0)
    ahead = np.concatenate([even, -odd], axis=0)[:, 48 : 48 + EDGE]
    return (
        joined_np(even),
        joined_np(odd),
        joined_np(both[:, :128]),
        joined_np(ahead),
        joined_np(back_even),
        joined_np(back_odd),
        joined_np(back_lag),
    )


def split(value):
    high = value.astype(bf16)
    low = (value - high.astype(f32)).astype(bf16)
    return high, low


def dot(a, b):
    return lax.dot_general(a, b, (((1,), (0,)), ((), ())), preferred_element_type=f32)


def main_kernel(
    x_hbm, g_hbm, sf_hbm, lf_hbm, fe_h, fo_h, fh_h, fa_h, be_h, bo_h, bl_h,
    din_hbm, lout, sout, pout,
    x_own, g_own, pkv, pq, nq, ng, nkv, sf, lf, fe, fo, fh, fa, be, bo, bl,
    xs, gs, kf, vf, ps, ds, hi, lo, sp, sd, sx, sh, er, orr, fil, dpr, df,
    din, lgs, sgs, lb1, sb1, lb2, sb2, zsrc, zbuf, szbuf, pbuf1, pbuf2, pbuf3, pone, ptwo, pthree,
    loads, own, stores, halo_s, halo_r, core_s, core_r, x_s, x_r, epi_s, epi_r,
):
    me = lax.axis_index("ctx")
    count = lax.axis_size("ctx")
    tp = lax.axis_index("tp")
    after = {"ctx": lax.rem(me + 1, count)}
    before = {"ctx": lax.rem(me + count - 1, count)}
    core = lax.rem(me, 2)
    x = lax.rem(me // 2, 2)
    z = me // 4
    hx = tp // 4
    y = lax.rem(tp, 4)
    rows = x_hbm.shape[1]
    groups = x_own.shape[0]

    def at(zz, xx, cc, hh, yy):
        return {"ctx": zz * 4 + xx * 2 + cc, "tp": hh * 4 + yy}

    pair = at(z, x, 1 - core, hx, y)
    cross = at(z, 1 - x, core, hx, y)
    diagonal = at(z, 1 - x, 1 - core, hx, y)
    rings = [at(lax.rem(z + n, 8), x, core, hx, y) for n in range(1, 8)]
    columns = [at(z, x, core, hx, lax.rem(y + n, 4)) for n in range(1, 4)]
    line = [
        at(z, (x + n // 2) % 2, (core + n) % 2, (hx + n // 4) % 2, y) for n in range(1, 8)
    ]
    barrier = pltpu.get_barrier_semaphore()
    for other in [after, before, *line, *columns, *rings]:
        pl.semaphore_signal(barrier, inc=1, device_id=other, device_id_type=MESH)

    def own_copies(i):
        lanes = pl.ds(pl.multiple_of(i * GROUP, GROUP), GROUP)
        return (
            pltpu.make_async_copy(x_hbm.at[:, :, lanes], x_own.at[i], own.at[0, i]),
            pltpu.make_async_copy(g_hbm.at[:, lanes], g_own.at[i], own.at[1, i]),
        )

    def halo_copies(i):
        lanes = pl.ds(pl.multiple_of(i * GROUP, GROUP), GROUP)
        plan = (
            (x_hbm.at[0, pl.ds(rows - NEAR, NEAR), lanes], pq.at[i], after),
            (x_hbm.at[pl.ds(1, 2), pl.ds(0, NEAR), lanes], nkv.at[i], before),
            (x_hbm.at[pl.ds(1, 2), pl.ds(rows - EDGE, EDGE), lanes], pkv.at[i], after),
            (x_hbm.at[0, pl.ds(0, EDGE), lanes], nq.at[i], before),
            (g_hbm.at[pl.ds(0, EDGE), lanes], ng.at[i], before),
        )
        return [
            pltpu.make_async_remote_copy(
                src_ref=source,
                dst_ref=target,
                send_sem=halo_s.at[n, i],
                recv_sem=halo_r.at[n, i],
                device_id=other,
                device_id_type=MESH,
            )
            for n, (source, target, other) in enumerate(plan)
        ]

    consts = [
        pltpu.make_async_copy(source, target, loads.at[n])
        for n, (source, target) in enumerate(
            ((sf_hbm, sf), (lf_hbm, lf), (fe_h, fe), (fo_h, fo), (fh_h, fh), (fa_h, fa), (be_h, be), (bo_h, bo), (bl_h, bl))
        )
    ]
    for copy in own_copies(0):
        copy.start()
    for copy in consts:
        copy.start()
    for i in range(1, groups):
        for copy in own_copies(i):
            copy.start()
    pl.semaphore_wait(barrier, 19)
    for i in range(groups):
        for copy in halo_copies(i):
            copy.start()
    for copy in consts:
        copy.wait()
    inner = (me > 0).astype(f32)
    outer = (me < count - 1).astype(f32)

    def remote(source, target, send, recv, other):
        return pltpu.make_async_remote_copy(
            src_ref=source, dst_ref=target, send_sem=send, recv_sem=recv, device_id=other, device_id_type=MESH
        )

    def core_copies(i):
        lanes = pl.ds(pl.multiple_of((1 - core) * 128, 128), 128)
        return (
            remote(
                lgs.at[i, pl.ds(pl.multiple_of((1 - core) * 64, 64), 64)], lb1.at[i], core_s.at[0, i], core_r.at[0, i], pair
            ),
            remote(sgs.at[i, :, lanes], sb1.at[i], core_s.at[1, i], core_r.at[1, i], pair),
        )

    def x_copies(i):
        return (
            remote(lb1.at[i, pl.ds(pl.multiple_of((1 - x) * 32, 32), 32)], lb2.at[i], x_s.at[i], x_r.at[i], cross),
        )

    def after_core(i):
        for copy in core_copies(i):
            copy.wait()
        lb1[i] = lb1[i] + lgs[i, pl.ds(pl.multiple_of(core * 64, 64), 64), :]
        sb1[i] = sb1[i] + sgs[i, :, pl.ds(pl.multiple_of(core * 128, 128), 128)]
        for copy in x_copies(i):
            copy.start()

    def group(i, top):
        for copy in own_copies(i):
            copy.wait()
        for copy in halo_copies(i):
            copy.wait_recv()
        for t in range(TILES):
            lanes = pl.ds(128 * t, 128)
            xs[0, t, 0:NEAR] = pq[i, :, lanes].astype(f32) * inner
            xs[0, t, NEAR : NEAR + 256] = x_own[i, 0, :, lanes].astype(f32)
            xs[0, t, NEAR + 256 : SIZE] = nq[i, :, lanes].astype(f32)
            for s in (1, 2):
                xs[s, t, 0:EDGE] = pkv[i, s - 1, :, lanes].astype(f32) * inner
                xs[s, t, EDGE : EDGE + 256] = x_own[i, s, :, lanes].astype(f32)
                xs[s, t, EDGE + 256 : SIZE] = nkv[i, s - 1, :, lanes].astype(f32)
            gs[t, 0:256] = g_own[i, :, lanes].astype(f32)
            gs[t, 256 : 256 + EDGE] = ng[i, :, lanes].astype(f32) * outer
            ps[t, SPAN:SIZE] = jnp.zeros((SIZE - SPAN, 128), f32)
            ds[t, SPAN:SIZE] = jnp.zeros((SIZE - SPAN, 128), f32)

        def tap(s, n, t):
            lanes = pl.ds(pl.multiple_of(i * GROUP + 128 * t, 128), 128)
            return sf[s, n : n + 1, lanes]

        for t in range(TILES):

            def features(c, _, t=t):
                base = pl.multiple_of(c * CHUNK, 8)
                parts = []
                for s in range(3):
                    total = None
                    for n in range(7):
                        term = xs[s, t, pl.ds(base + NEAR - n, CHUNK), :] * tap(s, n, t)
                        total = term if total is None else total + term
                    parts.append(total)
                here = pl.ds(base, CHUNK)
                kf[t, here, :] = parts[1]
                vf[t, here, :] = parts[2]
                ps[t, here, :] = parts[1] * parts[2]
                ds[t, here, :] = parts[0] * gs[t, here, :]
                return 0

            lax.fori_loop(0, SPAN // CHUNK, features, 0)

        def rows_of(ref, start, size):
            return jnp.concatenate([ref[t, start : start + size, :] for t in range(TILES)], axis=1)

        def put(slot, start, value):
            high, low = split(value)
            hi[slot, start : start + value.shape[0], :] = high
            lo[slot, start : start + value.shape[0], :] = low

        def taken(slot, size=HALF):
            high = hi[slot, 0:size, :]
            return jnp.concatenate([high, lo[slot, 0:size, :], high], axis=0)

        for b in range(BLOCKS):
            low_rows, high_rows = rows_of(ps, 16 * b, 16), rows_of(ps, HALF + 16 * b, 16)
            put(0, 16 * b, low_rows + high_rows)
            put(1, 16 * b, low_rows - high_rows)
            low_rows = rows_of(ds, 16 * b, 16)
            if b < 3:
                high_rows = rows_of(ds, HALF + 16 * b, 16)
                put(2, 16 * b, low_rows + high_rows)
                put(3, 16 * b, low_rows - high_rows)
            else:
                put(2, 16 * b, low_rows)
        for b in range(EDGE // 16):
            put(4, 16 * b, rows_of(ds, 256 + 16 * b, 16))
        for b in range(8):
            put(5, 16 * b, lf[16 * b : 16 * b + 16, pl.ds(pl.multiple_of(i * GROUP, GROUP), GROUP)])
        hi[3, 48:HALF, :] = hi[2, 48:HALF, :]
        lo[3, 48:HALF, :] = lo[2, 48:HALF, :]
        sh[...] = dot(fh[...], taken(5, 128))
        sp[0:HALF] = dot(fe[...], taken(0))
        sp[HALF:SIZE] = dot(fo[...], taken(1))
        sd[0:HALF] = dot(fe[...], taken(2))
        sd[HALF:SIZE] = dot(fo[...], taken(3))
        sx[...] = sd[...] + dot(fa[...], taken(4, EDGE))

        row = lax.broadcasted_iota(jnp.int32, (8, GROUP), 0)
        for part in range(2):
            for b in range(BLOCKS):
                start = HALF * part + 16 * b

                def two(ref, start=start):
                    return ref[start : start + 8, :], ref[start + 8 : start + 16, :]

                pr, pi = two(sp)
                hr, him = two(sh)
                dr, di = two(sd)
                xr, xi = two(sx)
                special = part == 0 and b == 0

                def pack(same, cross_, re, im, sign, special=special):
                    if special:
                        real = re + sign * jnp.where(row == 0, 0.0, same)
                        imag = jnp.where(row == 0, same, im + cross_)
                    else:
                        real = re + same if sign > 0 else re - same
                        imag = im + cross_
                    return jnp.concatenate([real, imag], axis=0)

                put(part, 16 * b, pack(pi * him, pi * hr, pr * hr, pr * him, -1.0))
                put(2 + part, 16 * b, pack(xi * him, xi * hr, xr * hr, -(xr * him), 1.0))
                put(4 + part, 16 * b, pack(di * pi, -(di * pr), dr * pr, dr * pi, 1.0))

        high = jnp.concatenate([hi[4, 0:HALF, :], hi[5, 0:HALF, :]], axis=0)
        low = jnp.concatenate([lo[4, 0:HALF, :], lo[5, 0:HALF, :]], axis=0)
        lgs[i] = dot(bl[...], jnp.concatenate([high, low, high], axis=0))
        er[0] = dot(be[...], taken(0))
        orr[0] = dot(bo[...], taken(1))
        er[1] = dot(be[...], taken(2))
        orr[1] = dot(bo[...], taken(3))

        for t in range(TILES):
            lanes = pl.ds(128 * t, 128)
            fil[t, 0:80, :] = er[0, 128:HALF, lanes] + orr[0, 128:HALF, lanes]
            fil[t, 80:264, :] = er[0, 0:184, lanes] - orr[0, 0:184, lanes]
            dpr[t, 0:HALF, :] = er[1, :, lanes] + orr[1, :, lanes]
            dpr[t, HALF:264, :] = er[1, 0:56, lanes] - orr[1, 0:56, lanes]
            df[0, t, 0:264, :] = gs[t, 0:264, :] * fil[t]
            df[1, t, 0:264, :] = dpr[t] * vf[t, 128:SPAN, :]
            df[2, t, 0:264, :] = dpr[t] * kf[t, 128:SPAN, :]

        for t in range(TILES):
            lanes = pl.ds(128 * t, 128)
            for s in range(3):
                shift = NEAR if s == 0 else EDGE

                def step(c, carry, s=s, t=t, lanes=lanes, shift=shift):
                    top, sums = carry
                    base = pl.multiple_of(c * 64, 8)
                    total = None
                    for n in range(7):
                        term = df[s, t, pl.ds(base + n, 64), :] * tap(s, n, t)
                        total = term if total is None else total + term
                    din[i, s, pl.ds(base, 64), lanes] = total
                    top = jnp.maximum(top, jnp.max(jnp.abs(total).reshape(8, 8, 128), axis=0))
                    here = df[s, t, pl.ds(base, 64), :]
                    new = []
                    for n in range(7):
                        term = here * xs[s, t, pl.ds(base + shift - n, 64), :]
                        new.append(sums[n] + jnp.sum(term.reshape(8, 8, 128), axis=0))
                    return top, tuple(new)

                zero = jnp.zeros((8, 128), f32)
                top, sums = lax.fori_loop(0, 4, step, (top, (zero,) * 7))
                sgs[i, 8 * s : 8 * s + 8, lanes] = jnp.concatenate(
                    [jnp.sum(v, axis=0, keepdims=True) for v in sums] + [jnp.zeros((1, 128), f32)], axis=0
                )
        din_copy(i).start()
        for copy in core_copies(i):
            copy.start()

        @pl.when(i > 0)
        def _():
            after_core(i - 1)

        return top

    def din_copy(i):
        lanes = pl.ds(pl.multiple_of(i * GROUP, GROUP), GROUP)
        return pltpu.make_async_copy(din.at[i], din_hbm.at[:, :, lanes], stores.at[i])

    top = lax.fori_loop(0, groups, group, jnp.zeros((8, 128), f32))

    pone[...] = top
    tops = [remote(pone, pbuf1.at[n], epi_s.at[n], epi_r.at[n], other) for n, other in enumerate(line)]
    for copy in tops:
        copy.start()
    after_core(groups - 1)
    for copy in tops:
        copy.wait()
    for n in range(7):
        top = jnp.maximum(top, pbuf1[n])
    ptwo[...] = top
    tops = [remote(ptwo, pbuf2.at[n], epi_s.at[7 + n], epi_r.at[7 + n], other) for n, other in enumerate(columns)]
    for copy in tops:
        copy.start()
    half = remote(sb1.at[pl.ds(pl.multiple_of((1 - x) * 2, 2), 2)], sb2, epi_s.at[10], epi_r.at[10], cross)
    half.start()
    for i in range(groups):
        for copy in x_copies(i):
            copy.wait()
        total = lb2[i] + lb1[i, pl.ds(pl.multiple_of(x * 32, 32), 32), :]
        for n in range(8):
            zsrc[n, :, GROUP * i : GROUP * (i + 1)] = total[4 * n : 4 * n + 4, :]
    for copy in tops:
        copy.wait()
    for n in range(3):
        top = jnp.maximum(top, pbuf2[n])
    pthree[...] = top
    tops = [remote(pthree, pbuf3.at[n], epi_s.at[11 + n], epi_r.at[11 + n], other) for n, other in enumerate(rings)]
    for copy in tops:
        copy.start()
    half.wait()
    two_x = pl.ds(pl.multiple_of(x * 2, 2), 2)
    mine = sb2[...] + sb1[two_x]
    sb2[...] = mine
    longs = [
        remote(zsrc.at[lax.rem(z + n + 1, 8)], zbuf.at[n], epi_s.at[18 + n], epi_r.at[18 + n], rings[n]) for n in range(7)
    ]
    shorts = [remote(sb2, szbuf.at[n], epi_s.at[25 + n], epi_r.at[25 + n], rings[n]) for n in range(7)]
    for copy in (*shorts, *longs):
        copy.start()
    for copy in tops:
        copy.wait()
    for n in range(7):
        top = jnp.maximum(top, pbuf3[n])
    pout[...] = top
    for copy in shorts:
        copy.wait()
    for n in range(7):
        mine = mine + szbuf[n]
    sout[core, two_x] = mine
    quarter = sout.at[core, two_x]
    lasts = [
        remote(quarter, quarter, epi_s.at[32 + n], epi_r.at[32 + n], other)
        for n, other in enumerate((pair, cross, diagonal))
    ]
    for copy in lasts:
        copy.start()
    for copy in longs:
        copy.wait()
    whole = zsrc[z]
    for n in range(7):
        whole = whole + zbuf[n]
    lout[...] = whole
    for i in range(groups):
        for copy in halo_copies(i):
            copy.wait_send()
        din_copy(i).wait()
    for copy in lasts:
        copy.wait()


def main(x3, cotangent, sf, lf):
    _, rows, chan = x3.shape
    consts = [jnp.asarray(c) for c in transforms()]
    groups = chan // GROUP
    anywhere = pl.BlockSpec(memory_space=pl.ANY)
    vmem = pl.BlockSpec(memory_space=pltpu.VMEM)
    V = pltpu.VMEM
    D = pltpu.SemaphoreType.DMA
    return pl.pallas_call(
        main_kernel,
        out_shape=[
            jax.ShapeDtypeStruct((3, rows, chan), f32),
            jax.ShapeDtypeStruct((4, chan), f32),
            jax.ShapeDtypeStruct((2, groups, 24, 128), f32),
            jax.ShapeDtypeStruct((8, 128), f32),
        ],
        in_specs=[anywhere] * (4 + len(consts)),
        out_specs=[anywhere, vmem, vmem, vmem],
        scratch_shapes=[
            V((groups, 3, rows, GROUP), bf16),
            V((groups, rows, GROUP), bf16),
            V((groups, 2, EDGE, GROUP), bf16),
            V((groups, NEAR, GROUP), bf16),
            V((groups, EDGE, GROUP), bf16),
            V((groups, EDGE, GROUP), bf16),
            V((groups, 2, NEAR, GROUP), bf16),
            V(sf.shape, f32),
            V(lf.shape, f32),
            *[V(c.shape, bf16) for c in consts],
            V((3, TILES, SIZE, 128), f32),
            V((TILES, 256 + EDGE, 128), f32),
            V((TILES, SPAN, 128), f32),
            V((TILES, SPAN, 128), f32),
            V((TILES, SIZE, 128), f32),
            V((TILES, SIZE, 128), f32),
            V((6, HALF, GROUP), bf16),
            V((6, HALF, GROUP), bf16),
            V((SIZE, GROUP), f32),
            V((SIZE, GROUP), f32),
            V((SIZE, GROUP), f32),
            V((SIZE, GROUP), f32),
            V((2, HALF, GROUP), f32),
            V((2, HALF, GROUP), f32),
            V((TILES, 264, 128), f32),
            V((TILES, 264, 128), f32),
            V((3, TILES, 272, 128), f32),
            V((groups, 3, rows, GROUP), f32),
            V((groups, 128, GROUP), f32),
            V((groups, 24, GROUP), f32),
            V((groups, 64, GROUP), f32),
            V((groups, 24, 128), f32),
            V((groups, 32, GROUP), f32),
            V((groups // 2, 24, 128), f32),
            V((8, 4, chan), f32),
            V((7, 4, chan), f32),
            V((7, groups // 2, 24, 128), f32),
            V((7, 8, 128), f32),
            V((3, 8, 128), f32),
            V((7, 8, 128), f32),
            V((8, 128), f32),
            V((8, 128), f32),
            V((8, 128), f32),
            D((9,)),
            D((2, groups)),
            D((groups,)),
            D((5, groups)),
            D((5, groups)),
            D((2, groups)),
            D((2, groups)),
            D((groups,)),
            D((groups,)),
            D((35,)),
            D((35,)),
        ],
        compiler_params=pltpu.CompilerParams(
            collective_id=0, has_side_effects=True, vmem_limit_bytes=56 * 1024 * 1024
        ),
        name="gradients",
    )(x3, cotangent, sf, lf, *consts)


def scale_kernel(din, peak, out, scale):
    top = jnp.max(peak[...]) + EPSILON
    out[...] = (din[...] * (FP8_RANGE / top)).astype(bf16)
    scale[0, 0] = top / FP8_RANGE


def scaled(din, peak):
    _, rows, chan = din.shape
    return pl.pallas_call(
        scale_kernel,
        grid=(4,),
        out_shape=[jax.ShapeDtypeStruct((3, rows, chan), bf16), jax.ShapeDtypeStruct((1, 1), f32)],
        in_specs=[
            pl.BlockSpec((3, rows // 4, chan), lambda i: (0, i, 0)),
            pl.BlockSpec((8, 128), lambda i: (0, 0)),
        ],
        out_specs=[
            pl.BlockSpec((3, rows // 4, chan), lambda i: (0, i, 0)),
            pl.BlockSpec((1, 1), lambda i: (0, 0), memory_space=pltpu.SMEM),
        ],
        compiler_params=pltpu.CompilerParams(vmem_limit_bytes=56 * 1024 * 1024),
        name="scaling",
    )(din, peak)


def body(projected, cotangent, short_filter, long_filter):
    chan = projected.shape[2]
    x3 = projected.transpose(1, 0, 2)
    sf = short_filter.transpose(1, 0, 2)
    din, long_grad, short_all, top = main(x3, cotangent, sf, long_filter)
    out, scale = scaled(din, top)
    parts = short_all.reshape(2, chan // GROUP, 3, 8, 128)[:, :, :, :7]
    short_grad = parts.transpose(3, 2, 1, 0, 4).reshape(7, 3, chan)
    return out.transpose(1, 0, 2), long_grad, short_grad, scale.reshape(())


def solution(mesh):
    placed = (P("ctx", None, "tp"), P("ctx", "tp"), P(None, None, "tp"), P(None, "tp"))
    return jax.shard_map(
        body,
        mesh=mesh,
        in_specs=placed,
        out_specs=(P("ctx", None, "tp"), P("ctx", "tp"), P(None, None, "tp"), P()),
        check_vma=False,
    )
```

```python
import functools

import jax
import jax.numpy as jnp
import ml_dtypes
import numpy as np
from jax import lax
from jax.experimental import pallas as pl
from jax.experimental.pallas import tpu as pltpu
from jax.sharding import PartitionSpec as P

EPSILON = 1e-06
FP8_RANGE = 448.0
MESH = pl.DeviceIdType.MESH

SIZE = 416
PAIRS = SIZE // 16
EDGE = 144
NEAR = 16
OWN = 240
SPAN = 400
KEEP = 264
GROUP = 256
TILES = GROUP // 128
CHUNK = 48
f32 = jnp.float32
bf16 = jnp.bfloat16


def joined_np(matrix):
    high = matrix.astype(ml_dtypes.bfloat16)
    low = (matrix - high.astype(np.float64)).astype(ml_dtypes.bfloat16)
    return np.concatenate([high, high, low], axis=1)


@functools.lru_cache(None)
def transforms():
    m = np.arange(SIZE)[None, :]
    k = np.arange(SIZE // 2)[:, None]
    re = np.cos(2 * np.pi * ((k * m) % SIZE) / SIZE)
    im = -np.sin(2 * np.pi * ((k * m) % SIZE) / SIZE)
    im[0] = np.cos(np.pi * m[0])
    weight = np.full((SIZE // 2, 1), 2.0 / SIZE)
    weight[0] = 1.0 / SIZE

    def blocks(a, b):
        return np.stack([a.reshape(PAIRS, 8, SIZE), b.reshape(PAIRS, 8, SIZE)], axis=1).reshape(SIZE, SIZE)

    ahead = blocks(re, im)
    back = blocks(re * weight, im * weight).T
    c = np.arange(128)
    core, x, z, r = c // 64, (c // 32) % 2, (c // 4) % 8, c % 4
    lag = 128 - ((z * 4 + x * 2 + core) * 4 + r)
    return (
        joined_np(ahead[:, :128]),
        joined_np(ahead[:, EDGE : EDGE + OWN]),
        joined_np(ahead[:, NEAR : NEAR + OWN]),
        joined_np(np.concatenate([ahead[:, :EDGE], ahead[:, EDGE + OWN : SPAN]], axis=1)),
        joined_np(ahead[:, :NEAR]),
        joined_np(ahead[:, NEAR + OWN : SPAN]),
        joined_np(back[lag]),
        joined_np(back[128 : 128 + KEEP]),
        joined_np(back[:KEEP]),
    )


def split(value):
    high = value.astype(bf16)
    low = (value - high.astype(f32)).astype(bf16)
    return high, low


def dot(a, b):
    return lax.dot_general(a, b, (((1,), (0,)), ((), ())), preferred_element_type=f32)


def main_kernel(
    x_hbm, g_hbm, sf_hbm, lf_hbm, fh_h, fp_h, fd_h, fph_h, fdn_h, fda_h, bl_h, bf_h, bd_h,
    din_hbm, lout, sout, pout,
    x_own, g_own, pkv, pq, nq, ng, nkv, sf, lf, fh, fp, fd, fph, fdn, fda, bl, bf, bd,
    xs, gs, kf, vf, sp, sd, sh, hi, lo, sx, fil, dpr, df,
    din, lgs, sgs, lb1, sb1, lb2, sb2, zsrc, zbuf, pbuf1, pbuf2, pbuf3, pone, ptwo, pthree,
    loads, own, stores, halo_s, halo_r, core_s, core_r, x_s, x_r, z_s, z_r, epi_s, epi_r,
):
    me = lax.axis_index("ctx")
    count = lax.axis_size("ctx")
    tp = lax.axis_index("tp")
    after = {"ctx": lax.rem(me + 1, count)}
    before = {"ctx": lax.rem(me + count - 1, count)}
    core = lax.rem(me, 2)
    x = lax.rem(me // 2, 2)
    z = me // 4
    hx = tp // 4
    y = lax.rem(tp, 4)
    rows = x_hbm.shape[1]
    groups = x_own.shape[0]

    def at(zz, xx, cc, hh, yy):
        return {"ctx": zz * 4 + xx * 2 + cc, "tp": hh * 4 + yy}

    pair = at(z, x, 1 - core, hx, y)
    cross = at(z, 1 - x, core, hx, y)
    rings = [at(lax.rem(z + n, 8), x, core, hx, y) for n in range(1, 8)]
    columns = [at(z, x, core, hx, lax.rem(y + n, 4)) for n in range(1, 4)]
    line = [at(z, (x + n // 2) % 2, (core + n) % 2, (hx + n // 4) % 2, y) for n in range(1, 8)]
    barrier = pltpu.get_barrier_semaphore()
    for other in [*rings, after, before, *columns, *line]:
        pl.semaphore_signal(barrier, inc=1, device_id=other, device_id_type=MESH)

    def lanes_of(i):
        return pl.ds(pl.multiple_of(i * GROUP, GROUP), GROUP)

    def own_copies(i):
        return (
            pltpu.make_async_copy(x_hbm.at[:, :, lanes_of(i)], x_own.at[i], own.at[0, i]),
            pltpu.make_async_copy(g_hbm.at[:, lanes_of(i)], g_own.at[i], own.at[1, i]),
        )

    def remote(source, target, send, recv, other):
        return pltpu.make_async_remote_copy(
            src_ref=source, dst_ref=target, send_sem=send, recv_sem=recv, device_id=other, device_id_type=MESH
        )

    def halo_copies(i):
        lanes = lanes_of(i)
        plan = (
            (x_hbm.at[0, pl.ds(rows - NEAR, NEAR), lanes], pq.at[i], after),
            (x_hbm.at[pl.ds(1, 2), pl.ds(0, NEAR), lanes], nkv.at[i], before),
            (x_hbm.at[pl.ds(1, 2), pl.ds(rows - EDGE, EDGE), lanes], pkv.at[i], after),
            (x_hbm.at[0, pl.ds(0, EDGE), lanes], nq.at[i], before),
            (g_hbm.at[pl.ds(0, EDGE), lanes], ng.at[i], before),
        )
        return [
            remote(source, target, halo_s.at[n, i], halo_r.at[n, i], other)
            for n, (source, target, other) in enumerate(plan)
        ]

    sources = (sf_hbm, lf_hbm, fh_h, fp_h, fd_h, fph_h, fdn_h, fda_h, bl_h, bf_h, bd_h)
    targets = (sf, lf, fh, fp, fd, fph, fdn, fda, bl, bf, bd)
    consts = [pltpu.make_async_copy(a, b, loads.at[n]) for n, (a, b) in enumerate(zip(sources, targets))]
    for copy in consts[:1]:
        copy.start()
    for copy in own_copies(0):
        copy.start()
    for copy in consts[1:5]:
        copy.start()
    for i in range(1, groups):
        for copy in own_copies(i):
            copy.start()
    for copy in consts[5:]:
        copy.start()
    pl.semaphore_wait(barrier, 19)
    for copy in halo_copies(0):
        copy.start()
    for copy in consts[:5]:
        copy.wait()
    inner = (me > 0).astype(f32)
    outer = (me < count - 1).astype(f32)

    def taps(i, t):
        lanes = pl.ds(pl.multiple_of(i * GROUP + 128 * t, 128), 128)
        return lambda s, n: sf[s, n : n + 1, lanes]

    def feature(i, t, s, start, size, tap):
        total = None
        for n in range(7):
            term = xs[i, s, t, pl.ds(start + NEAR - n, size), :] * tap(s, n)
            total = term if total is None else total + term
        return total

    def features(i, t, q_start, kv_start, size, p_slot, p_row, d_slot, d_row, tap):
        lanes = pl.ds(128 * t, 128)
        key = feature(i, t, 1, kv_start, size, tap)
        value = feature(i, t, 2, kv_start, size, tap)
        kf[i, t, pl.ds(kv_start, size), :] = key
        vf[i, t, pl.ds(kv_start, size), :] = value
        high, low = split(key * value)
        hi[p_slot, pl.ds(p_row, size), lanes] = high
        lo[p_slot, pl.ds(p_row, size), lanes] = low
        query = feature(i, t, 0, q_start, size, tap)
        high, low = split(query * gs[i, t, pl.ds(q_start, size), :])
        hi[d_slot, pl.ds(d_row, size), lanes] = high
        lo[d_slot, pl.ds(d_row, size), lanes] = low

    def taken(slot, size):
        high = hi[slot, 0:size, :]
        return jnp.concatenate([high, lo[slot, 0:size, :], high], axis=0)

    def put(slot, start, value):
        high, low = split(value)
        hi[slot, start : start + value.shape[0], :] = high
        lo[slot, start : start + value.shape[0], :] = low

    def local(i, _):
        for copy in own_copies(i):
            copy.wait()
        for t in range(TILES):
            lanes = pl.ds(128 * t, 128)
            xs[i, 0, t, NEAR : NEAR + 256] = x_own[i, 0, :, lanes].astype(f32)
            for s in (1, 2):
                xs[i, s, t, EDGE : EDGE + 256] = x_own[i, s, :, lanes].astype(f32)
            gs[i, t, 0:256] = g_own[i, :, lanes].astype(f32)
        for b in range(8):
            put(2, 16 * b, lf[16 * b : 16 * b + 16, lanes_of(i)])
        sh[i] = dot(fh[...], taken(2, 128))
        for t in range(TILES):
            tap = taps(i, t)

            def step(c, _, t=t, tap=tap):
                row = pl.multiple_of(c * CHUNK, 16)
                features(i, t, NEAR + row, EDGE + row, CHUNK, 0, row, 1, row, tap)
                return 0

            lax.fori_loop(0, OWN // CHUNK, step, 0)
        sp[i] = dot(fp[...], taken(0, OWN))
        sd[i] = dot(fd[...], taken(1, OWN))

        @pl.when(i < groups - 1)
        def _():
            for copy in halo_copies(i + 1):
                copy.start()

        return 0

    lax.fori_loop(0, groups, local, 0)
    for copy in consts[5:]:
        copy.wait()

    def core_copies(i):
        return (
            remote(
                lgs.at[i, pl.ds(pl.multiple_of((1 - core) * 64, 64), 64)], lb1.at[i], core_s.at[0, i], core_r.at[0, i], pair
            ),
            remote(sgs.at[i, 1 - core], sb1.at[i], core_s.at[1, i], core_r.at[1, i], pair),
        )

    def x_copies(i):
        return (
            remote(lb1.at[i, pl.ds(pl.multiple_of((1 - x) * 32, 32), 32)], lb2.at[i], x_s.at[0, i], x_r.at[0, i], cross),
            remote(sb1.at[i], sb2.at[i], x_s.at[1, i], x_r.at[1, i], cross),
        )

    def z_copies(i):
        return [
            remote(zsrc.at[i, lax.rem(z + n + 1, 8)], zbuf.at[i, n], z_s.at[i, n], z_r.at[i, n], rings[n]) for n in range(7)
        ]

    def after_core(i):
        for copy in core_copies(i):
            copy.wait()
        lb1[i] = lb1[i] + lgs[i, pl.ds(pl.multiple_of(core * 64, 64), 64), :]
        sb1[i] = sb1[i] + sgs[i, core]
        for copy in x_copies(i):
            copy.start()

    def after_x(i):
        for copy in x_copies(i):
            copy.wait()
        total = lb2[i] + lb1[i, pl.ds(pl.multiple_of(x * 32, 32), 32), :]
        short = sb2[i] + sb1[i]
        for n in range(8):
            zsrc[i, n, 0:4] = total[4 * n : 4 * n + 4, 0:128]
            zsrc[i, n, 4:8] = total[4 * n : 4 * n + 4, 128:256]
            zsrc[i, n, 8:32] = short
        for copy in z_copies(i):
            copy.start()

    def din_copy(i):
        return pltpu.make_async_copy(din.at[i], din_hbm.at[:, :, lanes_of(i)], stores.at[i])

    def group(i, top):
        for copy in halo_copies(i):
            copy.wait_recv()
        for t in range(TILES):
            lanes = pl.ds(128 * t, 128)
            xs[i, 0, t, 0:NEAR] = pq[i, :, lanes].astype(f32) * inner
            xs[i, 0, t, NEAR + 256 : SIZE] = nq[i, :, lanes].astype(f32)
            for s in (1, 2):
                xs[i, s, t, 0:EDGE] = pkv[i, s - 1, :, lanes].astype(f32) * inner
                xs[i, s, t, EDGE + 256 : SIZE] = nkv[i, s - 1, :, lanes].astype(f32)
            gs[i, t, 256:SPAN] = ng[i, :, lanes].astype(f32) * outer
        for t in range(TILES):
            tap = taps(i, t)

            def step(c, _, t=t, tap=tap):
                row = pl.multiple_of(c * CHUNK, 16)
                features(i, t, 256 + row, row, CHUNK, 0, row, 1, row, tap)
                return 0

            lax.fori_loop(0, EDGE // CHUNK, step, 0)
            features(i, t, 0, EDGE + OWN, NEAR, 0, EDGE, 2, 0, tap)
        sp[i] = sp[i] + dot(fph[...], taken(0, EDGE + NEAR))
        sd[i] = sd[i] + dot(fdn[...], taken(2, NEAR))
        sx[...] = sd[i] + dot(fda[...], taken(1, EDGE))

        row = lax.broadcasted_iota(jnp.int32, (8, GROUP), 0)
        for b in range(PAIRS):

            def two(ref, b=b):
                return ref[16 * b : 16 * b + 8, :], ref[16 * b + 8 : 16 * b + 16, :]

            pr, pi = two(sp.at[i])
            hr, him = two(sh.at[i])
            dr, di = two(sd.at[i])
            xr, xi = two(sx)

            def pack(same, cross_, re, im, sign, special=b == 0):
                if special:
                    real = re + sign * jnp.where(row == 0, 0.0, same)
                    imag = jnp.where(row == 0, same, im + cross_)
                else:
                    real = re + same if sign > 0 else re - same
                    imag = im + cross_
                return jnp.concatenate([real, imag], axis=0)

            put(0, 16 * b, pack(di * pi, -(di * pr), dr * pr, dr * pi, 1.0))
            put(1, 16 * b, pack(pi * him, pi * hr, pr * hr, pr * him, -1.0))
            put(2, 16 * b, pack(xi * him, xi * hr, xr * hr, -(xr * him), 1.0))

        lgs[i] = dot(bl[...], taken(0, SIZE))
        fil[...] = dot(bf[...], taken(1, SIZE))
        dpr[...] = dot(bd[...], taken(2, SIZE))

        for t in range(TILES):
            lanes = pl.ds(128 * t, 128)
            df[0, t, 0:KEEP, :] = gs[i, t, 0:KEEP, :] * fil[:, lanes]
            df[1, t, 0:KEEP, :] = dpr[:, lanes] * vf[i, t, 128 : 128 + KEEP, :]
            df[2, t, 0:KEEP, :] = dpr[:, lanes] * kf[i, t, 128 : 128 + KEEP, :]

        for t in range(TILES):
            lanes = pl.ds(128 * t, 128)
            tap = taps(i, t)
            for s in range(3):
                shift = NEAR if s == 0 else EDGE

                def step(c, carry, s=s, t=t, lanes=lanes, shift=shift, tap=tap):
                    top, sums = carry
                    base = pl.multiple_of(c * 64, 8)
                    total = None
                    for n in range(7):
                        term = df[s, t, pl.ds(base + n, 64), :] * tap(s, n)
                        total = term if total is None else total + term
                    din[i, s, pl.ds(base, 64), lanes] = total
                    top = jnp.maximum(top, jnp.max(jnp.abs(total).reshape(8, 8, 128), axis=0))
                    here = df[s, t, pl.ds(base, 64), :]
                    new = []
                    for n in range(7):
                        term = here * xs[i, s, t, pl.ds(base + shift - n, 64), :]
                        new.append(sums[n] + jnp.sum(term.reshape(8, 8, 128), axis=0))
                    return top, tuple(new)

                zero = jnp.zeros((8, 128), f32)
                top, sums = lax.fori_loop(0, 4, step, (top, (zero,) * 7))
                sgs[i, t, 8 * s : 8 * s + 8] = jnp.concatenate(
                    [jnp.sum(v, axis=0, keepdims=True) for v in sums] + [jnp.zeros((1, 128), f32)], axis=0
                )
        for copy in core_copies(i):
            copy.start()
        din_copy(i).start()

        @pl.when(jnp.logical_and(i > 0, i < groups - 1))
        def _():
            after_core(i - 1)

        @pl.when(jnp.logical_and(i > 1, i < groups - 1))
        def _():
            after_x(i - 2)

        return top

    top = lax.fori_loop(0, groups, group, jnp.zeros((8, 128), f32))

    def spread(source, slots, first, others):
        copies = [remote(source, slots.at[n], epi_s.at[first + n], epi_r.at[first + n], o) for n, o in enumerate(others)]
        for copy in copies:
            copy.start()
        return copies

    def gather(top, copies, slots):
        for copy in copies:
            copy.wait_recv()
        for n in range(len(copies)):
            top = jnp.maximum(top, slots[n])
        return top

    pone[...] = top
    ones = spread(pone, pbuf1, 0, line)
    after_core(groups - 2)
    after_x(groups - 3)
    after_core(groups - 1)
    top = gather(top, ones, pbuf1)
    ptwo[...] = top
    twos = spread(ptwo, pbuf2, 7, columns)
    after_x(groups - 2)
    after_x(groups - 1)
    top = gather(top, twos, pbuf2)
    pthree[...] = top
    threes = spread(pthree, pbuf3, 10, rings)
    for i in range(groups):
        for copy in z_copies(i):
            copy.wait_recv()
        whole = zsrc[i, z]
        for n in range(7):
            whole = whole + zbuf[i, n]
        lout[:, GROUP * i : GROUP * i + 128] = whole[0:4]
        lout[:, GROUP * i + 128 : GROUP * (i + 1)] = whole[4:8]
        sout[core, i] = whole[8:32]
    last = remote(sout.at[core], sout.at[core], epi_s.at[17], epi_r.at[17], pair)
    last.start()
    pout[...] = gather(top, threes, pbuf3)
    for copy in (*ones, *twos, *threes):
        copy.wait_send()
    for i in range(groups):
        for copy in (*halo_copies(i), *z_copies(i)):
            copy.wait_send()
        din_copy(i).wait()
    last.wait()


def main(x3, cotangent, sf, lf):
    _, rows, chan = x3.shape
    consts = [jnp.asarray(c) for c in transforms()]
    groups = chan // GROUP
    anywhere = pl.BlockSpec(memory_space=pl.ANY)
    vmem = pl.BlockSpec(memory_space=pltpu.VMEM)
    V = pltpu.VMEM
    D = pltpu.SemaphoreType.DMA
    return pl.pallas_call(
        main_kernel,
        out_shape=[
            jax.ShapeDtypeStruct((3, rows, chan), f32),
            jax.ShapeDtypeStruct((4, chan), f32),
            jax.ShapeDtypeStruct((2, groups, 24, 128), f32),
            jax.ShapeDtypeStruct((8, 128), f32),
        ],
        in_specs=[anywhere] * (4 + len(consts)),
        out_specs=[anywhere, vmem, vmem, vmem],
        scratch_shapes=[
            V((groups, 3, rows, GROUP), bf16),
            V((groups, rows, GROUP), bf16),
            V((groups, 2, EDGE, GROUP), bf16),
            V((groups, NEAR, GROUP), bf16),
            V((groups, EDGE, GROUP), bf16),
            V((groups, EDGE, GROUP), bf16),
            V((groups, 2, NEAR, GROUP), bf16),
            V(sf.shape, f32),
            V(lf.shape, f32),
            *[V(c.shape, bf16) for c in consts],
            V((groups, 3, TILES, SIZE, 128), f32),
            V((groups, TILES, SPAN, 128), f32),
            V((groups, TILES, SPAN, 128), f32),
            V((groups, TILES, SPAN, 128), f32),
            V((groups, SIZE, GROUP), f32),
            V((groups, SIZE, GROUP), f32),
            V((groups, SIZE, GROUP), f32),
            V((3, SIZE, GROUP), bf16),
            V((3, SIZE, GROUP), bf16),
            V((SIZE, GROUP), f32),
            V((KEEP, GROUP), f32),
            V((KEEP, GROUP), f32),
            V((3, TILES, KEEP + 8, 128), f32),
            V((groups, 3, rows, GROUP), f32),
            V((groups, 128, GROUP), f32),
            V((groups, 2, 24, 128), f32),
            V((groups, 64, GROUP), f32),
            V((groups, 24, 128), f32),
            V((groups, 32, GROUP), f32),
            V((groups, 24, 128), f32),
            V((groups, 8, 32, 128), f32),
            V((groups, 7, 32, 128), f32),
            V((7, 8, 128), f32),
            V((3, 8, 128), f32),
            V((7, 8, 128), f32),
            V((8, 128), f32),
            V((8, 128), f32),
            V((8, 128), f32),
            D((11,)),
            D((2, groups)),
            D((groups,)),
            D((5, groups)),
            D((5, groups)),
            D((2, groups)),
            D((2, groups)),
            D((2, groups)),
            D((2, groups)),
            D((groups, 7)),
            D((groups, 7)),
            D((18,)),
            D((18,)),
        ],
        compiler_params=pltpu.CompilerParams(
            collective_id=0, has_side_effects=True, vmem_limit_bytes=56 * 1024 * 1024
        ),
        name="gradients",
    )(x3, cotangent, sf, lf, *consts)


STEPS = 8


def scale_kernel(din_hbm, lsum, ssum, peak, out_hbm, lout, sout, scale, din, out, loads, stores):
    _, rows, _ = din.shape
    step = rows // STEPS
    ins, outs = [], []
    for n in range(STEPS):
        here = pl.ds(n * step, step)
        ins.append(pltpu.make_async_copy(din_hbm.at[:, here], din.at[:, here], loads.at[n]))
        outs.append(pltpu.make_async_copy(out.at[:, here], out_hbm.at[:, here], stores.at[n]))
        ins[n].start()
    top = jnp.max(peak[...]) + EPSILON
    factor = FP8_RANGE / top
    scale[0, 0] = top / FP8_RANGE
    lout[...] = lsum[...]
    for c in range(2):
        for i in range(ssum.shape[1]):
            start = GROUP * i + 128 * c
            for s in range(3):
                sout[s, :, start : start + 128] = ssum[c, i, 8 * s : 8 * s + 7]
    for n in range(STEPS):
        ins[n].wait()
        here = pl.ds(n * step, step)
        out[:, here] = (din[:, here] * factor).astype(bf16)
        outs[n].start()
    for copy in outs:
        copy.wait()


def scaled(din, lsum, ssum, peak):
    _, rows, chan = din.shape
    vmem = pl.BlockSpec(memory_space=pltpu.VMEM)
    anywhere = pl.BlockSpec(memory_space=pl.ANY)
    return pl.pallas_call(
        scale_kernel,
        out_shape=[
            jax.ShapeDtypeStruct((3, rows, chan), bf16),
            jax.ShapeDtypeStruct((4, chan), f32),
            jax.ShapeDtypeStruct((3, 7, chan), f32),
            jax.ShapeDtypeStruct((1, 1), f32),
        ],
        in_specs=[anywhere, vmem, vmem, vmem],
        out_specs=[anywhere, vmem, vmem, pl.BlockSpec(memory_space=pltpu.SMEM)],
        scratch_shapes=[
            pltpu.VMEM((3, rows, chan), f32),
            pltpu.VMEM((3, rows, chan), bf16),
            pltpu.SemaphoreType.DMA((STEPS,)),
            pltpu.SemaphoreType.DMA((STEPS,)),
        ],
        compiler_params=pltpu.CompilerParams(vmem_limit_bytes=56 * 1024 * 1024),
        name="scaling",
    )(din, lsum, ssum, peak)


def body(projected, cotangent, short_filter, long_filter):
    x3 = projected.transpose(1, 0, 2)
    sf = short_filter.transpose(1, 0, 2)
    out, long_grad, short_grad, scale = scaled(*main(x3, cotangent, sf, long_filter))
    return out.transpose(1, 0, 2), long_grad, short_grad.transpose(1, 0, 2), scale.reshape(())


def solution(mesh):
    placed = (P("ctx", None, "tp"), P("ctx", "tp"), P(None, None, "tp"), P(None, "tp"))
    return jax.shard_map(
        body,
        mesh=mesh,
        in_specs=placed,
        out_specs=(P("ctx", None, "tp"), P("ctx", "tp"), P(None, None, "tp"), P()),
        check_vma=False,
    )
```

```python
import functools

import jax
import jax.numpy as jnp
import ml_dtypes
import numpy as np
from jax import lax
from jax.experimental import pallas as pl
from jax.experimental.pallas import tpu as pltpu
from jax.sharding import PartitionSpec as P

EPSILON = 1e-06
FP8_RANGE = 448.0
MESH = pl.DeviceIdType.MESH

SIZE = 416
PAIRS = SIZE // 16
EDGE = 144
NEAR = 16
FAR = 128
POWER = 11
REACH = 2048.0
LEAST = 1e-30
OWN = 240
SPAN = 400
KEEP = 264
GROUP = 256
TILES = GROUP // 128
CHUNK = 48
f32 = jnp.float32
bf16 = jnp.bfloat16


def joined_np(matrix):
    high = matrix.astype(ml_dtypes.bfloat16)
    low = (matrix - high.astype(np.float64)).astype(ml_dtypes.bfloat16)
    return np.concatenate([high, high, low], axis=1)


@functools.lru_cache(None)
def transforms():
    m = np.arange(SIZE)[None, :]
    k = np.arange(SIZE // 2)[:, None]
    re = np.cos(2 * np.pi * ((k * m) % SIZE) / SIZE)
    im = -np.sin(2 * np.pi * ((k * m) % SIZE) / SIZE)
    im[0] = np.cos(np.pi * m[0])
    weight = np.full((SIZE // 2, 1), 2.0 / SIZE)
    weight[0] = 1.0 / SIZE

    def blocks(a, b):
        return np.stack([a.reshape(PAIRS, 8, SIZE), b.reshape(PAIRS, 8, SIZE)], axis=1).reshape(SIZE, SIZE)

    ahead = blocks(re, im)
    back = blocks(re * weight, im * weight).T
    c = np.arange(128)
    core, x, z, r = c // 64, (c // 32) % 2, (c // 4) % 8, c % 4
    lag = 128 - ((z * 4 + x * 2 + core) * 4 + r)
    return (
        joined_np(ahead[:, :128]),
        joined_np(ahead[:, EDGE : EDGE + OWN]),
        joined_np(ahead[:, NEAR : NEAR + OWN]),
        joined_np(np.concatenate([ahead[:, :EDGE], ahead[:, EDGE + OWN : SPAN]], axis=1)),
        joined_np(ahead[:, :NEAR]),
        joined_np(ahead[:, NEAR + OWN : SPAN]),
        joined_np(back[lag]),
        joined_np(back[128 : 128 + KEEP]),
        joined_np(back[:KEEP]),
    )


def split(value):
    high = value.astype(bf16)
    low = (value - high.astype(f32)).astype(bf16)
    return high, low


def coded(value):
    most = jnp.maximum(jnp.max(jnp.abs(value), axis=0, keepdims=True), LEAST)
    u = value * (REACH / most)
    u2 = u * u
    u4 = u2 * u2
    return ((u4 * u4) * (u2 * u)).astype(bf16), most


def decoded(code, most):
    y = code.astype(f32)
    root = jnp.exp2(jnp.log2(jnp.maximum(jnp.abs(y), 1.2e-38)) * (1.0 / POWER))
    return jnp.where(y < 0, -root, root) * (most * (1.0 / REACH))


def dot(a, b):
    return lax.dot_general(a, b, (((1,), (0,)), ((), ())), preferred_element_type=f32)


def main_kernel(
    x_hbm, g_hbm, sf_hbm, lf_hbm, fh_h, fp_h, fd_h, fph_h, fdn_h, fda_h, bl_h, bf_h, bd_h,
    din, lout, sout, pout,
    x_own, g_own, tail, head, ghead, pcode, dcode, pmost, dmost, pmine, dmine, pmm, dmm, pf, dfil, sf, lf, fh, fp, fd, fph, fdn, fda, bl, bf, bd,
    xs, gs, kf, vf, sp, sd, sh, hi, lo, sx, fil, dpr, df,
    lgs, sgs, lb1, sb1, lb2, sh1, sh2, zsrc, zbuf, pbuf1, pbuf2, pbuf3, pone, ptwo, pthree,
    loads, own, raw_s, raw_r, halo_s, halo_r, core_s, core_r, x_s, x_r, z_s, z_r, epi_s, epi_r,
):
    me = lax.axis_index("ctx")
    count = lax.axis_size("ctx")
    tp = lax.axis_index("tp")
    after = {"ctx": lax.rem(me + 1, count)}
    before = {"ctx": lax.rem(me + count - 1, count)}
    core = lax.rem(me, 2)
    x = lax.rem(me // 2, 2)
    z = me // 4
    hx = tp // 4
    y = lax.rem(tp, 4)
    rows = x_hbm.shape[1]
    groups = x_own.shape[0]

    def at(zz, xx, cc, hh, yy):
        return {"ctx": zz * 4 + xx * 2 + cc, "tp": hh * 4 + yy}

    pair = at(z, x, 1 - core, hx, y)
    cross = at(z, 1 - x, core, hx, y)
    diagonal = at(z, 1 - x, 1 - core, hx, y)
    rings = [at(lax.rem(z + n, 8), x, core, hx, y) for n in range(1, 8)]
    columns = [at(z, x, core, hx, lax.rem(y + n, 4)) for n in range(1, 4)]
    line = [at(z, (x + n // 2) % 2, (core + n) % 2, (hx + n // 4) % 2, y) for n in range(1, 8)]
    barrier = pltpu.get_barrier_semaphore()
    for other in [*rings, after, before, *columns, *line]:
        pl.semaphore_signal(barrier, inc=1, device_id=other, device_id_type=MESH)

    def lanes_of(i):
        return pl.ds(pl.multiple_of(i * GROUP, GROUP), GROUP)

    def own_copies(i):
        return (
            pltpu.make_async_copy(x_hbm.at[:, :, lanes_of(i)], x_own.at[i], own.at[0, i]),
            pltpu.make_async_copy(g_hbm.at[:, lanes_of(i)], g_own.at[i], own.at[1, i]),
        )

    def remote(source, target, send, recv, other):
        return pltpu.make_async_remote_copy(
            src_ref=source, dst_ref=target, send_sem=send, recv_sem=recv, device_id=other, device_id_type=MESH
        )

    def raw_copies():
        plan = (
            (x_hbm.at[:, pl.ds(rows - NEAR, NEAR)], tail, after),
            (x_hbm.at[:, pl.ds(0, NEAR)], head, before),
            (g_hbm.at[pl.ds(0, NEAR)], ghead, before),
        )
        return [remote(a, b, raw_s.at[n], raw_r.at[n], other) for n, (a, b, other) in enumerate(plan)]

    def halo_copies(i):
        plan = (
            (pmine, pcode, after),
            (dmine, dcode, before),
            (pmm, pmost, after),
            (dmm, dmost, before),
        )
        return [
            remote(a.at[i], b.at[i], halo_s.at[n, i], halo_r.at[n, i], other) for n, (a, b, other) in enumerate(plan)
        ]

    sources = (sf_hbm, lf_hbm, fh_h, fp_h, fd_h, fph_h, fdn_h, fda_h, bl_h, bf_h, bd_h)
    targets = (sf, lf, fh, fp, fd, fph, fdn, fda, bl, bf, bd)
    consts = [pltpu.make_async_copy(a, b, loads.at[n]) for n, (a, b) in enumerate(zip(sources, targets))]
    for copy in consts[:1]:
        copy.start()
    for copy in own_copies(0):
        copy.start()
    for copy in consts[1:5]:
        copy.start()
    for i in range(1, groups):
        for copy in own_copies(i):
            copy.start()
    for copy in consts[5:]:
        copy.start()
    for copy in consts[:5]:
        copy.wait()
    inner = (me > 0).astype(f32)
    outer = (me < count - 1).astype(f32)

    def lanes_t(t):
        return pl.ds(128 * t, 128)

    def taps(i, t):
        lanes = pl.ds(pl.multiple_of(i * GROUP + 128 * t, 128), 128)
        return lambda s, n: sf[s, n : n + 1, lanes]

    def feature(i, t, s, start, size, tap):
        total = None
        for n in range(7):
            term = xs[i, s, t, pl.ds(start + NEAR - n, size), :] * tap(s, n)
            total = term if total is None else total + term
        return total

    def features(i, t, q_start, kv_start, size, p_slot, p_row, d_slot, d_row, tap, own_rows=False):
        lanes = pl.ds(128 * t, 128)
        key = feature(i, t, 1, kv_start, size, tap)
        value = feature(i, t, 2, kv_start, size, tap)
        kf[i, t, pl.ds(kv_start, size), :] = key
        vf[i, t, pl.ds(kv_start, size), :] = value
        product = key * value
        if own_rows:
            pf[t, pl.ds(p_row, size), :] = product
        high, low = split(product)
        hi[p_slot, pl.ds(p_row, size), lanes] = high
        lo[p_slot, pl.ds(p_row, size), lanes] = low
        query = feature(i, t, 0, q_start, size, tap)
        gradient = query * gs[i, t, pl.ds(q_start, size), :]
        if own_rows:
            dfil[t, pl.ds(d_row, size), :] = gradient
        high, low = split(gradient)
        hi[d_slot, pl.ds(d_row, size), lanes] = high
        lo[d_slot, pl.ds(d_row, size), lanes] = low

    def taken(slot, size):
        high = hi[slot, 0:size, :]
        return jnp.concatenate([high, lo[slot, 0:size, :], high], axis=0)

    def put(slot, start, value):
        high, low = split(value)
        hi[slot, start : start + value.shape[0], :] = high
        lo[slot, start : start + value.shape[0], :] = low

    def local(i, _, send=True):
        for copy in own_copies(i):
            copy.wait()
        for t in range(TILES):
            lanes = pl.ds(128 * t, 128)
            xs[i, 0, t, NEAR : NEAR + 256] = x_own[i, 0, :, lanes].astype(f32)
            for s in (1, 2):
                xs[i, s, t, EDGE : EDGE + 256] = x_own[i, s, :, lanes].astype(f32)
            gs[i, t, 0:256] = g_own[i, :, lanes].astype(f32)
        for b in range(8):
            put(2, 16 * b, lf[16 * b : 16 * b + 16, lanes_of(i)])
        sh[i] = dot(fh[...], taken(2, 128))
        for t in range(TILES):
            tap = taps(i, t)

            def step(c, _, t=t, tap=tap):
                row = pl.multiple_of(c * CHUNK, 16)
                features(i, t, NEAR + row, EDGE + row, CHUNK, 0, row, 1, row, tap, True)
                return 0

            lax.fori_loop(0, OWN // CHUNK, step, 0)
            pmine[i, :, lanes_t(t)], pmm[i, :, lanes_t(t)] = coded(pf[t, OWN - FAR : OWN, :])
            dmine[i, :, lanes_t(t)], dmm[i, :, lanes_t(t)] = coded(dfil[t, 0:FAR, :])
        if send:
            for copy in halo_copies(i):
                copy.start()
        sp[i] = dot(fp[...], taken(0, OWN))
        sd[i] = dot(fd[...], taken(1, OWN))
        return 0

    local(0, 0, False)
    pl.semaphore_wait(barrier, 19)
    for copy in raw_copies():
        copy.start()
    for copy in halo_copies(0):
        copy.start()
    lax.fori_loop(1, groups, local, 0)
    for copy in raw_copies():
        copy.wait()
    for copy in consts[5:]:
        copy.wait()

    def core_copies(i):
        return (
            remote(
                lgs.at[i, pl.ds(pl.multiple_of((1 - core) * 64, 64), 64)], lb1.at[i], core_s.at[0, i], core_r.at[0, i], pair
            ),
            remote(sgs.at[i, 1 - core], sb1.at[i], core_s.at[1, i], core_r.at[1, i], pair),
        )

    def x_copies(i):
        return (
            remote(lb1.at[i, pl.ds(pl.multiple_of((1 - x) * 32, 32), 32)], lb2.at[i], x_s.at[0, i], x_r.at[0, i], cross),
            remote(sh1.at[i, 1 - x], sh2.at[i], x_s.at[1, i], x_r.at[1, i], cross),
        )

    def z_copies(i):
        return [
            remote(zsrc.at[i, lax.rem(z + n + 1, 8)], zbuf.at[i, n], z_s.at[i, n], z_r.at[i, n], rings[n]) for n in range(7)
        ]

    def after_core(i):
        for copy in core_copies(i):
            copy.wait()
        lb1[i] = lb1[i] + lgs[i, pl.ds(pl.multiple_of(core * 64, 64), 64), :]
        both = sb1[i] + sgs[i, core]
        sh1[i, 0] = both[0:12]
        sh1[i, 1] = both[12:24]
        for copy in x_copies(i):
            copy.start()

    def after_x(i):
        for copy in x_copies(i):
            copy.wait()
        total = lb2[i] + lb1[i, pl.ds(pl.multiple_of(x * 32, 32), 32), :]
        short = sh2[i] + sh1[i, x]
        for n in range(8):
            zsrc[i, n, 0:4] = total[4 * n : 4 * n + 4, 0:128]
            zsrc[i, n, 4:8] = total[4 * n : 4 * n + 4, 128:256]
            zsrc[i, n, 8:20] = short
        for copy in z_copies(i):
            copy.start()

    def group(i, top):
        for copy in halo_copies(i):
            copy.wait_recv()
        for t in range(TILES):
            wide = pl.ds(pl.multiple_of(i * GROUP + 128 * t, 128), 128)
            lanes = lanes_t(t)
            tap = taps(i, t)
            xs[i, 0, t, 0:NEAR] = tail[0, :, wide].astype(f32) * inner
            xs[i, 0, t, NEAR + 256 : 2 * NEAR + 256] = head[0, :, wide].astype(f32)
            for s in (1, 2):
                xs[i, s, t, FAR:EDGE] = tail[s, :, wide].astype(f32) * inner
                xs[i, s, t, EDGE + 256 : SIZE] = head[s, :, wide].astype(f32)
            gs[i, t, 256 : 256 + NEAR] = ghead[:, wide].astype(f32) * outer
            for c in range(0, FAR, 32):
                high, low = split(decoded(pcode[i, c : c + 32, lanes], pmost[i, :, lanes] * inner))
                hi[0, c : c + 32, lanes] = high
                lo[0, c : c + 32, lanes] = low
                high, low = split(decoded(dcode[i, c : c + 32, lanes], dmost[i, :, lanes] * outer))
                hi[1, NEAR + c : NEAR + c + 32, lanes] = high
                lo[1, NEAR + c : NEAR + c + 32, lanes] = low
            features(i, t, 0, FAR, NEAR, 0, FAR, 2, 0, tap)
            features(i, t, 256, EDGE + OWN, NEAR, 0, EDGE, 1, 0, tap)
        sp[i] = sp[i] + dot(fph[...], taken(0, EDGE + NEAR))
        sd[i] = sd[i] + dot(fdn[...], taken(2, NEAR))
        sx[...] = sd[i] + dot(fda[...], taken(1, EDGE))

        row = lax.broadcasted_iota(jnp.int32, (8, GROUP), 0)
        for b in range(PAIRS):

            def two(ref, b=b):
                return ref[16 * b : 16 * b + 8, :], ref[16 * b + 8 : 16 * b + 16, :]

            pr, pi = two(sp.at[i])
            hr, him = two(sh.at[i])
            dr, di = two(sd.at[i])
            xr, xi = two(sx)

            def pack(same, cross_, re, im, sign, special=b == 0):
                if special:
                    real = re + sign * jnp.where(row == 0, 0.0, same)
                    imag = jnp.where(row == 0, same, im + cross_)
                else:
                    real = re + same if sign > 0 else re - same
                    imag = im + cross_
                return jnp.concatenate([real, imag], axis=0)

            put(0, 16 * b, pack(di * pi, -(di * pr), dr * pr, dr * pi, 1.0))
            put(1, 16 * b, pack(pi * him, pi * hr, pr * hr, pr * him, -1.0))
            put(2, 16 * b, pack(xi * him, xi * hr, xr * hr, -(xr * him), 1.0))

        lgs[i] = dot(bl[...], taken(0, SIZE))
        fil[...] = dot(bf[...], taken(1, SIZE))
        dpr[...] = dot(bd[...], taken(2, SIZE))

        for t in range(TILES):
            lanes = pl.ds(128 * t, 128)
            df[0, t, 0:KEEP, :] = gs[i, t, 0:KEEP, :] * fil[:, lanes]
            df[1, t, 0:KEEP, :] = dpr[:, lanes] * vf[i, t, 128 : 128 + KEEP, :]
            df[2, t, 0:KEEP, :] = dpr[:, lanes] * kf[i, t, 128 : 128 + KEEP, :]

        for t in range(TILES):
            lanes = pl.ds(128 * t, 128)
            tap = taps(i, t)
            for s in range(3):
                shift = NEAR if s == 0 else EDGE

                def step(c, carry, s=s, t=t, lanes=lanes, shift=shift, tap=tap):
                    top, sums = carry
                    base = pl.multiple_of(c * 64, 8)
                    total = None
                    for n in range(7):
                        term = df[s, t, pl.ds(base + n, 64), :] * tap(s, n)
                        total = term if total is None else total + term
                    din[i, s, pl.ds(base, 64), lanes] = total
                    top = jnp.maximum(top, jnp.max(jnp.abs(total).reshape(8, 8, 128), axis=0))
                    here = df[s, t, pl.ds(base, 64), :]
                    new = []
                    for n in range(7):
                        term = here * xs[i, s, t, pl.ds(base + shift - n, 64), :]
                        new.append(sums[n] + jnp.sum(term.reshape(8, 8, 128), axis=0))
                    return top, tuple(new)

                zero = jnp.zeros((8, 128), f32)
                top, sums = lax.fori_loop(0, 4, step, (top, (zero,) * 7))
                sgs[i, t, 8 * s : 8 * s + 8] = jnp.concatenate(
                    [jnp.sum(v, axis=0, keepdims=True) for v in sums] + [jnp.zeros((1, 128), f32)], axis=0
                )
        for copy in core_copies(i):
            copy.start()

        @pl.when(jnp.logical_and(i > 0, i < groups - 1))
        def _():
            after_core(i - 1)

        @pl.when(jnp.logical_and(i > 1, i < groups - 1))
        def _():
            after_x(i - 2)

        return top

    top = lax.fori_loop(0, groups, group, jnp.zeros((8, 128), f32))

    def spread(source, slots, first, others):
        copies = [remote(source, slots.at[n], epi_s.at[first + n], epi_r.at[first + n], o) for n, o in enumerate(others)]
        for copy in copies:
            copy.start()
        return copies

    def gather(top, copies, slots):
        for copy in copies:
            copy.wait_recv()
        for n in range(len(copies)):
            top = jnp.maximum(top, slots[n])
        return top

    pone[...] = top
    ones = spread(pone, pbuf1, 0, line)
    after_core(groups - 2)
    after_x(groups - 3)
    after_core(groups - 1)
    top = gather(top, ones, pbuf1)
    ptwo[...] = top
    twos = spread(ptwo, pbuf2, 7, columns)
    after_x(groups - 2)
    after_x(groups - 1)
    top = gather(top, twos, pbuf2)
    pthree[...] = top
    threes = spread(pthree, pbuf3, 10, rings)
    for i in range(groups):
        for copy in z_copies(i):
            copy.wait_recv()
        whole = zsrc[i, z]
        for n in range(7):
            whole = whole + zbuf[i, n]
        lout[:, GROUP * i : GROUP * i + 128] = whole[0:4]
        lout[:, GROUP * i + 128 : GROUP * (i + 1)] = whole[4:8]
        sout[core, x, i] = whole[8:20]
    quarter = sout.at[core, x]
    lasts = [
        remote(quarter, quarter, epi_s.at[17 + n], epi_r.at[17 + n], o) for n, o in enumerate((pair, cross, diagonal))
    ]
    for copy in lasts:
        copy.start()
    pout[...] = gather(top, threes, pbuf3)
    for copy in (*ones, *twos, *threes):
        copy.wait_send()
    for i in range(groups):
        for copy in (*halo_copies(i), *z_copies(i)):
            copy.wait_send()
    for copy in lasts:
        copy.wait()


def main(x3, cotangent, sf, lf):
    _, rows, chan = x3.shape
    consts = [jnp.asarray(c) for c in transforms()]
    groups = chan // GROUP
    anywhere = pl.BlockSpec(memory_space=pl.ANY)
    vmem = pl.BlockSpec(memory_space=pltpu.VMEM)
    V = pltpu.VMEM
    D = pltpu.SemaphoreType.DMA
    return pl.pallas_call(
        main_kernel,
        out_shape=[
            V((groups, 3, rows, GROUP), f32),
            jax.ShapeDtypeStruct((4, chan), f32),
            jax.ShapeDtypeStruct((2, 2, groups, 12, 128), f32),
            jax.ShapeDtypeStruct((8, 128), f32),
        ],
        in_specs=[anywhere] * (4 + len(consts)),
        out_specs=[vmem, vmem, vmem, vmem],
        scratch_shapes=[
            V((groups, 3, rows, GROUP), bf16),
            V((groups, rows, GROUP), bf16),
            V((3, NEAR, chan), bf16),
            V((3, NEAR, chan), bf16),
            V((NEAR, chan), bf16),
            V((groups, FAR, GROUP), bf16),
            V((groups, FAR, GROUP), bf16),
            V((groups, 1, GROUP), f32),
            V((groups, 1, GROUP), f32),
            V((groups, FAR, GROUP), bf16),
            V((groups, FAR, GROUP), bf16),
            V((groups, 1, GROUP), f32),
            V((groups, 1, GROUP), f32),
            V((TILES, OWN, 128), f32),
            V((TILES, OWN, 128), f32),
            V(sf.shape, f32),
            V(lf.shape, f32),
            *[V(c.shape, bf16) for c in consts],
            V((groups, 3, TILES, SIZE, 128), f32),
            V((groups, TILES, SPAN, 128), f32),
            V((groups, TILES, SPAN, 128), f32),
            V((groups, TILES, SPAN, 128), f32),
            V((groups, SIZE, GROUP), f32),
            V((groups, SIZE, GROUP), f32),
            V((groups, SIZE, GROUP), f32),
            V((3, SIZE, GROUP), bf16),
            V((3, SIZE, GROUP), bf16),
            V((SIZE, GROUP), f32),
            V((KEEP, GROUP), f32),
            V((KEEP, GROUP), f32),
            V((3, TILES, KEEP + 8, 128), f32),
            V((groups, 128, GROUP), f32),
            V((groups, 2, 24, 128), f32),
            V((groups, 64, GROUP), f32),
            V((groups, 24, 128), f32),
            V((groups, 32, GROUP), f32),
            V((groups, 2, 12, 128), f32),
            V((groups, 12, 128), f32),
            V((groups, 8, 20, 128), f32),
            V((groups, 7, 20, 128), f32),
            V((7, 8, 128), f32),
            V((3, 8, 128), f32),
            V((7, 8, 128), f32),
            V((8, 128), f32),
            V((8, 128), f32),
            V((8, 128), f32),
            D((11,)),
            D((2, groups)),
            D((3,)),
            D((3,)),
            D((4, groups)),
            D((4, groups)),
            D((2, groups)),
            D((2, groups)),
            D((2, groups)),
            D((2, groups)),
            D((groups, 7)),
            D((groups, 7)),
            D((20,)),
            D((20,)),
        ],
        compiler_params=pltpu.CompilerParams(
            collective_id=0, has_side_effects=True, vmem_limit_bytes=56 * 1024 * 1024
        ),
        name="gradients",
    )(x3, cotangent, sf, lf, *consts)


STEPS = 2


def scale_kernel(din, lsum, ssum, peak, out_hbm, lout, sout, scale, out, stores):
    groups, streams, rows, _ = din.shape
    step = rows // STEPS
    top = jnp.max(peak[...]) + EPSILON
    factor = FP8_RANGE / top
    copies = []
    for s in range(streams):
        for n in range(STEPS):
            here = pl.ds(n * step, step)
            for i in range(groups):
                out[s, here, GROUP * i : GROUP * (i + 1)] = (din[i, s, here, :] * factor).astype(bf16)
            copies.append(pltpu.make_async_copy(out.at[s, here], out_hbm.at[s, here], stores.at[s * STEPS + n]))
            copies[-1].start()
    scale[0, 0] = top / FP8_RANGE
    lout[...] = lsum[...]
    for c in range(2):
        for i in range(groups):
            lanes = pl.ds(GROUP * i + 128 * c, 128)
            sout[0, :, lanes] = ssum[c, 0, i, 0:7]
            sout[1, 0:4, lanes] = ssum[c, 0, i, 8:12]
            sout[1, 4:7, lanes] = ssum[c, 1, i, 0:3]
            sout[2, :, lanes] = ssum[c, 1, i, 4:11]
    for copy in copies:
        copy.wait()


def scaled(din, lsum, ssum, peak):
    groups, _, rows, _ = din.shape
    chan = groups * GROUP
    vmem = pl.BlockSpec(memory_space=pltpu.VMEM)
    anywhere = pl.BlockSpec(memory_space=pl.ANY)
    din = pltpu.with_memory_space_constraint(din, pltpu.VMEM)
    return pl.pallas_call(
        scale_kernel,
        out_shape=[
            jax.ShapeDtypeStruct((3, rows, chan), bf16),
            jax.ShapeDtypeStruct((4, chan), f32),
            jax.ShapeDtypeStruct((3, 7, chan), f32),
            jax.ShapeDtypeStruct((1, 1), f32),
        ],
        in_specs=[vmem, vmem, vmem, vmem],
        out_specs=[anywhere, vmem, vmem, pl.BlockSpec(memory_space=pltpu.SMEM)],
        scratch_shapes=[pltpu.VMEM((3, rows, chan), bf16), pltpu.SemaphoreType.DMA((3 * STEPS,))],
        compiler_params=pltpu.CompilerParams(vmem_limit_bytes=32 * 1024 * 1024),
        name="scaling",
    )(din, lsum, ssum, peak)


def body(projected, cotangent, short_filter, long_filter):
    x3 = projected.transpose(1, 0, 2)
    sf = short_filter.transpose(1, 0, 2)
    out, long_grad, short_grad, scale = scaled(*main(x3, cotangent, sf, long_filter))
    return out.transpose(1, 0, 2), long_grad, short_grad.transpose(1, 0, 2), scale.reshape(())


def solution(mesh):
    placed = (P("ctx", None, "tp"), P("ctx", "tp"), P(None, None, "tp"), P(None, "tp"))
    return jax.shard_map(
        body,
        mesh=mesh,
        in_specs=placed,
        out_specs=(P("ctx", None, "tp"), P("ctx", "tp"), P(None, None, "tp"), P()),
        check_vma=False,
    )
```

```python
import functools

import jax
import jax.numpy as jnp
import ml_dtypes
import numpy as np
from jax import lax
from jax.experimental import pallas as pl
from jax.experimental.pallas import tpu as pltpu
from jax.sharding import PartitionSpec as P

EPSILON = 1e-06
FP8_RANGE = 448.0
MESH = pl.DeviceIdType.MESH

SIZE = 416
PAIRS = SIZE // 16
EDGE = 144
NEAR = 16
FAR = 128
POWER = 11
REACH = 2048.0
LEAST = 1e-30
OWN = 240
SPAN = 400
KEEP = 264
GROUP = 256
TILES = GROUP // 128
CHUNK = 48
f32 = jnp.float32
bf16 = jnp.bfloat16


def joined_np(matrix):
    high = matrix.astype(ml_dtypes.bfloat16)
    low = (matrix - high.astype(np.float64)).astype(ml_dtypes.bfloat16)
    return np.concatenate([high, high, low], axis=1)


@functools.lru_cache(None)
def transforms():
    m = np.arange(SIZE)[None, :]
    k = np.arange(SIZE // 2)[:, None]
    re = np.cos(2 * np.pi * ((k * m) % SIZE) / SIZE)
    im = -np.sin(2 * np.pi * ((k * m) % SIZE) / SIZE)
    im[0] = np.cos(np.pi * m[0])
    weight = np.full((SIZE // 2, 1), 2.0 / SIZE)
    weight[0] = 1.0 / SIZE

    def blocks(a, b):
        return np.stack([a.reshape(PAIRS, 8, SIZE), b.reshape(PAIRS, 8, SIZE)], axis=1).reshape(SIZE, SIZE)

    ahead = blocks(re, im)
    back = blocks(re * weight, im * weight).T
    c = np.arange(128)
    core, x, z, r = c // 64, (c // 32) % 2, (c // 4) % 8, c % 4
    lag = 128 - ((z * 4 + x * 2 + core) * 4 + r)
    return (
        joined_np(ahead[:, :128]),
        joined_np(ahead[:, EDGE : EDGE + OWN]),
        joined_np(ahead[:, NEAR : NEAR + OWN]),
        joined_np(np.concatenate([ahead[:, :EDGE], ahead[:, EDGE + OWN : SPAN]], axis=1)),
        joined_np(ahead[:, :NEAR]),
        joined_np(ahead[:, NEAR + OWN : SPAN]),
        joined_np(back[lag]),
        joined_np(back[128 : 128 + KEEP]),
        joined_np(back[:KEEP]),
    )


def split(value):
    high = value.astype(bf16)
    low = (value - high.astype(f32)).astype(bf16)
    return high, low


def coded(value):
    most = jnp.maximum(jnp.max(jnp.abs(value), axis=0, keepdims=True), LEAST)
    u = value * (REACH / most)
    u2 = u * u
    u4 = u2 * u2
    return ((u4 * u4) * (u2 * u)).astype(bf16), most


def decoded(code, most):
    y = code.astype(f32)
    root = jnp.exp2(jnp.log2(jnp.maximum(jnp.abs(y), 1.2e-38)) * (1.0 / POWER))
    return jnp.where(y < 0, -root, root) * (most * (1.0 / REACH))


def dot(a, b):
    return lax.dot_general(a, b, (((1,), (0,)), ((), ())), preferred_element_type=f32)


def main_kernel(
    x_hbm, g_hbm, sf_hbm, lf_hbm, fh_h, fp_h, fd_h, fph_h, fdn_h, fda_h, bl_h, bf_h, bd_h,
    din, lout, sout, pout,
    x_own, g_own, tail, head, ghead, pcode, dcode, pmost, dmost, pmine, dmine, pmm, dmm, pf, dfil, sf, lf, fh, fp, fd, fph, fdn, fda, bl, bf, bd,
    xs, gs, kf, vf, sp, sd, sh, ohi, olo, hi, lo, sx, fil, dpr, df,
    quart, qbuf, zsrc, zbuf, pbuf1, pbuf2, pbuf3, pone, ptwo, pthree,
    loads, own, raw_s, raw_r, halo_s, halo_r, line_s, line_r, z_s, z_r, epi_s, epi_r,
):
    me = lax.axis_index("ctx")
    count = lax.axis_size("ctx")
    tp = lax.axis_index("tp")
    after = {"ctx": lax.rem(me + 1, count)}
    before = {"ctx": lax.rem(me + count - 1, count)}
    core = lax.rem(me, 2)
    x = lax.rem(me // 2, 2)
    z = me // 4
    hx = tp // 4
    y = lax.rem(tp, 4)
    rows = x_hbm.shape[1]
    groups = x_own.shape[0]

    def at(zz, xx, cc, hh, yy):
        return {"ctx": zz * 4 + xx * 2 + cc, "tp": hh * 4 + yy}

    pair = at(z, x, 1 - core, hx, y)
    cross = at(z, 1 - x, core, hx, y)
    diagonal = at(z, 1 - x, 1 - core, hx, y)
    rings = [at(lax.rem(z + n, 8), x, core, hx, y) for n in range(1, 8)]
    columns = [at(z, x, core, hx, lax.rem(y + n, 4)) for n in range(1, 4)]
    line = [at(z, (x + n // 2) % 2, (core + n) % 2, (hx + n // 4) % 2, y) for n in range(1, 8)]
    barrier = pltpu.get_barrier_semaphore()
    for other in [*rings, after, before, *columns, *line]:
        pl.semaphore_signal(barrier, inc=1, device_id=other, device_id_type=MESH)

    def lanes_of(i):
        return pl.ds(pl.multiple_of(i * GROUP, GROUP), GROUP)

    def own_copies(i):
        return (
            pltpu.make_async_copy(x_hbm.at[:, :, lanes_of(i)], x_own.at[i], own.at[0, i]),
            pltpu.make_async_copy(g_hbm.at[:, lanes_of(i)], g_own.at[i], own.at[1, i]),
        )

    def remote(source, target, send, recv, other):
        return pltpu.make_async_remote_copy(
            src_ref=source, dst_ref=target, send_sem=send, recv_sem=recv, device_id=other, device_id_type=MESH
        )

    def raw_copies():
        plan = (
            (x_hbm.at[:, pl.ds(rows - NEAR, NEAR)], tail, after),
            (x_hbm.at[:, pl.ds(0, NEAR)], head, before),
            (g_hbm.at[pl.ds(0, NEAR)], ghead, before),
        )
        return [remote(a, b, raw_s.at[n], raw_r.at[n], other) for n, (a, b, other) in enumerate(plan)]

    def halo_copies(i):
        plan = (
            (pmine, pcode, after),
            (dmine, dcode, before),
            (pmm, pmost, after),
            (dmm, dmost, before),
        )
        return [
            remote(a.at[i], b.at[i], halo_s.at[n, i], halo_r.at[n, i], other) for n, (a, b, other) in enumerate(plan)
        ]

    sources = (sf_hbm, lf_hbm, fh_h, fp_h, fd_h, fph_h, fdn_h, fda_h, bl_h, bf_h, bd_h)
    targets = (sf, lf, fh, fp, fd, fph, fdn, fda, bl, bf, bd)
    consts = [pltpu.make_async_copy(a, b, loads.at[n]) for n, (a, b) in enumerate(zip(sources, targets))]
    for copy in consts[:1]:
        copy.start()
    for copy in own_copies(0):
        copy.start()
    for copy in consts[1:5]:
        copy.start()
    for i in range(1, groups):
        for copy in own_copies(i):
            copy.start()
    for copy in consts[5:]:
        copy.start()
    for copy in consts[:5]:
        copy.wait()
    inner = (me > 0).astype(f32)
    outer = (me < count - 1).astype(f32)

    def lanes_t(t):
        return pl.ds(128 * t, 128)

    def taps(i, t):
        lanes = pl.ds(pl.multiple_of(i * GROUP + 128 * t, 128), 128)
        return lambda s, n: sf[s, n : n + 1, lanes]

    def feature(i, t, s, start, size, tap):
        total = None
        for n in range(7):
            term = xs[i, s, t, pl.ds(start + NEAR - n, size), :] * tap(s, n)
            total = term if total is None else total + term
        return total

    def features(i, t, q_start, kv_start, size, p_slot, p_row, d_slot, d_row, tap, own_rows=False):
        lanes = pl.ds(128 * t, 128)
        p_hi, p_lo = p_slot
        d_hi, d_lo = d_slot
        key = feature(i, t, 1, kv_start, size, tap)
        value = feature(i, t, 2, kv_start, size, tap)
        kf[i, t, pl.ds(kv_start, size), :] = key
        vf[i, t, pl.ds(kv_start, size), :] = value
        product = key * value
        if own_rows:
            pf[t, pl.ds(p_row, size), :] = product
        high, low = split(product)
        p_hi[pl.ds(p_row, size), lanes] = high
        p_lo[pl.ds(p_row, size), lanes] = low
        query = feature(i, t, 0, q_start, size, tap)
        gradient = query * gs[i, t, pl.ds(q_start, size), :]
        if own_rows:
            dfil[t, pl.ds(d_row, size), :] = gradient
        high, low = split(gradient)
        d_hi[pl.ds(d_row, size), lanes] = high
        d_lo[pl.ds(d_row, size), lanes] = low

    def at_slot(slot):
        return hi.at[slot], lo.at[slot]

    def tripled(high, low):
        return jnp.concatenate([high, low, high], axis=0)

    def taken(slot, size):
        return tripled(hi[slot, 0:size, :], lo[slot, 0:size, :])

    def put(slot, start, value):
        high, low = split(value)
        hi[slot, start : start + value.shape[0], :] = high
        lo[slot, start : start + value.shape[0], :] = low

    def near(i):
        for copy in own_copies(i):
            copy.wait()
        for t in range(TILES):
            lanes = lanes_t(t)
            xs[i, 0, t, NEAR : NEAR + 256] = x_own[i, 0, :, lanes].astype(f32)
            for s in (1, 2):
                xs[i, s, t, EDGE : EDGE + 256] = x_own[i, s, :, lanes].astype(f32)
            gs[i, t, 0:256] = g_own[i, :, lanes].astype(f32)
        product = (ohi.at[i, 0], olo.at[i, 0])
        gradient = (ohi.at[i, 1], olo.at[i, 1])
        for t in range(TILES):
            tap = taps(i, t)
            for row in range(0, OWN, CHUNK):
                features(i, t, NEAR + row, EDGE + row, CHUNK, product, row, gradient, row, tap, True)
            pmine[i, :, lanes_t(t)], pmm[i, :, lanes_t(t)] = coded(pf[t, OWN - FAR : OWN, :])
            dmine[i, :, lanes_t(t)], dmm[i, :, lanes_t(t)] = coded(dfil[t, 0:FAR, :])

    def spectra(i):
        for b in range(8):
            put(2, 16 * b, lf[16 * b : 16 * b + 16, lanes_of(i)])
        sh[i] = dot(fh[...], taken(2, 128))
        sp[i] = dot(fp[...], tripled(ohi[i, 0], olo[i, 0]))
        sd[i] = dot(fd[...], tripled(ohi[i, 1], olo[i, 1]))

    def send_halo(i):
        for copy in halo_copies(i):
            copy.start()

    def local(i, _):
        near(i)
        spectra(i - 1)
        send_halo(i)
        return 0

    near(0)
    near(1)
    spectra(0)
    pl.semaphore_wait(barrier, 19)
    for copy in raw_copies():
        copy.start()
    send_halo(0)
    send_halo(1)
    lax.fori_loop(2, groups, local, 0)
    spectra(groups - 1)
    for copy in raw_copies():
        copy.wait()
    for copy in consts[5:]:
        copy.wait()

    mine = core * 2 + x
    trio = [(at(z, (x + n // 2) % 2, (core + n) % 2, hx, y), (core + n) % 2 * 2 + (x + n // 2) % 2) for n in (1, 2, 3)]

    def line_copies(i):
        return [
            remote(quart.at[i, whose], qbuf.at[i, n], line_s.at[i, n], line_r.at[i, n], other)
            for n, (other, whose) in enumerate(trio)
        ]

    def z_copies(first, size):
        here = pl.ds(first, size)
        return [
            remote(
                zsrc.at[lax.rem(z + n + 1, 8), here], zbuf.at[n, here], z_s.at[first, n], z_r.at[first, n], rings[n]
            )
            for n in range(7)
        ]

    def after_line(i):
        for copy in line_copies(i):
            copy.wait()
        total = quart[i, mine] + qbuf[i, 0] + qbuf[i, 1] + qbuf[i, 2]
        for n in range(8):
            zsrc[n, i, 0:4] = total[4 * n : 4 * n + 4]
            zsrc[n, i, 4:8] = total[32 + 4 * n : 36 + 4 * n]
            zsrc[n, i, 8:20] = total[64:76]

    def group(i, top):
        for copy in halo_copies(i):
            copy.wait_recv()
        for t in range(TILES):
            wide = pl.ds(pl.multiple_of(i * GROUP + 128 * t, 128), 128)
            lanes = lanes_t(t)
            tap = taps(i, t)
            xs[i, 0, t, 0:NEAR] = tail[0, :, wide].astype(f32) * inner
            xs[i, 0, t, NEAR + 256 : 2 * NEAR + 256] = head[0, :, wide].astype(f32)
            for s in (1, 2):
                xs[i, s, t, FAR:EDGE] = tail[s, :, wide].astype(f32) * inner
                xs[i, s, t, EDGE + 256 : SIZE] = head[s, :, wide].astype(f32)
            gs[i, t, 256 : 256 + NEAR] = ghead[:, wide].astype(f32) * outer
            for c in range(0, FAR, 32):
                high, low = split(decoded(pcode[i, c : c + 32, lanes], pmost[i, :, lanes] * inner))
                hi[0, c : c + 32, lanes] = high
                lo[0, c : c + 32, lanes] = low
                high, low = split(decoded(dcode[i, c : c + 32, lanes], dmost[i, :, lanes] * outer))
                hi[1, NEAR + c : NEAR + c + 32, lanes] = high
                lo[1, NEAR + c : NEAR + c + 32, lanes] = low
            features(i, t, 0, FAR, NEAR, at_slot(0), FAR, at_slot(2), 0, tap)
            features(i, t, 256, EDGE + OWN, NEAR, at_slot(0), EDGE, at_slot(1), 0, tap)
        sp[i] = sp[i] + dot(fph[...], taken(0, EDGE + NEAR))
        sd[i] = sd[i] + dot(fdn[...], taken(2, NEAR))
        sx[...] = sd[i] + dot(fda[...], taken(1, EDGE))

        row = lax.broadcasted_iota(jnp.int32, (8, GROUP), 0)
        for b in range(PAIRS):

            def two(ref, b=b):
                return ref[16 * b : 16 * b + 8, :], ref[16 * b + 8 : 16 * b + 16, :]

            pr, pi = two(sp.at[i])
            hr, him = two(sh.at[i])
            dr, di = two(sd.at[i])
            xr, xi = two(sx)

            def pack(same, cross_, re, im, sign, special=b == 0):
                if special:
                    real = re + sign * jnp.where(row == 0, 0.0, same)
                    imag = jnp.where(row == 0, same, im + cross_)
                else:
                    real = re + same if sign > 0 else re - same
                    imag = im + cross_
                return jnp.concatenate([real, imag], axis=0)

            put(0, 16 * b, pack(di * pi, -(di * pr), dr * pr, dr * pi, 1.0))
            put(1, 16 * b, pack(pi * him, pi * hr, pr * hr, pr * him, -1.0))
            put(2, 16 * b, pack(xi * him, xi * hr, xr * hr, -(xr * him), 1.0))

        long_sum = dot(bl[...], taken(0, SIZE))
        for n in range(4):
            for t in range(TILES):
                quart[i, n, 32 * t : 32 * t + 32] = long_sum[32 * n : 32 * n + 32, 128 * t : 128 * t + 128]
        fil[...] = dot(bf[...], taken(1, SIZE))
        dpr[...] = dot(bd[...], taken(2, SIZE))

        for t in range(TILES):
            lanes = pl.ds(128 * t, 128)
            df[0, t, 0:KEEP, :] = gs[i, t, 0:KEEP, :] * fil[:, lanes]
            df[1, t, 0:KEEP, :] = dpr[:, lanes] * vf[i, t, 128 : 128 + KEEP, :]
            df[2, t, 0:KEEP, :] = dpr[:, lanes] * kf[i, t, 128 : 128 + KEEP, :]

        for t in range(TILES):
            short = []
            for s in range(3):
                shift = NEAR if s == 0 else EDGE
                sums = [jnp.zeros((8, 128), f32)] * 7
                for base in range(0, 256, 64):
                    here = df[s, t, pl.ds(base, 64), :]
                    for n in range(7):
                        term = here * xs[i, s, t, pl.ds(base + shift - n, 64), :]
                        sums[n] = sums[n] + jnp.sum(term.reshape(8, 8, 128), axis=0)
                short += [jnp.sum(v, axis=0, keepdims=True) for v in sums] + [jnp.zeros((1, 128), f32)]
            quart[i, 2 * t, 64:76] = jnp.concatenate(short[:12], axis=0)
            quart[i, 2 * t + 1, 64:76] = jnp.concatenate(short[12:], axis=0)
        for copy in line_copies(i):
            copy.start()

        @pl.when(i > 0)
        def _():
            after_line(i - 1)

        @pl.when(i == groups - 1)
        def _():
            for copy in z_copies(0, groups - 1):
                copy.start()

        for t in range(TILES):
            lanes = lanes_t(t)
            tap = taps(i, t)
            for s in range(3):
                for base in range(0, 256, 64):
                    total = None
                    for n in range(7):
                        term = df[s, t, pl.ds(base + n, 64), :] * tap(s, n)
                        total = term if total is None else total + term
                    din[i, s, pl.ds(base, 64), lanes] = total
                    top = jnp.maximum(top, jnp.max(jnp.abs(total).reshape(8, 8, 128), axis=0))
        return top

    top = lax.fori_loop(0, groups, group, jnp.zeros((8, 128), f32))

    def spread(source, slots, first, others):
        copies = [remote(source, slots.at[n], epi_s.at[first + n], epi_r.at[first + n], o) for n, o in enumerate(others)]
        for copy in copies:
            copy.start()
        return copies

    def gather(top, copies, slots):
        for copy in copies:
            copy.wait_recv()
        for n in range(len(copies)):
            top = jnp.maximum(top, slots[n])
        return top

    pone[...] = top
    ones = spread(pone, pbuf1, 0, line)
    after_line(groups - 1)
    lasts_z = z_copies(groups - 1, 1)
    for copy in lasts_z:
        copy.start()
    zs = (*z_copies(0, groups - 1), *lasts_z)
    top = gather(top, ones, pbuf1)
    ptwo[...] = top
    twos = spread(ptwo, pbuf2, 7, columns)
    top = gather(top, twos, pbuf2)
    pthree[...] = top
    threes = spread(pthree, pbuf3, 10, rings)
    for copy in zs:
        copy.wait_recv()
    whole = zsrc[z]
    for n in range(7):
        whole = whole + zbuf[n]
    for i in range(groups):
        lout[:, GROUP * i : GROUP * i + 128] = whole[i, 0:4]
        lout[:, GROUP * i + 128 : GROUP * (i + 1)] = whole[i, 4:8]
    sout[core, x] = whole[:, 8:20]
    quarter = sout.at[core, x]
    lasts = [
        remote(quarter, quarter, epi_s.at[17 + n], epi_r.at[17 + n], o) for n, o in enumerate((pair, cross, diagonal))
    ]
    for copy in lasts:
        copy.start()
    pout[...] = gather(top, threes, pbuf3)
    for copy in (*ones, *twos, *threes, *zs):
        copy.wait_send()
    for i in range(groups):
        for copy in halo_copies(i):
            copy.wait_send()
    for copy in lasts:
        copy.wait()


def main(x3, cotangent, sf, lf):
    _, rows, chan = x3.shape
    consts = [jnp.asarray(c) for c in transforms()]
    groups = chan // GROUP
    anywhere = pl.BlockSpec(memory_space=pl.ANY)
    vmem = pl.BlockSpec(memory_space=pltpu.VMEM)
    V = pltpu.VMEM
    D = pltpu.SemaphoreType.DMA
    return pl.pallas_call(
        main_kernel,
        out_shape=[
            V((groups, 3, rows, GROUP), f32),
            V((4, chan), f32),
            V((2, 2, groups, 12, 128), f32),
            V((8, 128), f32),
        ],
        in_specs=[anywhere] * (4 + len(consts)),
        out_specs=[vmem, vmem, vmem, vmem],
        scratch_shapes=[
            V((groups, 3, rows, GROUP), bf16),
            V((groups, rows, GROUP), bf16),
            V((3, NEAR, chan), bf16),
            V((3, NEAR, chan), bf16),
            V((NEAR, chan), bf16),
            V((groups, FAR, GROUP), bf16),
            V((groups, FAR, GROUP), bf16),
            V((groups, 1, GROUP), f32),
            V((groups, 1, GROUP), f32),
            V((groups, FAR, GROUP), bf16),
            V((groups, FAR, GROUP), bf16),
            V((groups, 1, GROUP), f32),
            V((groups, 1, GROUP), f32),
            V((TILES, OWN, 128), f32),
            V((TILES, OWN, 128), f32),
            V(sf.shape, f32),
            V(lf.shape, f32),
            *[V(c.shape, bf16) for c in consts],
            V((groups, 3, TILES, SIZE, 128), f32),
            V((groups, TILES, SPAN, 128), f32),
            V((groups, TILES, SPAN, 128), f32),
            V((groups, TILES, SPAN, 128), f32),
            V((groups, SIZE, GROUP), f32),
            V((groups, SIZE, GROUP), f32),
            V((groups, SIZE, GROUP), f32),
            V((groups, 2, OWN, GROUP), bf16),
            V((groups, 2, OWN, GROUP), bf16),
            V((3, SIZE, GROUP), bf16),
            V((3, SIZE, GROUP), bf16),
            V((SIZE, GROUP), f32),
            V((KEEP, GROUP), f32),
            V((KEEP, GROUP), f32),
            V((3, TILES, KEEP + 8, 128), f32),
            V((groups, 4, 76, 128), f32),
            V((groups, 3, 76, 128), f32),
            V((8, groups, 20, 128), f32),
            V((7, groups, 20, 128), f32),
            V((7, 8, 128), f32),
            V((3, 8, 128), f32),
            V((7, 8, 128), f32),
            V((8, 128), f32),
            V((8, 128), f32),
            V((8, 128), f32),
            D((11,)),
            D((2, groups)),
            D((3,)),
            D((3,)),
            D((4, groups)),
            D((4, groups)),
            D((groups, 3)),
            D((groups, 3)),
            D((groups, 7)),
            D((groups, 7)),
            D((20,)),
            D((20,)),
        ],
        compiler_params=pltpu.CompilerParams(
            collective_id=0, has_side_effects=True, vmem_limit_bytes=60 * 1024 * 1024
        ),
        name="gradients",
    )(x3, cotangent, sf, lf, *consts)


STEPS = 2


def scale_kernel(din, lsum, ssum, peak, out_hbm, lout, sout, scale, out, stores):
    groups, streams, rows, _ = din.shape
    step = rows // STEPS
    top = jnp.max(peak[...]) + EPSILON
    factor = FP8_RANGE / top
    copies = []
    for s in range(streams):
        for n in range(STEPS):
            here = pl.ds(n * step, step)
            for i in range(groups):
                out[s, here, GROUP * i : GROUP * (i + 1)] = (din[i, s, here, :] * factor).astype(bf16)
            copies.append(pltpu.make_async_copy(out.at[s, here], out_hbm.at[s, here], stores.at[s * STEPS + n]))
            copies[-1].start()
    scale[0, 0] = top / FP8_RANGE
    lout[...] = lsum[...]
    for c in range(2):
        for i in range(groups):
            lanes = pl.ds(GROUP * i + 128 * c, 128)
            sout[0, :, lanes] = ssum[c, 0, i, 0:7]
            sout[1, 0:4, lanes] = ssum[c, 0, i, 8:12]
            sout[1, 4:7, lanes] = ssum[c, 1, i, 0:3]
            sout[2, :, lanes] = ssum[c, 1, i, 4:11]
    for copy in copies:
        copy.wait()


def scaled(din, lsum, ssum, peak):
    groups, _, rows, _ = din.shape
    chan = groups * GROUP
    vmem = pl.BlockSpec(memory_space=pltpu.VMEM)
    anywhere = pl.BlockSpec(memory_space=pl.ANY)
    din, lsum, ssum, peak = [pltpu.with_memory_space_constraint(a, pltpu.VMEM) for a in (din, lsum, ssum, peak)]
    return pl.pallas_call(
        scale_kernel,
        out_shape=[
            jax.ShapeDtypeStruct((3, rows, chan), bf16),
            jax.ShapeDtypeStruct((4, chan), f32),
            jax.ShapeDtypeStruct((3, 7, chan), f32),
            jax.ShapeDtypeStruct((1, 1), f32),
        ],
        in_specs=[vmem, vmem, vmem, vmem],
        out_specs=[anywhere, vmem, vmem, pl.BlockSpec(memory_space=pltpu.SMEM)],
        scratch_shapes=[pltpu.VMEM((3, rows, chan), bf16), pltpu.SemaphoreType.DMA((3 * STEPS,))],
        compiler_params=pltpu.CompilerParams(vmem_limit_bytes=32 * 1024 * 1024),
        name="scaling",
    )(din, lsum, ssum, peak)


def body(projected, cotangent, short_filter, long_filter):
    x3 = projected.transpose(1, 0, 2)
    sf = short_filter.transpose(1, 0, 2)
    out, long_grad, short_grad, scale = scaled(*main(x3, cotangent, sf, long_filter))
    return out.transpose(1, 0, 2), long_grad, short_grad.transpose(1, 0, 2), scale.reshape(())


def solution(mesh):
    placed = (P("ctx", None, "tp"), P("ctx", "tp"), P(None, None, "tp"), P(None, "tp"))
    return jax.shard_map(
        body,
        mesh=mesh,
        in_specs=placed,
        out_specs=(P("ctx", None, "tp"), P("ctx", "tp"), P(None, None, "tp"), P()),
        check_vma=False,
    )
```

```python
import functools

import jax
import jax.numpy as jnp
import ml_dtypes
import numpy as np
from jax import lax
from jax.experimental import pallas as pl
from jax.experimental.pallas import tpu as pltpu
from jax.sharding import PartitionSpec as P

EPSILON = 1e-06
FP8_RANGE = 448.0
MESH = pl.DeviceIdType.MESH

SIZE = 416
PAIRS = SIZE // 16
EDGE = 144
NEAR = 16
FAR = 128
AHEAD = FAR + 2 * NEAR
BACK = FAR + 4 * NEAR
POWER = 11
REACH = 2048.0
LEAST = 1e-30
OWN = 240
SPAN = 400
KEEP = 264
GROUP = 256
TILES = GROUP // 128
CHUNK = 48
f32 = jnp.float32
bf16 = jnp.bfloat16


def joined_np(matrix):
    high = matrix.astype(ml_dtypes.bfloat16)
    low = (matrix - high.astype(np.float64)).astype(ml_dtypes.bfloat16)
    return np.concatenate([high, high, low], axis=1)


@functools.lru_cache(None)
def transforms():
    m = np.arange(SIZE)[None, :]
    k = np.arange(SIZE // 2)[:, None]
    re = np.cos(2 * np.pi * ((k * m) % SIZE) / SIZE)
    im = -np.sin(2 * np.pi * ((k * m) % SIZE) / SIZE)
    im[0] = np.cos(np.pi * m[0])
    weight = np.full((SIZE // 2, 1), 2.0 / SIZE)
    weight[0] = 1.0 / SIZE

    def blocks(a, b):
        return np.stack([a.reshape(PAIRS, 8, SIZE), b.reshape(PAIRS, 8, SIZE)], axis=1).reshape(SIZE, SIZE)

    ahead = blocks(re, im)
    back = blocks(re * weight, im * weight).T
    c = np.arange(128)
    core, x, z, r = c // 64, (c // 32) % 2, (c // 4) % 8, c % 4
    lag = 128 - ((z * 4 + x * 2 + core) * 4 + r)
    return (
        joined_np(ahead[:, :128]),
        joined_np(ahead[:, EDGE : EDGE + OWN]),
        joined_np(ahead[:, NEAR : NEAR + OWN]),
        joined_np(np.concatenate([ahead[:, :EDGE], ahead[:, EDGE + OWN : SPAN]], axis=1)),
        joined_np(ahead[:, :NEAR]),
        joined_np(ahead[:, NEAR + OWN : SPAN]),
        joined_np(back[lag]),
        joined_np(back[128 : 128 + KEEP]),
        joined_np(back[:KEEP]),
    )


def split(value):
    high = value.astype(bf16)
    low = (value - high.astype(f32)).astype(bf16)
    return high, low


def coded(value):
    most = jnp.maximum(jnp.max(jnp.abs(value), axis=0, keepdims=True), LEAST).astype(bf16).astype(f32)
    u = value * (REACH / most)
    u2 = u * u
    u4 = u2 * u2
    return ((u4 * u4) * (u2 * u)).astype(bf16), most


def decoded(code, most):
    y = code.astype(f32)
    root = jnp.exp2(jnp.log2(jnp.maximum(jnp.abs(y), 1.2e-38)) * (1.0 / POWER))
    return jnp.where(y < 0, -root, root) * (most * (1.0 / REACH))


def dot(a, b):
    return lax.dot_general(a, b, (((1,), (0,)), ((), ())), preferred_element_type=f32)


def main_kernel(
    x_hbm, g_hbm, sf_hbm, lf_hbm, fh_h, fp_h, fd_h, fph_h, fdn_h, fda_h, bl_h, bf_h, bd_h,
    din, lout, sout, pout,
    x_own, g_own, ahead, back, from_before, from_after, pf, dfil, sf, lf, fh, fp, fd, fph, fdn, fda, bl, bf, bd,
    xs, gs, kf, vf, sp, sd, sh, ohi, olo, hi, lo, sx, fil, dpr, df,
    quart, qbuf, zsrc, zbuf, pbuf1, pbuf2, pbuf3, pone, ptwo, pthree,
    loads, own, halo_s, halo_r, line_s, line_r, z_s, z_r, epi_s, epi_r,
):
    me = lax.axis_index("ctx")
    count = lax.axis_size("ctx")
    tp = lax.axis_index("tp")
    after = {"ctx": lax.rem(me + 1, count)}
    before = {"ctx": lax.rem(me + count - 1, count)}
    core = lax.rem(me, 2)
    x = lax.rem(me // 2, 2)
    z = me // 4
    hx = tp // 4
    y = lax.rem(tp, 4)
    rows = x_hbm.shape[1]
    groups = x_own.shape[0]

    def at(zz, xx, cc, hh, yy):
        return {"ctx": zz * 4 + xx * 2 + cc, "tp": hh * 4 + yy}

    pair = at(z, x, 1 - core, hx, y)
    rings = [at(lax.rem(z + n, 8), x, core, hx, y) for n in range(1, 8)]
    columns = [at(z, x, core, hx, lax.rem(y + n, 4)) for n in range(1, 4)]
    line = [at(z, (x + n // 2) % 2, (core + n) % 2, (hx + n // 4) % 2, y) for n in range(1, 8)]

    def lanes_of(i):
        return pl.ds(pl.multiple_of(i * GROUP, GROUP), GROUP)

    def own_copies(i):
        return (
            pltpu.make_async_copy(x_hbm.at[:, :, lanes_of(i)], x_own.at[i], own.at[0, i]),
            pltpu.make_async_copy(g_hbm.at[:, lanes_of(i)], g_own.at[i], own.at[1, i]),
        )

    def remote(source, target, send, recv, other):
        return pltpu.make_async_remote_copy(
            src_ref=source, dst_ref=target, send_sem=send, recv_sem=recv, device_id=other, device_id_type=MESH
        )

    def halo_copies(i):
        return (
            remote(ahead.at[i], from_before.at[i], halo_s.at[0, i], halo_r.at[0, i], after),
            remote(back.at[i], from_after.at[i], halo_s.at[1, i], halo_r.at[1, i], before),
        )

    sources = (sf_hbm, lf_hbm, fh_h, fp_h, fd_h, fph_h, fdn_h, fda_h, bl_h, bf_h, bd_h)
    targets = (sf, lf, fh, fp, fd, fph, fdn, fda, bl, bf, bd)
    consts = [pltpu.make_async_copy(a, b, loads.at[n]) for n, (a, b) in enumerate(zip(sources, targets))]
    for copy in consts[:1]:
        copy.start()
    for copy in own_copies(0):
        copy.start()
    barrier = pltpu.get_barrier_semaphore()
    for other in [*rings, after, before, *columns, *line]:
        pl.semaphore_signal(barrier, inc=1, device_id=other, device_id_type=MESH)
    for copy in consts[1:5]:
        copy.start()
    for i in range(1, groups):
        for copy in own_copies(i):
            copy.start()
    for copy in consts[5:]:
        copy.start()
    consts[0].wait()
    inner = (me > 0).astype(f32)
    outer = (me < count - 1).astype(f32)

    def lanes_t(t):
        return pl.ds(128 * t, 128)

    def taps(i, t):
        lanes = pl.ds(pl.multiple_of(i * GROUP + 128 * t, 128), 128)
        return lambda s, n: sf[s, n : n + 1, lanes]

    def feature(i, t, s, start, size, tap):
        total = None
        for n in range(7):
            term = xs[i, s, t, pl.ds(start + NEAR - n, size), :] * tap(s, n)
            total = term if total is None else total + term
        return total

    def features(i, t, q_start, kv_start, size, p_slot, p_row, d_slot, d_row, tap, own_rows=False):
        lanes = pl.ds(128 * t, 128)
        p_hi, p_lo = p_slot
        d_hi, d_lo = d_slot
        key = feature(i, t, 1, kv_start, size, tap)
        value = feature(i, t, 2, kv_start, size, tap)
        kf[i, t, pl.ds(kv_start, size), :] = key
        vf[i, t, pl.ds(kv_start, size), :] = value
        product = key * value
        if own_rows:
            pf[t, pl.ds(p_row, size), :] = product
        high, low = split(product)
        p_hi[pl.ds(p_row, size), lanes] = high
        p_lo[pl.ds(p_row, size), lanes] = low
        query = feature(i, t, 0, q_start, size, tap)
        gradient = query * gs[i, t, pl.ds(q_start, size), :]
        if own_rows:
            dfil[t, pl.ds(d_row, size), :] = gradient
        high, low = split(gradient)
        d_hi[pl.ds(d_row, size), lanes] = high
        d_lo[pl.ds(d_row, size), lanes] = low

    def at_slot(slot):
        return hi.at[slot], lo.at[slot]

    def tripled(high, low):
        return jnp.concatenate([high, low, high], axis=0)

    def taken(slot, size):
        return tripled(hi[slot, 0:size, :], lo[slot, 0:size, :])

    def put(slot, start, value):
        high, low = split(value)
        hi[slot, start : start + value.shape[0], :] = high
        lo[slot, start : start + value.shape[0], :] = low

    def near(i):
        for copy in own_copies(i):
            copy.wait()
        for t in range(TILES):
            lanes = lanes_t(t)
            xs[i, 0, t, NEAR : NEAR + 256] = x_own[i, 0, :, lanes].astype(f32)
            for s in (1, 2):
                xs[i, s, t, EDGE : EDGE + 256] = x_own[i, s, :, lanes].astype(f32)
            gs[i, t, 0:256] = g_own[i, :, lanes].astype(f32)
        product = (ohi.at[i, 0], olo.at[i, 0])
        gradient = (ohi.at[i, 1], olo.at[i, 1])
        for t in range(TILES):
            tap = taps(i, t)
            for row in range(0, OWN, CHUNK):
                features(i, t, NEAR + row, EDGE + row, CHUNK, product, row, gradient, row, tap, True)
            lanes = lanes_t(t)
            code, most = coded(pf[t, OWN - FAR : OWN, :])
            ahead[i, 0:FAR, lanes] = code
            for n, parts in enumerate(((jnp.broadcast_to(most, (8, 128)), xs[i, 0, t, 264:272]), (xs[i, 1, t, 392:400], xs[i, 2, t, 392:400]))):
                ahead[i, FAR + NEAR * n : FAR + NEAR * (n + 1), lanes] = jnp.concatenate(parts, axis=0).astype(bf16)
            code, most = coded(dfil[t, 0:FAR, :])
            back[i, 0:FAR, lanes] = code
            back[i, FAR : FAR + NEAR, lanes] = x_own[i, 0, 0:NEAR, lanes]
            back[i, FAR + NEAR : FAR + 2 * NEAR, lanes] = g_own[i, 0:NEAR, lanes]
            back[i, FAR + 2 * NEAR : FAR + 3 * NEAR, lanes] = jnp.concatenate(
                [xs[i, 1, t, EDGE : EDGE + 8], xs[i, 2, t, EDGE : EDGE + 8]], axis=0
            ).astype(bf16)
            back[i, FAR + 3 * NEAR : BACK, lanes] = jnp.broadcast_to(most, (NEAR, 128)).astype(bf16)

    def spectra(i):
        for b in range(8):
            put(2, 16 * b, lf[16 * b : 16 * b + 16, lanes_of(i)])
        sh[i] = dot(fh[...], taken(2, 128))
        sp[i] = dot(fp[...], tripled(ohi[i, 0], olo[i, 0]))
        sd[i] = dot(fd[...], tripled(ohi[i, 1], olo[i, 1]))

    def send_halo(i):
        for copy in halo_copies(i):
            copy.start()

    def local(i, _):
        near(i)
        spectra(i - 1)
        send_halo(i)
        return 0

    near(0)
    pl.semaphore_wait(barrier, 19)
    send_halo(0)
    for copy in consts[1:5]:
        copy.wait()
    lax.fori_loop(1, groups, local, 0)
    spectra(groups - 1)
    for copy in consts[5:]:
        copy.wait()

    mine = core * 2 + x
    trio = [(at(z, (x + n // 2) % 2, (core + n) % 2, hx, y), (core + n) % 2 * 2 + (x + n // 2) % 2) for n in (1, 2, 3)]

    def line_copies(i):
        return [
            remote(quart.at[i, whose], qbuf.at[i, n], line_s.at[i, n], line_r.at[i, n], other)
            for n, (other, whose) in enumerate(trio)
        ]

    def z_copies(first, size):
        here = pl.ds(first, size)
        return [
            remote(
                zsrc.at[lax.rem(z + n + 1, 8), here], zbuf.at[n, here], z_s.at[first, n], z_r.at[first, n], rings[n]
            )
            for n in range(7)
        ]

    def after_line(i):
        for copy in line_copies(i):
            copy.wait()
        total = quart[i, mine] + qbuf[i, 0] + qbuf[i, 1] + qbuf[i, 2]
        for n in range(8):
            zsrc[n, i, 0:4] = total[4 * n : 4 * n + 4]
            zsrc[n, i, 4:8] = total[32 + 4 * n : 36 + 4 * n]
            zsrc[n, i, 8:32] = total[64:88]

    def group(i, top):
        for copy in halo_copies(i):
            copy.wait_recv()
        for t in range(TILES):
            lanes = lanes_t(t)
            tap = taps(i, t)
            edge = from_before[i, FAR : FAR + NEAR, lanes].astype(f32) * inner
            pmost = edge[0:1]
            xs[i, 0, t, 8:NEAR] = edge[8:NEAR]
            edge = from_before[i, FAR + NEAR : AHEAD, lanes].astype(f32) * inner
            xs[i, 1, t, FAR + 8 : EDGE] = edge[0:8]
            xs[i, 2, t, FAR + 8 : EDGE] = edge[8:NEAR]
            xs[i, 0, t, NEAR + 256 : 2 * NEAR + 256] = from_after[i, FAR : FAR + NEAR, lanes].astype(f32)
            gs[i, t, 256 : 256 + NEAR] = from_after[i, FAR + NEAR : FAR + 2 * NEAR, lanes].astype(f32) * outer
            edge = from_after[i, FAR + 2 * NEAR : FAR + 3 * NEAR, lanes].astype(f32)
            for s in (1, 2):
                xs[i, s, t, EDGE + 256 : EDGE + 264] = edge[8 * s - 8 : 8 * s]
                xs[i, s, t, EDGE + 264 : SIZE] = jnp.zeros((8, 128), f32)
            dmost = from_after[i, FAR + 3 * NEAR : BACK, lanes].astype(f32)[0:1] * outer
            for c in range(0, FAR, 32):
                high, low = split(decoded(from_before[i, c : c + 32, lanes], pmost))
                hi[0, c : c + 32, lanes] = high
                lo[0, c : c + 32, lanes] = low
                high, low = split(decoded(from_after[i, c : c + 32, lanes], dmost))
                hi[1, NEAR + c : NEAR + c + 32, lanes] = high
                lo[1, NEAR + c : NEAR + c + 32, lanes] = low
            features(i, t, 0, FAR, NEAR, at_slot(0), FAR, at_slot(2), 0, tap)
            features(i, t, 256, EDGE + OWN, NEAR, at_slot(0), EDGE, at_slot(1), 0, tap)
        sp[i] = sp[i] + dot(fph[...], taken(0, EDGE + NEAR))
        sd[i] = sd[i] + dot(fdn[...], taken(2, NEAR))
        sx[...] = sd[i] + dot(fda[...], taken(1, EDGE))

        row = lax.broadcasted_iota(jnp.int32, (8, GROUP), 0)
        for b in range(PAIRS):

            def two(ref, b=b):
                return ref[16 * b : 16 * b + 8, :], ref[16 * b + 8 : 16 * b + 16, :]

            pr, pi = two(sp.at[i])
            hr, him = two(sh.at[i])
            dr, di = two(sd.at[i])
            xr, xi = two(sx)

            def pack(same, cross_, re, im, sign, special=b == 0):
                if special:
                    real = re + sign * jnp.where(row == 0, 0.0, same)
                    imag = jnp.where(row == 0, same, im + cross_)
                else:
                    real = re + same if sign > 0 else re - same
                    imag = im + cross_
                return jnp.concatenate([real, imag], axis=0)

            put(0, 16 * b, pack(di * pi, -(di * pr), dr * pr, dr * pi, 1.0))
            put(1, 16 * b, pack(pi * him, pi * hr, pr * hr, pr * him, -1.0))
            put(2, 16 * b, pack(xi * him, xi * hr, xr * hr, -(xr * him), 1.0))

        long_sum = dot(bl[...], taken(0, SIZE))
        for n in range(4):
            for t in range(TILES):
                quart[i, n, 32 * t : 32 * t + 32] = long_sum[32 * n : 32 * n + 32, 128 * t : 128 * t + 128]
        fil[...] = dot(bf[...], taken(1, SIZE))
        dpr[...] = dot(bd[...], taken(2, SIZE))

        for t in range(TILES):
            lanes = pl.ds(128 * t, 128)
            df[0, t, 0:KEEP, :] = gs[i, t, 0:KEEP, :] * fil[:, lanes]
            df[1, t, 0:KEEP, :] = dpr[:, lanes] * vf[i, t, 128 : 128 + KEEP, :]
            df[2, t, 0:KEEP, :] = dpr[:, lanes] * kf[i, t, 128 : 128 + KEEP, :]

        for t in range(TILES):
            short = []
            for s in range(3):
                shift = NEAR if s == 0 else EDGE
                sums = [jnp.zeros((8, 128), f32)] * 7
                for base in range(0, 256, 64):
                    here = df[s, t, pl.ds(base, 64), :]
                    for n in range(7):
                        term = here * xs[i, s, t, pl.ds(base + shift - n, 64), :]
                        sums[n] = sums[n] + jnp.sum(term.reshape(8, 8, 128), axis=0)
                short += [jnp.sum(v, axis=0, keepdims=True) for v in sums] + [jnp.zeros((1, 128), f32)]
            for n in range(2):
                quart[i, 2 * t + n, 64:88] = jnp.concatenate(short, axis=0)
        for copy in line_copies(i):
            copy.start()

        @pl.when(i > 1)
        def _():
            after_line(i - 2)

        @pl.when(i == groups - 1)
        def _():
            for copy in z_copies(0, groups - 2):
                copy.start()

        for t in range(TILES):
            lanes = lanes_t(t)
            tap = taps(i, t)
            for s in range(3):
                for base in range(0, 256, 64):
                    total = None
                    for n in range(7):
                        term = df[s, t, pl.ds(base + n, 64), :] * tap(s, n)
                        total = term if total is None else total + term
                    din[i, s, pl.ds(base, 64), lanes] = total
                    top = jnp.maximum(top, jnp.max(jnp.abs(total).reshape(8, 8, 128), axis=0))
        return top

    top = lax.fori_loop(0, groups, group, jnp.zeros((8, 128), f32))

    def spread(source, slots, first, others):
        copies = [remote(source, slots.at[n], epi_s.at[first + n], epi_r.at[first + n], o) for n, o in enumerate(others)]
        for copy in copies:
            copy.start()
        return copies

    def gather(top, copies, slots):
        for copy in copies:
            copy.wait_recv()
        for n in range(len(copies)):
            top = jnp.maximum(top, slots[n])
        return top

    pone[...] = top
    ones = spread(pone, pbuf1, 0, line)
    zs = [*z_copies(0, groups - 2), *z_copies(groups - 2, 1), *z_copies(groups - 1, 1)]
    after_line(groups - 2)
    for copy in zs[7:14]:
        copy.start()
    top = gather(top, ones, pbuf1)
    ptwo[...] = top
    twos = spread(ptwo, pbuf2, 7, columns)
    after_line(groups - 1)
    for copy in zs[14:]:
        copy.start()
    top = gather(top, twos, pbuf2)
    pthree[...] = top
    threes = spread(pthree, pbuf3, 10, rings)
    for copy in zs:
        copy.wait_recv()
    whole = zsrc[z]
    for n in range(7):
        whole = whole + zbuf[n]
    for i in range(groups):
        lout[:, GROUP * i : GROUP * i + 128] = whole[i, 0:4]
        lout[:, GROUP * i + 128 : GROUP * (i + 1)] = whole[i, 4:8]
    sout[core] = whole[:, 8:32]
    last = remote(sout.at[core], sout.at[core], epi_s.at[17], epi_r.at[17], pair)
    last.start()
    pout[...] = gather(top, threes, pbuf3)
    for copy in (*ones, *twos, *threes, *zs):
        copy.wait_send()
    for i in range(groups):
        for copy in halo_copies(i):
            copy.wait_send()
    last.wait()


def main(x3, cotangent, sf, lf):
    _, rows, chan = x3.shape
    consts = [jnp.asarray(c) for c in transforms()]
    groups = chan // GROUP
    anywhere = pl.BlockSpec(memory_space=pl.ANY)
    vmem = pl.BlockSpec(memory_space=pltpu.VMEM)
    V = pltpu.VMEM
    D = pltpu.SemaphoreType.DMA
    return pl.pallas_call(
        main_kernel,
        out_shape=[
            V((groups, 3, rows, GROUP), f32),
            V((4, chan), f32),
            V((2, groups, 24, 128), f32),
            V((8, 128), f32),
        ],
        in_specs=[anywhere] * (4 + len(consts)),
        out_specs=[vmem, vmem, vmem, vmem],
        scratch_shapes=[
            V((groups, 3, rows, GROUP), bf16),
            V((groups, rows, GROUP), bf16),
            V((groups, AHEAD, GROUP), bf16),
            V((groups, BACK, GROUP), bf16),
            V((groups, AHEAD, GROUP), bf16),
            V((groups, BACK, GROUP), bf16),
            V((TILES, OWN, 128), f32),
            V((TILES, OWN, 128), f32),
            V(sf.shape, f32),
            V(lf.shape, f32),
            *[V(c.shape, bf16) for c in consts],
            V((groups, 3, TILES, SIZE, 128), f32),
            V((groups, TILES, SPAN, 128), f32),
            V((groups, TILES, SPAN, 128), f32),
            V((groups, TILES, SPAN, 128), f32),
            V((groups, SIZE, GROUP), f32),
            V((groups, SIZE, GROUP), f32),
            V((groups, SIZE, GROUP), f32),
            V((groups, 2, OWN, GROUP), bf16),
            V((groups, 2, OWN, GROUP), bf16),
            V((3, SIZE, GROUP), bf16),
            V((3, SIZE, GROUP), bf16),
            V((SIZE, GROUP), f32),
            V((KEEP, GROUP), f32),
            V((KEEP, GROUP), f32),
            V((3, TILES, KEEP + 8, 128), f32),
            V((groups, 4, 88, 128), f32),
            V((groups, 3, 88, 128), f32),
            V((8, groups, 32, 128), f32),
            V((7, groups, 32, 128), f32),
            V((7, 8, 128), f32),
            V((3, 8, 128), f32),
            V((7, 8, 128), f32),
            V((8, 128), f32),
            V((8, 128), f32),
            V((8, 128), f32),
            D((11,)),
            D((2, groups)),
            D((2, groups)),
            D((2, groups)),
            D((groups, 3)),
            D((groups, 3)),
            D((groups, 7)),
            D((groups, 7)),
            D((18,)),
            D((18,)),
        ],
        compiler_params=pltpu.CompilerParams(
            collective_id=0, has_side_effects=True, vmem_limit_bytes=60 * 1024 * 1024
        ),
        name="gradients",
    )(x3, cotangent, sf, lf, *consts)


STEPS = 2


def scale_kernel(din, lsum, ssum, peak, out_hbm, lout, sout, scale, out, stores):
    groups, streams, rows, _ = din.shape
    step = rows // STEPS
    top = jnp.max(peak[...]) + EPSILON
    factor = FP8_RANGE / top
    copies = []
    for s in range(streams):
        for n in range(STEPS):
            here = pl.ds(n * step, step)
            for i in range(groups):
                out[s, here, GROUP * i : GROUP * (i + 1)] = (din[i, s, here, :] * factor).astype(bf16)
            copies.append(pltpu.make_async_copy(out.at[s, here], out_hbm.at[s, here], stores.at[s * STEPS + n]))
            copies[-1].start()
    scale[0, 0] = top / FP8_RANGE
    lout[...] = lsum[...]
    for c in range(2):
        for i in range(groups):
            lanes = pl.ds(GROUP * i + 128 * c, 128)
            for s in range(streams):
                sout[s, :, lanes] = ssum[c, i, 8 * s : 8 * s + 7]
    for copy in copies:
        copy.wait()


def scaled(din, lsum, ssum, peak):
    groups, _, rows, _ = din.shape
    chan = groups * GROUP
    vmem = pl.BlockSpec(memory_space=pltpu.VMEM)
    anywhere = pl.BlockSpec(memory_space=pl.ANY)
    din, lsum, ssum, peak = [pltpu.with_memory_space_constraint(a, pltpu.VMEM) for a in (din, lsum, ssum, peak)]
    return pl.pallas_call(
        scale_kernel,
        out_shape=[
            jax.ShapeDtypeStruct((3, rows, chan), bf16),
            jax.ShapeDtypeStruct((4, chan), f32),
            jax.ShapeDtypeStruct((3, 7, chan), f32),
            jax.ShapeDtypeStruct((1, 1), f32),
        ],
        in_specs=[vmem, vmem, vmem, vmem],
        out_specs=[anywhere, vmem, vmem, pl.BlockSpec(memory_space=pltpu.SMEM)],
        scratch_shapes=[pltpu.VMEM((3, rows, chan), bf16), pltpu.SemaphoreType.DMA((3 * STEPS,))],
        compiler_params=pltpu.CompilerParams(vmem_limit_bytes=32 * 1024 * 1024),
        name="scaling",
    )(din, lsum, ssum, peak)


def body(projected, cotangent, short_filter, long_filter):
    x3 = projected.transpose(1, 0, 2)
    sf = short_filter.transpose(1, 0, 2)
    out, long_grad, short_grad, scale = scaled(*main(x3, cotangent, sf, long_filter))
    return out.transpose(1, 0, 2), long_grad, short_grad.transpose(1, 0, 2), scale.reshape(())


def solution(mesh):
    placed = (P("ctx", None, "tp"), P("ctx", "tp"), P(None, None, "tp"), P(None, "tp"))
    return jax.shard_map(
        body,
        mesh=mesh,
        in_specs=placed,
        out_specs=(P("ctx", None, "tp"), P("ctx", "tp"), P(None, None, "tp"), P()),
        check_vma=False,
    )
```

```python
import functools

import jax
import jax.numpy as jnp
import ml_dtypes
import numpy as np
from jax import lax
from jax.experimental import pallas as pl
from jax.experimental.pallas import tpu as pltpu
from jax.sharding import PartitionSpec as P

EPSILON = 1e-06
FP8_RANGE = 448.0
MESH = pl.DeviceIdType.MESH

SIZE = 416
PAIRS = SIZE // 16
EDGE = 144
NEAR = 16
FAR = 128
AHEAD = FAR + 2 * NEAR
BACK = FAR + 4 * NEAR
POWER = 11
REACH = 2048.0
LEAST = 1e-30
OWN = 240
SPAN = 400
KEEP = 264
GROUP = 256
TILES = GROUP // 128
CHUNK = 48
f32 = jnp.float32
bf16 = jnp.bfloat16


def joined_np(matrix):
    high = matrix.astype(ml_dtypes.bfloat16)
    low = (matrix - high.astype(np.float64)).astype(ml_dtypes.bfloat16)
    return np.concatenate([high, high, low], axis=1)


@functools.lru_cache(None)
def transforms():
    m = np.arange(SIZE)[None, :]
    k = np.arange(SIZE // 2)[:, None]
    re = np.cos(2 * np.pi * ((k * m) % SIZE) / SIZE)
    im = -np.sin(2 * np.pi * ((k * m) % SIZE) / SIZE)
    im[0] = np.cos(np.pi * m[0])
    weight = np.full((SIZE // 2, 1), 2.0 / SIZE)
    weight[0] = 1.0 / SIZE

    def blocks(a, b):
        return np.stack([a.reshape(PAIRS, 8, SIZE), b.reshape(PAIRS, 8, SIZE)], axis=1).reshape(SIZE, SIZE)

    ahead = blocks(re, im)
    back = blocks(re * weight, im * weight).T
    c = np.arange(128)
    core, x, z, r = c // 64, (c // 32) % 2, (c // 4) % 8, c % 4
    lag = 128 - ((z * 4 + x * 2 + core) * 4 + r)
    return (
        joined_np(ahead[:, :128]),
        joined_np(ahead[:, EDGE : EDGE + OWN]),
        joined_np(ahead[:, NEAR : NEAR + OWN]),
        joined_np(np.concatenate([ahead[:, :EDGE], ahead[:, EDGE + OWN : SPAN]], axis=1)),
        joined_np(ahead[:, :NEAR]),
        joined_np(ahead[:, NEAR + OWN : SPAN]),
        joined_np(back[lag]),
        joined_np(back[128 : 128 + KEEP]),
        joined_np(back[:KEEP]),
    )


def split(value):
    high = value.astype(bf16)
    low = (value - high.astype(f32)).astype(bf16)
    return high, low


def powered(value):
    most = jnp.maximum(jnp.max(jnp.abs(value), axis=0, keepdims=True), LEAST).astype(bf16).astype(f32)
    u = value * (REACH / most)
    u2 = u * u
    u4 = u2 * u2
    return (u4 * u4) * (u2 * u), most


def coded(value):
    power, most = powered(value)
    return power.astype(bf16), most


def decoded(code, most):
    y = code.astype(f32)
    root = jnp.exp2(jnp.log2(jnp.maximum(jnp.abs(y), 1.2e-38)) * (1.0 / POWER))
    return jnp.where(y < 0, -root, root) * (most * (1.0 / REACH))


def dot(a, b):
    return lax.dot_general(a, b, (((1,), (0,)), ((), ())), preferred_element_type=f32)


def main_kernel(
    x_hbm, g_hbm, sf_hbm, lf_hbm, fh_h, fp_h, fd_h, fph_h, fdn_h, fda_h, bl_h, bf_h, bd_h,
    din, lout, sout, pout,
    x_own, g_own, ahead, back, from_before, from_after, pf, dfil, sf, lf, fh, fp, fd, fph, fdn, fda, bl, bf, bd,
    xs, gs, kf, vf, sp, sd, sh, ohi, olo, hi, lo, sx, fil, dpr, df,
    quart, qbuf, zsrc, zbuf, pbuf1, pbuf2, pbuf3, pone, ptwo, pthree,
    loads, own, halo_s, halo_r, line_s, line_r, z_s, z_r, epi_s, epi_r,
):
    me = lax.axis_index("ctx")
    count = lax.axis_size("ctx")
    tp = lax.axis_index("tp")
    after = {"ctx": lax.rem(me + 1, count)}
    before = {"ctx": lax.rem(me + count - 1, count)}
    core = lax.rem(me, 2)
    x = lax.rem(me // 2, 2)
    z = me // 4
    hx = tp // 4
    y = lax.rem(tp, 4)
    rows = x_hbm.shape[1]
    groups = x_own.shape[0]

    def at(zz, xx, cc, hh, yy):
        return {"ctx": zz * 4 + xx * 2 + cc, "tp": hh * 4 + yy}

    pair = at(z, x, 1 - core, hx, y)
    rings = [at(lax.rem(z + n, 8), x, core, hx, y) for n in range(1, 8)]
    columns = [at(z, x, core, hx, lax.rem(y + n, 4)) for n in range(1, 4)]
    line = [at(z, (x + n // 2) % 2, (core + n) % 2, (hx + n // 4) % 2, y) for n in range(1, 8)]

    def lanes_of(i):
        return pl.ds(pl.multiple_of(i * GROUP, GROUP), GROUP)

    def own_copies(i):
        return (
            pltpu.make_async_copy(x_hbm.at[:, :, lanes_of(i)], x_own.at[i], own.at[0, i]),
            pltpu.make_async_copy(g_hbm.at[:, lanes_of(i)], g_own.at[i], own.at[1, i]),
        )

    def remote(source, target, send, recv, other):
        return pltpu.make_async_remote_copy(
            src_ref=source, dst_ref=target, send_sem=send, recv_sem=recv, device_id=other, device_id_type=MESH
        )

    def halo_copies(i):
        return (
            remote(ahead.at[i], from_before.at[i], halo_s.at[0, i], halo_r.at[0, i], after),
            remote(back.at[i], from_after.at[i], halo_s.at[1, i], halo_r.at[1, i], before),
        )

    sources = (sf_hbm, lf_hbm, fh_h, fp_h, fd_h, fph_h, fdn_h, fda_h, bl_h, bf_h, bd_h)
    targets = (sf, lf, fh, fp, fd, fph, fdn, fda, bl, bf, bd)
    consts = [pltpu.make_async_copy(a, b, loads.at[n]) for n, (a, b) in enumerate(zip(sources, targets))]
    for copy in consts[:1]:
        copy.start()
    for copy in own_copies(0):
        copy.start()
    barrier = pltpu.get_barrier_semaphore()
    for other in [*rings, after, before, *columns, *line]:
        pl.semaphore_signal(barrier, inc=1, device_id=other, device_id_type=MESH)
    for copy in consts[1:5]:
        copy.start()
    for i in range(1, groups):
        for copy in own_copies(i):
            copy.start()
    for copy in consts[5:]:
        copy.start()
    consts[0].wait()
    inner = (me > 0).astype(f32)
    outer = (me < count - 1).astype(f32)

    def lanes_t(t):
        return pl.ds(128 * t, 128)

    def taps(i, t):
        lanes = pl.ds(pl.multiple_of(i * GROUP + 128 * t, 128), 128)
        return lambda s, n: sf[s, n : n + 1, lanes]

    def feature(i, t, s, start, size, tap):
        total = None
        for n in range(7):
            term = xs[i, s, t, pl.ds(start + NEAR - n, size), :] * tap(s, n)
            total = term if total is None else total + term
        return total

    def features(i, t, q_start, kv_start, size, p_slot, p_row, d_slot, d_row, tap, own_rows=False):
        lanes = pl.ds(128 * t, 128)
        p_hi, p_lo = p_slot
        d_hi, d_lo = d_slot
        key = feature(i, t, 1, kv_start, size, tap)
        value = feature(i, t, 2, kv_start, size, tap)
        kf[i, t, pl.ds(kv_start, size), :] = key
        vf[i, t, pl.ds(kv_start, size), :] = value
        product = key * value
        if own_rows:
            pf[t, pl.ds(p_row, size), :] = product
        high, low = split(product)
        p_hi[pl.ds(p_row, size), lanes] = high
        p_lo[pl.ds(p_row, size), lanes] = low
        query = feature(i, t, 0, q_start, size, tap)
        gradient = query * gs[i, t, pl.ds(q_start, size), :]
        if own_rows:
            dfil[t, pl.ds(d_row, size), :] = gradient
        high, low = split(gradient)
        d_hi[pl.ds(d_row, size), lanes] = high
        d_lo[pl.ds(d_row, size), lanes] = low

    def at_slot(slot):
        return hi.at[slot], lo.at[slot]

    def tripled(high, low):
        return jnp.concatenate([high, low, high], axis=0)

    def taken(slot, size):
        return tripled(hi[slot, 0:size, :], lo[slot, 0:size, :])

    def put(slot, start, value):
        high, low = split(value)
        hi[slot, start : start + value.shape[0], :] = high
        lo[slot, start : start + value.shape[0], :] = low

    def near(i):
        for copy in own_copies(i):
            copy.wait()
        for t in range(TILES):
            lanes = lanes_t(t)
            xs[i, 0, t, NEAR : NEAR + 256] = x_own[i, 0, :, lanes].astype(f32)
            for s in (1, 2):
                xs[i, s, t, EDGE : EDGE + 256] = x_own[i, s, :, lanes].astype(f32)
            gs[i, t, 0:256] = g_own[i, :, lanes].astype(f32)
        product = (ohi.at[i, 0], olo.at[i, 0])
        gradient = (ohi.at[i, 1], olo.at[i, 1])
        for t in range(TILES):
            tap = taps(i, t)
            for row in range(0, OWN, CHUNK):
                features(i, t, NEAR + row, EDGE + row, CHUNK, product, row, gradient, row, tap, True)
            lanes = lanes_t(t)
            code, most = coded(pf[t, OWN - FAR : OWN, :])
            ahead[i, 0:FAR, lanes] = code
            for n, parts in enumerate(((jnp.broadcast_to(most, (8, 128)), xs[i, 0, t, 264:272]), (xs[i, 1, t, 392:400], xs[i, 2, t, 392:400]))):
                ahead[i, FAR + NEAR * n : FAR + NEAR * (n + 1), lanes] = jnp.concatenate(parts, axis=0).astype(bf16)
            code, most = coded(dfil[t, 0:FAR, :])
            back[i, 0:FAR, lanes] = code
            back[i, FAR : FAR + NEAR, lanes] = x_own[i, 0, 0:NEAR, lanes]
            back[i, FAR + NEAR : FAR + 2 * NEAR, lanes] = g_own[i, 0:NEAR, lanes]
            back[i, FAR + 2 * NEAR : FAR + 3 * NEAR, lanes] = jnp.concatenate(
                [xs[i, 1, t, EDGE : EDGE + 8], xs[i, 2, t, EDGE : EDGE + 8]], axis=0
            ).astype(bf16)
            back[i, FAR + 3 * NEAR : BACK, lanes] = jnp.broadcast_to(most, (NEAR, 128)).astype(bf16)

    def spectra(i):
        for b in range(8):
            put(2, 16 * b, lf[16 * b : 16 * b + 16, lanes_of(i)])
        sh[i] = dot(fh[...], taken(2, 128))
        sp[i] = dot(fp[...], tripled(ohi[i, 0], olo[i, 0]))
        sd[i] = dot(fd[...], tripled(ohi[i, 1], olo[i, 1]))

    def send_halo(i):
        for copy in halo_copies(i):
            copy.start()

    def local(i, _):
        near(i)
        spectra(i - 1)
        send_halo(i)
        return 0

    near(0)
    pl.semaphore_wait(barrier, 19)
    send_halo(0)
    for copy in consts[1:5]:
        copy.wait()
    lax.fori_loop(1, groups, local, 0)
    spectra(groups - 1)
    for copy in consts[5:]:
        copy.wait()

    mine = core * 2 + x
    trio = [(at(z, (x + n // 2) % 2, (core + n) % 2, hx, y), (core + n) % 2 * 2 + (x + n // 2) % 2) for n in (1, 2, 3)]

    def line_copies(i):
        return [
            remote(quart.at[i, whose], qbuf.at[i, n], line_s.at[i, n], line_r.at[i, n], other)
            for n, (other, whose) in enumerate(trio)
        ]

    def z_copies(i):
        return [
            remote(zsrc.at[lax.rem(z + n + 1, 8), i], zbuf.at[n, i], z_s.at[i, n], z_r.at[i, n], rings[n]) for n in range(7)
        ]

    def after_line(i):
        for copy in line_copies(i):
            copy.wait()
        total = quart[i, mine] + qbuf[i, 0] + qbuf[i, 1] + qbuf[i, 2]
        long_power, long_most = powered(total[0:64])
        short_power, short_most = powered(total[64:88])
        spot = lax.broadcasted_iota(jnp.int32, (24, 128), 0)
        short_power = jnp.where(spot == 7, long_most, jnp.where(spot == 15, short_most, short_power))
        for n in range(8):
            parts = [long_power[4 * n : 4 * n + 4], long_power[32 + 4 * n : 36 + 4 * n], short_power]
            zsrc[n, i] = jnp.concatenate(parts, axis=0).astype(bf16)

    def group(i, top):
        for copy in halo_copies(i):
            copy.wait_recv()
        for t in range(TILES):
            lanes = lanes_t(t)
            tap = taps(i, t)
            edge = from_before[i, FAR : FAR + NEAR, lanes].astype(f32) * inner
            pmost = edge[0:1]
            xs[i, 0, t, 8:NEAR] = edge[8:NEAR]
            edge = from_before[i, FAR + NEAR : AHEAD, lanes].astype(f32) * inner
            xs[i, 1, t, FAR + 8 : EDGE] = edge[0:8]
            xs[i, 2, t, FAR + 8 : EDGE] = edge[8:NEAR]
            xs[i, 0, t, NEAR + 256 : 2 * NEAR + 256] = from_after[i, FAR : FAR + NEAR, lanes].astype(f32)
            gs[i, t, 256 : 256 + NEAR] = from_after[i, FAR + NEAR : FAR + 2 * NEAR, lanes].astype(f32) * outer
            edge = from_after[i, FAR + 2 * NEAR : FAR + 3 * NEAR, lanes].astype(f32)
            for s in (1, 2):
                xs[i, s, t, EDGE + 256 : EDGE + 264] = edge[8 * s - 8 : 8 * s]
                xs[i, s, t, EDGE + 264 : SIZE] = jnp.zeros((8, 128), f32)
            dmost = from_after[i, FAR + 3 * NEAR : BACK, lanes].astype(f32)[0:1] * outer
            for c in range(0, FAR, 32):
                high, low = split(decoded(from_before[i, c : c + 32, lanes], pmost))
                hi[0, c : c + 32, lanes] = high
                lo[0, c : c + 32, lanes] = low
                high, low = split(decoded(from_after[i, c : c + 32, lanes], dmost))
                hi[1, NEAR + c : NEAR + c + 32, lanes] = high
                lo[1, NEAR + c : NEAR + c + 32, lanes] = low
            features(i, t, 0, FAR, NEAR, at_slot(0), FAR, at_slot(2), 0, tap)
            features(i, t, 256, EDGE + OWN, NEAR, at_slot(0), EDGE, at_slot(1), 0, tap)
        sp[i] = sp[i] + dot(fph[...], taken(0, EDGE + NEAR))
        sd[i] = sd[i] + dot(fdn[...], taken(2, NEAR))
        sx[...] = sd[i] + dot(fda[...], taken(1, EDGE))

        row = lax.broadcasted_iota(jnp.int32, (8, GROUP), 0)
        for b in range(PAIRS):

            def two(ref, b=b):
                return ref[16 * b : 16 * b + 8, :], ref[16 * b + 8 : 16 * b + 16, :]

            pr, pi = two(sp.at[i])
            hr, him = two(sh.at[i])
            dr, di = two(sd.at[i])
            xr, xi = two(sx)

            def pack(same, cross_, re, im, sign, special=b == 0):
                if special:
                    real = re + sign * jnp.where(row == 0, 0.0, same)
                    imag = jnp.where(row == 0, same, im + cross_)
                else:
                    real = re + same if sign > 0 else re - same
                    imag = im + cross_
                return jnp.concatenate([real, imag], axis=0)

            put(0, 16 * b, pack(di * pi, -(di * pr), dr * pr, dr * pi, 1.0))
            put(1, 16 * b, pack(pi * him, pi * hr, pr * hr, pr * him, -1.0))
            put(2, 16 * b, pack(xi * him, xi * hr, xr * hr, -(xr * him), 1.0))

        long_sum = dot(bl[...], taken(0, SIZE))
        for n in range(4):
            for t in range(TILES):
                quart[i, n, 32 * t : 32 * t + 32] = long_sum[32 * n : 32 * n + 32, 128 * t : 128 * t + 128]
        fil[...] = dot(bf[...], taken(1, SIZE))
        dpr[...] = dot(bd[...], taken(2, SIZE))

        for t in range(TILES):
            lanes = pl.ds(128 * t, 128)
            df[0, t, 0:KEEP, :] = gs[i, t, 0:KEEP, :] * fil[:, lanes]
            df[1, t, 0:KEEP, :] = dpr[:, lanes] * vf[i, t, 128 : 128 + KEEP, :]
            df[2, t, 0:KEEP, :] = dpr[:, lanes] * kf[i, t, 128 : 128 + KEEP, :]

        for t in range(TILES):
            short = []
            for s in range(3):
                shift = NEAR if s == 0 else EDGE
                sums = [jnp.zeros((8, 128), f32)] * 7
                for base in range(0, 256, 64):
                    here = df[s, t, pl.ds(base, 64), :]
                    for n in range(7):
                        term = here * xs[i, s, t, pl.ds(base + shift - n, 64), :]
                        sums[n] = sums[n] + jnp.sum(term.reshape(8, 8, 128), axis=0)
                short += [jnp.sum(v, axis=0, keepdims=True) for v in sums] + [jnp.zeros((1, 128), f32)]
            for n in range(2):
                quart[i, 2 * t + n, 64:88] = jnp.concatenate(short, axis=0)
        for copy in line_copies(i):
            copy.start()

        @pl.when(i > 1)
        def _():
            after_line(i - 2)
            for copy in z_copies(i - 2):
                copy.start()

        for t in range(TILES):
            lanes = lanes_t(t)
            tap = taps(i, t)
            for s in range(3):
                for base in range(0, 256, 64):
                    total = None
                    for n in range(7):
                        term = df[s, t, pl.ds(base + n, 64), :] * tap(s, n)
                        total = term if total is None else total + term
                    din[i, s, pl.ds(base, 64), lanes] = total
                    top = jnp.maximum(top, jnp.max(jnp.abs(total).reshape(8, 8, 128), axis=0))
        return top

    top = lax.fori_loop(0, groups, group, jnp.zeros((8, 128), f32))

    def spread(source, slots, first, others):
        copies = [remote(source, slots.at[n], epi_s.at[first + n], epi_r.at[first + n], o) for n, o in enumerate(others)]
        for copy in copies:
            copy.start()
        return copies

    def gather(top, copies, slots):
        for copy in copies:
            copy.wait_recv()
        for n in range(len(copies)):
            top = jnp.maximum(top, slots[n])
        return top

    pone[...] = top
    ones = spread(pone, pbuf1, 0, rings)
    zs = [copy for i in range(groups) for copy in z_copies(i)]
    for i in (groups - 2, groups - 1):
        after_line(i)
        for copy in zs[7 * i : 7 * i + 7]:
            copy.start()
    top = gather(top, ones, pbuf1)
    ptwo[...] = top
    twos = spread(ptwo, pbuf2, 7, line)
    top = gather(top, twos, pbuf2)
    pthree[...] = top
    threes = spread(pthree, pbuf3, 14, columns)
    for copy in zs:
        copy.wait_recv()
    for i in range(groups):
        long_sum, short_sum = 0.0, 0.0
        for n in range(8):
            block = (zsrc[z, i] if n == 7 else zbuf[n, i]).astype(f32)
            long_sum = long_sum + decoded(block[0:8], block[15:16])
            short_sum = short_sum + decoded(block[8:32], block[23:24])
        lout[:, GROUP * i : GROUP * i + 128] = long_sum[0:4]
        lout[:, GROUP * i + 128 : GROUP * (i + 1)] = long_sum[4:8]
        sout[core, i] = short_sum
    last = remote(sout.at[core], sout.at[core], epi_s.at[17], epi_r.at[17], pair)
    last.start()
    pout[...] = gather(top, threes, pbuf3)
    for copy in (*ones, *twos, *threes, *zs):
        copy.wait_send()
    for i in range(groups):
        for copy in halo_copies(i):
            copy.wait_send()
    last.wait()


def main(x3, cotangent, sf, lf):
    _, rows, chan = x3.shape
    consts = [jnp.asarray(c) for c in transforms()]
    groups = chan // GROUP
    anywhere = pl.BlockSpec(memory_space=pl.ANY)
    vmem = pl.BlockSpec(memory_space=pltpu.VMEM)
    V = pltpu.VMEM
    D = pltpu.SemaphoreType.DMA
    return pl.pallas_call(
        main_kernel,
        out_shape=[
            V((groups, 3, rows, GROUP), f32),
            V((4, chan), f32),
            V((2, groups, 24, 128), f32),
            V((8, 128), f32),
        ],
        in_specs=[anywhere] * (4 + len(consts)),
        out_specs=[vmem, vmem, vmem, vmem],
        scratch_shapes=[
            V((groups, 3, rows, GROUP), bf16),
            V((groups, rows, GROUP), bf16),
            V((groups, AHEAD, GROUP), bf16),
            V((groups, BACK, GROUP), bf16),
            V((groups, AHEAD, GROUP), bf16),
            V((groups, BACK, GROUP), bf16),
            V((TILES, OWN, 128), f32),
            V((TILES, OWN, 128), f32),
            V(sf.shape, f32),
            V(lf.shape, f32),
            *[V(c.shape, bf16) for c in consts],
            V((groups, 3, TILES, SIZE, 128), f32),
            V((groups, TILES, SPAN, 128), f32),
            V((groups, TILES, SPAN, 128), f32),
            V((groups, TILES, SPAN, 128), f32),
            V((groups, SIZE, GROUP), f32),
            V((groups, SIZE, GROUP), f32),
            V((groups, SIZE, GROUP), f32),
            V((groups, 2, OWN, GROUP), bf16),
            V((groups, 2, OWN, GROUP), bf16),
            V((3, SIZE, GROUP), bf16),
            V((3, SIZE, GROUP), bf16),
            V((SIZE, GROUP), f32),
            V((KEEP, GROUP), f32),
            V((KEEP, GROUP), f32),
            V((3, TILES, KEEP + 8, 128), f32),
            V((groups, 4, 88, 128), f32),
            V((groups, 3, 88, 128), f32),
            V((8, groups, 32, 128), bf16),
            V((7, groups, 32, 128), bf16),
            V((7, 8, 128), f32),
            V((7, 8, 128), f32),
            V((3, 8, 128), f32),
            V((8, 128), f32),
            V((8, 128), f32),
            V((8, 128), f32),
            D((11,)),
            D((2, groups)),
            D((2, groups)),
            D((2, groups)),
            D((groups, 3)),
            D((groups, 3)),
            D((groups, 7)),
            D((groups, 7)),
            D((18,)),
            D((18,)),
        ],
        compiler_params=pltpu.CompilerParams(
            collective_id=0, has_side_effects=True, vmem_limit_bytes=60 * 1024 * 1024
        ),
        name="gradients",
    )(x3, cotangent, sf, lf, *consts)


STEPS = 2


def scale_kernel(din, lsum, ssum, peak, out_hbm, lout, sout, scale, out, stores):
    groups, streams, rows, _ = din.shape
    step = rows // STEPS
    top = jnp.max(peak[...]) + EPSILON
    factor = FP8_RANGE / top
    copies = []
    for s in range(streams):
        for n in range(STEPS):
            here = pl.ds(n * step, step)
            for i in range(groups):
                out[s, here, GROUP * i : GROUP * (i + 1)] = (din[i, s, here, :] * factor).astype(bf16)
            copies.append(pltpu.make_async_copy(out.at[s, here], out_hbm.at[s, here], stores.at[s * STEPS + n]))
            copies[-1].start()
    scale[0, 0] = top / FP8_RANGE
    lout[...] = lsum[...]
    for c in range(2):
        for i in range(groups):
            lanes = pl.ds(GROUP * i + 128 * c, 128)
            for s in range(streams):
                sout[s, :, lanes] = ssum[c, i, 8 * s : 8 * s + 7]
    for copy in copies:
        copy.wait()


def scaled(din, lsum, ssum, peak):
    groups, _, rows, _ = din.shape
    chan = groups * GROUP
    vmem = pl.BlockSpec(memory_space=pltpu.VMEM)
    anywhere = pl.BlockSpec(memory_space=pl.ANY)
    din, lsum, ssum, peak = [pltpu.with_memory_space_constraint(a, pltpu.VMEM) for a in (din, lsum, ssum, peak)]
    return pl.pallas_call(
        scale_kernel,
        out_shape=[
            jax.ShapeDtypeStruct((3, rows, chan), bf16),
            jax.ShapeDtypeStruct((4, chan), f32),
            jax.ShapeDtypeStruct((3, 7, chan), f32),
            jax.ShapeDtypeStruct((1, 1), f32),
        ],
        in_specs=[vmem, vmem, vmem, vmem],
        out_specs=[anywhere, vmem, vmem, pl.BlockSpec(memory_space=pltpu.SMEM)],
        scratch_shapes=[pltpu.VMEM((3, rows, chan), bf16), pltpu.SemaphoreType.DMA((3 * STEPS,))],
        compiler_params=pltpu.CompilerParams(vmem_limit_bytes=32 * 1024 * 1024),
        name="scaling",
    )(din, lsum, ssum, peak)


def body(projected, cotangent, short_filter, long_filter):
    x3 = projected.transpose(1, 0, 2)
    sf = short_filter.transpose(1, 0, 2)
    out, long_grad, short_grad, scale = scaled(*main(x3, cotangent, sf, long_filter))
    return out.transpose(1, 0, 2), long_grad, short_grad.transpose(1, 0, 2), scale.reshape(())


def solution(mesh):
    placed = (P("ctx", None, "tp"), P("ctx", "tp"), P(None, None, "tp"), P(None, "tp"))
    return jax.shard_map(
        body,
        mesh=mesh,
        in_specs=placed,
        out_specs=(P("ctx", None, "tp"), P("ctx", "tp"), P(None, None, "tp"), P()),
        check_vma=False,
    )
```

```python
import functools

import jax
import jax.numpy as jnp
import ml_dtypes
import numpy as np
from jax import lax
from jax.experimental import pallas as pl
from jax.experimental.pallas import tpu as pltpu
from jax.sharding import PartitionSpec as P

EPSILON = 1e-06
FP8_RANGE = 448.0
MESH = pl.DeviceIdType.MESH

SIZE = 416
PAIRS = SIZE // 16
EDGE = 144
NEAR = 16
FAR = 128
AHEAD = FAR + 2 * NEAR
BACK = FAR + 4 * NEAR
POWER = 11
REACH = 2048.0
LEAST = 1e-30
OWN = 240
SPAN = 400
KEEP = 264
GROUP = 256
TILES = GROUP // 128
CHUNK = 48
f32 = jnp.float32
bf16 = jnp.bfloat16


def joined_np(matrix):
    high = matrix.astype(ml_dtypes.bfloat16)
    low = (matrix - high.astype(np.float64)).astype(ml_dtypes.bfloat16)
    return np.concatenate([high, high, low], axis=1)


@functools.lru_cache(None)
def transforms():
    m = np.arange(SIZE)[None, :]
    k = np.arange(SIZE // 2)[:, None]
    re = np.cos(2 * np.pi * ((k * m) % SIZE) / SIZE)
    im = -np.sin(2 * np.pi * ((k * m) % SIZE) / SIZE)
    im[0] = np.cos(np.pi * m[0])
    weight = np.full((SIZE // 2, 1), 2.0 / SIZE)
    weight[0] = 1.0 / SIZE

    def blocks(a, b):
        return np.stack([a.reshape(PAIRS, 8, SIZE), b.reshape(PAIRS, 8, SIZE)], axis=1).reshape(SIZE, SIZE)

    ahead = blocks(re, im)
    back = blocks(re * weight, im * weight).T
    c = np.arange(128)
    core, x, z, r = c // 64, (c // 32) % 2, (c // 4) % 8, c % 4
    lag = 128 - ((z * 4 + x * 2 + core) * 4 + r)
    return (
        joined_np(ahead[:, :128]),
        joined_np(ahead[:, EDGE : EDGE + OWN]),
        joined_np(ahead[:, NEAR : NEAR + OWN]),
        joined_np(np.concatenate([ahead[:, :EDGE], ahead[:, EDGE + OWN : SPAN]], axis=1)),
        joined_np(ahead[:, :NEAR]),
        joined_np(ahead[:, NEAR + OWN : SPAN]),
        joined_np(back[lag]),
        joined_np(back[128 : 128 + KEEP]),
        joined_np(back[:KEEP]),
    )


def split(value):
    high = value.astype(bf16)
    low = (value - high.astype(f32)).astype(bf16)
    return high, low


def powered(value):
    most = jnp.maximum(jnp.max(jnp.abs(value), axis=0, keepdims=True), LEAST).astype(bf16).astype(f32)
    u = value * (REACH / most)
    u2 = u * u
    u4 = u2 * u2
    return (u4 * u4) * (u2 * u), most


def coded(value):
    power, most = powered(value)
    return power.astype(bf16), most


def decoded(code, most):
    y = code.astype(f32)
    root = jnp.exp2(jnp.log2(jnp.maximum(jnp.abs(y), 1.2e-38)) * (1.0 / POWER))
    return jnp.where(y < 0, -root, root) * (most * (1.0 / REACH))


def dot(a, b):
    return lax.dot_general(a, b, (((1,), (0,)), ((), ())), preferred_element_type=f32)


def main_kernel(
    x_hbm, g_hbm, sf_hbm, lf_hbm, fh_h, fp_h, fd_h, fph_h, fdn_h, fda_h, bl_h, bf_h, bd_h,
    din, lout, sout, pout,
    x_own, g_own, ahead, back, from_before, from_after, pf, dfil, sf, lf, fh, fp, fd, fph, fdn, fda, bl, bf, bd,
    xs, gs, kf, vf, sp, sd, sh, ohi, olo, hi, lo, sx, fil, dpr, df,
    quart, qbuf, zsrc, zbuf, pbuf1, pbuf2, pbuf3, pone, ptwo, pthree,
    loads, own, halo_s, halo_r, line_s, line_r, z_s, z_r, epi_s, epi_r,
):
    me = lax.axis_index("ctx")
    count = lax.axis_size("ctx")
    tp = lax.axis_index("tp")
    after = {"ctx": lax.rem(me + 1, count)}
    before = {"ctx": lax.rem(me + count - 1, count)}
    core = lax.rem(me, 2)
    x = lax.rem(me // 2, 2)
    z = me // 4
    hx = tp // 4
    y = lax.rem(tp, 4)
    rows = x_hbm.shape[1]
    groups = x_own.shape[0]

    def at(zz, xx, cc, hh, yy):
        return {"ctx": zz * 4 + xx * 2 + cc, "tp": hh * 4 + yy}

    pair = at(z, x, 1 - core, hx, y)
    rings = [at(lax.rem(z + n, 8), x, core, hx, y) for n in range(1, 8)]
    columns = [at(z, x, core, hx, lax.rem(y + n, 4)) for n in range(1, 4)]
    line = [at(z, (x + n // 2) % 2, (core + n) % 2, (hx + n // 4) % 2, y) for n in range(1, 8)]

    def lanes_of(i):
        return pl.ds(pl.multiple_of(i * GROUP, GROUP), GROUP)

    def own_copies(i):
        return (
            pltpu.make_async_copy(x_hbm.at[:, :, lanes_of(i)], x_own.at[i], own.at[0, i]),
            pltpu.make_async_copy(g_hbm.at[:, lanes_of(i)], g_own.at[i], own.at[1, i]),
        )

    def remote(source, target, send, recv, other):
        return pltpu.make_async_remote_copy(
            src_ref=source, dst_ref=target, send_sem=send, recv_sem=recv, device_id=other, device_id_type=MESH
        )

    def halo_copies(i):
        return (
            remote(ahead.at[i], from_before.at[i], halo_s.at[0, i], halo_r.at[0, i], after),
            remote(back.at[i], from_after.at[i], halo_s.at[1, i], halo_r.at[1, i], before),
        )

    sources = (sf_hbm, lf_hbm, fh_h, fp_h, fd_h, fph_h, fdn_h, fda_h, bl_h, bf_h, bd_h)
    targets = (sf, lf, fh, fp, fd, fph, fdn, fda, bl, bf, bd)
    consts = [pltpu.make_async_copy(a, b, loads.at[n]) for n, (a, b) in enumerate(zip(sources, targets))]
    for copy in consts[:1]:
        copy.start()
    for copy in own_copies(0):
        copy.start()
    barrier = pltpu.get_barrier_semaphore()
    for other in [*rings, after, before, *columns, *line]:
        pl.semaphore_signal(barrier, inc=1, device_id=other, device_id_type=MESH)
    for copy in consts[1:5]:
        copy.start()
    for i in range(1, groups):
        for copy in own_copies(i):
            copy.start()
    for copy in consts[5:]:
        copy.start()
    consts[0].wait()
    inner = (me > 0).astype(f32)
    outer = (me < count - 1).astype(f32)

    def lanes_t(t):
        return pl.ds(128 * t, 128)

    def taps(i, t):
        lanes = pl.ds(pl.multiple_of(i * GROUP + 128 * t, 128), 128)
        return lambda s, n: sf[s, n : n + 1, lanes]

    def feature(i, t, s, start, size, tap):
        total = None
        for n in range(7):
            term = xs[i, s, t, pl.ds(start + NEAR - n, size), :] * tap(s, n)
            total = term if total is None else total + term
        return total

    def features(i, t, q_start, kv_start, size, p_slot, p_row, d_slot, d_row, tap, own_rows=False):
        lanes = pl.ds(128 * t, 128)
        p_hi, p_lo = p_slot
        d_hi, d_lo = d_slot
        key = feature(i, t, 1, kv_start, size, tap)
        value = feature(i, t, 2, kv_start, size, tap)
        kf[i, t, pl.ds(kv_start, size), :] = key
        vf[i, t, pl.ds(kv_start, size), :] = value
        product = key * value
        if own_rows:
            pf[t, pl.ds(p_row, size), :] = product
        high, low = split(product)
        p_hi[pl.ds(p_row, size), lanes] = high
        p_lo[pl.ds(p_row, size), lanes] = low
        query = feature(i, t, 0, q_start, size, tap)
        gradient = query * gs[i, t, pl.ds(q_start, size), :]
        if own_rows:
            dfil[t, pl.ds(d_row, size), :] = gradient
        high, low = split(gradient)
        d_hi[pl.ds(d_row, size), lanes] = high
        d_lo[pl.ds(d_row, size), lanes] = low

    def at_slot(slot):
        return hi.at[slot], lo.at[slot]

    def tripled(high, low):
        return jnp.concatenate([high, low, high], axis=0)

    def taken(slot, size):
        return tripled(hi[slot, 0:size, :], lo[slot, 0:size, :])

    def put(slot, start, value):
        high, low = split(value)
        hi[slot, start : start + value.shape[0], :] = high
        lo[slot, start : start + value.shape[0], :] = low

    def near(i):
        for copy in own_copies(i):
            copy.wait()
        for t in range(TILES):
            lanes = lanes_t(t)
            xs[i, 0, t, NEAR : NEAR + 256] = x_own[i, 0, :, lanes].astype(f32)
            for s in (1, 2):
                xs[i, s, t, EDGE : EDGE + 256] = x_own[i, s, :, lanes].astype(f32)
            gs[i, t, 0:256] = g_own[i, :, lanes].astype(f32)
        product = (ohi.at[i, 0], olo.at[i, 0])
        gradient = (ohi.at[i, 1], olo.at[i, 1])
        for t in range(TILES):
            tap = taps(i, t)
            for row in range(0, OWN, CHUNK):
                features(i, t, NEAR + row, EDGE + row, CHUNK, product, row, gradient, row, tap, True)
            lanes = lanes_t(t)
            code, most = coded(pf[t, OWN - FAR : OWN, :])
            ahead[i, 0:FAR, lanes] = code
            for n, parts in enumerate(((jnp.broadcast_to(most, (8, 128)), xs[i, 0, t, 264:272]), (xs[i, 1, t, 392:400], xs[i, 2, t, 392:400]))):
                ahead[i, FAR + NEAR * n : FAR + NEAR * (n + 1), lanes] = jnp.concatenate(parts, axis=0).astype(bf16)
            code, most = coded(dfil[t, 0:FAR, :])
            back[i, 0:FAR, lanes] = code
            back[i, FAR : FAR + NEAR, lanes] = x_own[i, 0, 0:NEAR, lanes]
            back[i, FAR + NEAR : FAR + 2 * NEAR, lanes] = g_own[i, 0:NEAR, lanes]
            back[i, FAR + 2 * NEAR : FAR + 3 * NEAR, lanes] = jnp.concatenate(
                [xs[i, 1, t, EDGE : EDGE + 8], xs[i, 2, t, EDGE : EDGE + 8]], axis=0
            ).astype(bf16)
            back[i, FAR + 3 * NEAR : BACK, lanes] = jnp.broadcast_to(most, (NEAR, 128)).astype(bf16)

    def spectra(i):
        for b in range(8):
            put(2, 16 * b, lf[16 * b : 16 * b + 16, lanes_of(i)])
        sh[i] = dot(fh[...], taken(2, 128))
        sp[i] = dot(fp[...], tripled(ohi[i, 0], olo[i, 0]))
        sd[i] = dot(fd[...], tripled(ohi[i, 1], olo[i, 1]))

    def send_halo(i):
        for copy in halo_copies(i):
            copy.start()

    def local(i, _):
        near(i)
        spectra(i - 1)
        send_halo(i)
        return 0

    near(0)
    pl.semaphore_wait(barrier, 19)
    send_halo(0)
    for copy in consts[1:5]:
        copy.wait()
    lax.fori_loop(1, groups, local, 0)
    spectra(groups - 1)
    for copy in consts[5:]:
        copy.wait()

    mine = core * 2 + x
    trio = [(at(z, (x + n // 2) % 2, (core + n) % 2, hx, y), (core + n) % 2 * 2 + (x + n // 2) % 2) for n in (3, 2, 1)]

    def line_copies(i):
        return [
            remote(quart.at[i, whose], qbuf.at[i, n], line_s.at[i, n], line_r.at[i, n], other)
            for n, (other, whose) in enumerate(trio)
        ]

    def z_copies(i):
        return [
            remote(zsrc.at[lax.rem(z + n + 1, 8), i], zbuf.at[n, i], z_s.at[i, n], z_r.at[i, n], rings[n]) for n in range(7)
        ]

    def after_line(i):
        for copy in line_copies(i):
            copy.wait()
        total = quart[i, mine] + qbuf[i, 0] + qbuf[i, 1] + qbuf[i, 2]
        long_power, long_most = powered(total[0:64])
        short_power, short_most = powered(total[64:88])
        spot = lax.broadcasted_iota(jnp.int32, (24, 128), 0)
        short_power = jnp.where(spot == 7, long_most, jnp.where(spot == 15, short_most, short_power))
        for n in range(8):
            parts = [long_power[4 * n : 4 * n + 4], long_power[32 + 4 * n : 36 + 4 * n], short_power]
            zsrc[n, i] = jnp.concatenate(parts, axis=0).astype(bf16)

    def group(i, top):
        for copy in halo_copies(i):
            copy.wait_recv()
        for t in range(TILES):
            lanes = lanes_t(t)
            tap = taps(i, t)
            edge = from_before[i, FAR : FAR + NEAR, lanes].astype(f32) * inner
            pmost = edge[0:1]
            xs[i, 0, t, 8:NEAR] = edge[8:NEAR]
            edge = from_before[i, FAR + NEAR : AHEAD, lanes].astype(f32) * inner
            xs[i, 1, t, FAR + 8 : EDGE] = edge[0:8]
            xs[i, 2, t, FAR + 8 : EDGE] = edge[8:NEAR]
            xs[i, 0, t, NEAR + 256 : 2 * NEAR + 256] = from_after[i, FAR : FAR + NEAR, lanes].astype(f32)
            gs[i, t, 256 : 256 + NEAR] = from_after[i, FAR + NEAR : FAR + 2 * NEAR, lanes].astype(f32) * outer
            edge = from_after[i, FAR + 2 * NEAR : FAR + 3 * NEAR, lanes].astype(f32)
            for s in (1, 2):
                xs[i, s, t, EDGE + 256 : EDGE + 264] = edge[8 * s - 8 : 8 * s]
                xs[i, s, t, EDGE + 264 : SIZE] = jnp.zeros((8, 128), f32)
            dmost = from_after[i, FAR + 3 * NEAR : BACK, lanes].astype(f32)[0:1] * outer
            for c in range(0, FAR, 32):
                high, low = split(decoded(from_before[i, c : c + 32, lanes], pmost))
                hi[0, c : c + 32, lanes] = high
                lo[0, c : c + 32, lanes] = low
                high, low = split(decoded(from_after[i, c : c + 32, lanes], dmost))
                hi[1, NEAR + c : NEAR + c + 32, lanes] = high
                lo[1, NEAR + c : NEAR + c + 32, lanes] = low
            features(i, t, 0, FAR, NEAR, at_slot(0), FAR, at_slot(2), 0, tap)
            features(i, t, 256, EDGE + OWN, NEAR, at_slot(0), EDGE, at_slot(1), 0, tap)
        sp[i] = sp[i] + dot(fph[...], taken(0, EDGE + NEAR))
        sd[i] = sd[i] + dot(fdn[...], taken(2, NEAR))
        sx[...] = sd[i] + dot(fda[...], taken(1, EDGE))

        row = lax.broadcasted_iota(jnp.int32, (8, GROUP), 0)
        for b in range(PAIRS):

            def two(ref, b=b):
                return ref[16 * b : 16 * b + 8, :], ref[16 * b + 8 : 16 * b + 16, :]

            pr, pi = two(sp.at[i])
            hr, him = two(sh.at[i])
            dr, di = two(sd.at[i])
            xr, xi = two(sx)

            def pack(same, cross_, re, im, sign, special=b == 0):
                if special:
                    real = re + sign * jnp.where(row == 0, 0.0, same)
                    imag = jnp.where(row == 0, same, im + cross_)
                else:
                    real = re + same if sign > 0 else re - same
                    imag = im + cross_
                return jnp.concatenate([real, imag], axis=0)

            put(0, 16 * b, pack(di * pi, -(di * pr), dr * pr, dr * pi, 1.0))
            put(1, 16 * b, pack(pi * him, pi * hr, pr * hr, pr * him, -1.0))
            put(2, 16 * b, pack(xi * him, xi * hr, xr * hr, -(xr * him), 1.0))

        long_sum = dot(bl[...], taken(0, SIZE))
        for n in range(4):
            for t in range(TILES):
                quart[i, n, 32 * t : 32 * t + 32] = long_sum[32 * n : 32 * n + 32, 128 * t : 128 * t + 128]
        fil[...] = dot(bf[...], taken(1, SIZE))
        dpr[...] = dot(bd[...], taken(2, SIZE))

        for t in range(TILES):
            lanes = pl.ds(128 * t, 128)
            df[0, t, 0:KEEP, :] = gs[i, t, 0:KEEP, :] * fil[:, lanes]
            df[1, t, 0:KEEP, :] = dpr[:, lanes] * vf[i, t, 128 : 128 + KEEP, :]
            df[2, t, 0:KEEP, :] = dpr[:, lanes] * kf[i, t, 128 : 128 + KEEP, :]

        for t in range(TILES):
            short = []
            for s in range(3):
                shift = NEAR if s == 0 else EDGE
                sums = [jnp.zeros((8, 128), f32)] * 7
                for base in range(0, 256, 64):
                    here = df[s, t, pl.ds(base, 64), :]
                    for n in range(7):
                        term = here * xs[i, s, t, pl.ds(base + shift - n, 64), :]
                        sums[n] = sums[n] + jnp.sum(term.reshape(8, 8, 128), axis=0)
                short += [jnp.sum(v, axis=0, keepdims=True) for v in sums] + [jnp.zeros((1, 128), f32)]
            for n in range(2):
                quart[i, 2 * t + n, 64:88] = jnp.concatenate(short, axis=0)
        for copy in line_copies(i):
            copy.start()

        for t in range(TILES):
            lanes = lanes_t(t)
            tap = taps(i, t)
            for s in range(3):
                for base in range(0, 256, 64):
                    total = None
                    for n in range(7):
                        term = df[s, t, pl.ds(base + n, 64), :] * tap(s, n)
                        total = term if total is None else total + term
                    din[i, s, pl.ds(base, 64), lanes] = total
                    top = jnp.maximum(top, jnp.max(jnp.abs(total).reshape(8, 8, 128), axis=0))
        return top

    top = lax.fori_loop(0, groups, group, jnp.zeros((8, 128), f32))

    def spread(source, slots, first, others):
        copies = [remote(source, slots.at[n], epi_s.at[first + n], epi_r.at[first + n], o) for n, o in enumerate(others)]
        for copy in copies:
            copy.start()
        return copies

    def gather(top, copies, slots):
        for copy in copies:
            copy.wait_recv()
        for n in range(len(copies)):
            top = jnp.maximum(top, slots[n])
        return top

    pone[...] = top
    ones = spread(pone, pbuf1, 0, rings)
    zs = [copy for i in range(groups) for copy in z_copies(i)]
    for i in range(groups):
        after_line(i)
        for copy in zs[7 * i : 7 * i + 7]:
            copy.start()
    top = gather(top, ones, pbuf1)
    ptwo[...] = top
    twos = spread(ptwo, pbuf2, 7, line)
    top = gather(top, twos, pbuf2)
    pthree[...] = top
    threes = spread(pthree, pbuf3, 14, columns)
    for copy in zs:
        copy.wait_recv()
    for i in range(groups):
        long_sum, short_sum = 0.0, 0.0
        for n in range(8):
            block = (zsrc[z, i] if n == 7 else zbuf[n, i]).astype(f32)
            long_sum = long_sum + decoded(block[0:8], block[15:16])
            short_sum = short_sum + decoded(block[8:32], block[23:24])
        lout[:, GROUP * i : GROUP * i + 128] = long_sum[0:4]
        lout[:, GROUP * i + 128 : GROUP * (i + 1)] = long_sum[4:8]
        sout[core, i] = short_sum
    last = remote(sout.at[core], sout.at[core], epi_s.at[17], epi_r.at[17], pair)
    last.start()
    pout[...] = gather(top, threes, pbuf3)
    for copy in (*ones, *twos, *threes, *zs):
        copy.wait_send()
    for i in range(groups):
        for copy in halo_copies(i):
            copy.wait_send()
    last.wait()


def main(x3, cotangent, sf, lf):
    _, rows, chan = x3.shape
    consts = [jnp.asarray(c) for c in transforms()]
    groups = chan // GROUP
    anywhere = pl.BlockSpec(memory_space=pl.ANY)
    vmem = pl.BlockSpec(memory_space=pltpu.VMEM)
    V = pltpu.VMEM
    D = pltpu.SemaphoreType.DMA
    return pl.pallas_call(
        main_kernel,
        out_shape=[
            V((groups, 3, rows, GROUP), f32),
            V((4, chan), f32),
            V((2, groups, 24, 128), f32),
            V((8, 128), f32),
        ],
        in_specs=[anywhere] * (4 + len(consts)),
        out_specs=[vmem, vmem, vmem, vmem],
        scratch_shapes=[
            V((groups, 3, rows, GROUP), bf16),
            V((groups, rows, GROUP), bf16),
            V((groups, AHEAD, GROUP), bf16),
            V((groups, BACK, GROUP), bf16),
            V((groups, AHEAD, GROUP), bf16),
            V((groups, BACK, GROUP), bf16),
            V((TILES, OWN, 128), f32),
            V((TILES, OWN, 128), f32),
            V(sf.shape, f32),
            V(lf.shape, f32),
            *[V(c.shape, bf16) for c in consts],
            V((groups, 3, TILES, SIZE, 128), f32),
            V((groups, TILES, SPAN, 128), f32),
            V((groups, TILES, SPAN, 128), f32),
            V((groups, TILES, SPAN, 128), f32),
            V((groups, SIZE, GROUP), f32),
            V((groups, SIZE, GROUP), f32),
            V((groups, SIZE, GROUP), f32),
            V((groups, 2, OWN, GROUP), bf16),
            V((groups, 2, OWN, GROUP), bf16),
            V((3, SIZE, GROUP), bf16),
            V((3, SIZE, GROUP), bf16),
            V((SIZE, GROUP), f32),
            V((KEEP, GROUP), f32),
            V((KEEP, GROUP), f32),
            V((3, TILES, KEEP + 8, 128), f32),
            V((groups, 4, 88, 128), f32),
            V((groups, 3, 88, 128), f32),
            V((8, groups, 32, 128), bf16),
            V((7, groups, 32, 128), bf16),
            V((7, 8, 128), f32),
            V((7, 8, 128), f32),
            V((3, 8, 128), f32),
            V((8, 128), f32),
            V((8, 128), f32),
            V((8, 128), f32),
            D((11,)),
            D((2, groups)),
            D((2, groups)),
            D((2, groups)),
            D((groups, 3)),
            D((groups, 3)),
            D((groups, 7)),
            D((groups, 7)),
            D((18,)),
            D((18,)),
        ],
        compiler_params=pltpu.CompilerParams(
            collective_id=0, has_side_effects=True, vmem_limit_bytes=60 * 1024 * 1024
        ),
        name="gradients",
    )(x3, cotangent, sf, lf, *consts)


STEPS = 2


def scale_kernel(din, lsum, ssum, peak, out_hbm, lout, sout, scale, out, stores):
    groups, streams, rows, _ = din.shape
    step = rows // STEPS
    top = jnp.max(peak[...]) + EPSILON
    factor = FP8_RANGE / top
    copies = []
    for s in range(streams):
        for n in range(STEPS):
            here = pl.ds(n * step, step)
            for i in range(groups):
                out[s, here, GROUP * i : GROUP * (i + 1)] = (din[i, s, here, :] * factor).astype(bf16)
            copies.append(pltpu.make_async_copy(out.at[s, here], out_hbm.at[s, here], stores.at[s * STEPS + n]))
            copies[-1].start()
    scale[0, 0] = top / FP8_RANGE
    lout[...] = lsum[...]
    for c in range(2):
        for i in range(groups):
            lanes = pl.ds(GROUP * i + 128 * c, 128)
            for s in range(streams):
                sout[s, :, lanes] = ssum[c, i, 8 * s : 8 * s + 7]
    for copy in copies:
        copy.wait()


def scaled(din, lsum, ssum, peak):
    groups, _, rows, _ = din.shape
    chan = groups * GROUP
    vmem = pl.BlockSpec(memory_space=pltpu.VMEM)
    anywhere = pl.BlockSpec(memory_space=pl.ANY)
    din, lsum, ssum, peak = [pltpu.with_memory_space_constraint(a, pltpu.VMEM) for a in (din, lsum, ssum, peak)]
    return pl.pallas_call(
        scale_kernel,
        out_shape=[
            jax.ShapeDtypeStruct((3, rows, chan), bf16),
            jax.ShapeDtypeStruct((4, chan), f32),
            jax.ShapeDtypeStruct((3, 7, chan), f32),
            jax.ShapeDtypeStruct((1, 1), f32),
        ],
        in_specs=[vmem, vmem, vmem, vmem],
        out_specs=[anywhere, vmem, vmem, pl.BlockSpec(memory_space=pltpu.SMEM)],
        scratch_shapes=[pltpu.VMEM((3, rows, chan), bf16), pltpu.SemaphoreType.DMA((3 * STEPS,))],
        compiler_params=pltpu.CompilerParams(vmem_limit_bytes=32 * 1024 * 1024),
        name="scaling",
    )(din, lsum, ssum, peak)


def body(projected, cotangent, short_filter, long_filter):
    x3 = projected.transpose(1, 0, 2)
    sf = short_filter.transpose(1, 0, 2)
    out, long_grad, short_grad, scale = scaled(*main(x3, cotangent, sf, long_filter))
    return out.transpose(1, 0, 2), long_grad, short_grad.transpose(1, 0, 2), scale.reshape(())


def solution(mesh):
    placed = (P("ctx", None, "tp"), P("ctx", "tp"), P(None, None, "tp"), P(None, "tp"))
    return jax.shard_map(
        body,
        mesh=mesh,
        in_specs=placed,
        out_specs=(P("ctx", None, "tp"), P("ctx", "tp"), P(None, None, "tp"), P()),
        check_vma=False,
    )
```

```python
import functools

import jax
import jax.numpy as jnp
import ml_dtypes
import numpy as np
from jax import lax
from jax.experimental import pallas as pl
from jax.experimental.pallas import tpu as pltpu
from jax.sharding import PartitionSpec as P

EPSILON = 1e-06
FP8_RANGE = 448.0
MESH = pl.DeviceIdType.MESH

SIZE = 416
PAIRS = SIZE // 16
EDGE = 144
NEAR = 16
FAR = 128
AHEAD = FAR + 2 * NEAR
BACK = FAR + 4 * NEAR
POWER = 11
REACH = 2048.0
LEAST = 1e-30
OWN = 240
SPAN = 400
KEEP = 264
GROUP = 256
TILES = GROUP // 128
CHUNK = 48
f32 = jnp.float32
bf16 = jnp.bfloat16


def joined_np(matrix):
    high = matrix.astype(ml_dtypes.bfloat16)
    low = (matrix - high.astype(np.float64)).astype(ml_dtypes.bfloat16)
    return np.concatenate([high, high, low], axis=1)


@functools.lru_cache(None)
def transforms():
    m = np.arange(SIZE)[None, :]
    k = np.arange(SIZE // 2)[:, None]
    re = np.cos(2 * np.pi * ((k * m) % SIZE) / SIZE)
    im = -np.sin(2 * np.pi * ((k * m) % SIZE) / SIZE)
    im[0] = np.cos(np.pi * m[0])
    weight = np.full((SIZE // 2, 1), 2.0 / SIZE)
    weight[0] = 1.0 / SIZE

    def blocks(a, b):
        return np.stack([a.reshape(PAIRS, 8, SIZE), b.reshape(PAIRS, 8, SIZE)], axis=1).reshape(SIZE, SIZE)

    ahead = blocks(re, im)
    back = blocks(re * weight, im * weight).T
    c = np.arange(128)
    core, x, z, r = c // 64, (c // 32) % 2, (c // 4) % 8, c % 4
    lag = 128 - ((z * 4 + x * 2 + core) * 4 + r)
    return (
        joined_np(ahead[:, :128]),
        joined_np(ahead[:, EDGE : EDGE + OWN]),
        joined_np(ahead[:, NEAR : NEAR + OWN]),
        joined_np(np.concatenate([ahead[:, :EDGE], ahead[:, EDGE + OWN : SPAN]], axis=1)),
        joined_np(ahead[:, :NEAR]),
        joined_np(ahead[:, NEAR + OWN : SPAN]),
        joined_np(back[lag]),
        joined_np(back[128 : 128 + KEEP]),
        joined_np(back[:KEEP]),
    )


def split(value):
    high = value.astype(bf16)
    low = (value - high.astype(f32)).astype(bf16)
    return high, low


def powered(value):
    most = jnp.maximum(jnp.max(jnp.abs(value), axis=0, keepdims=True), LEAST).astype(bf16).astype(f32)
    u = value * (REACH / most)
    u2 = u * u
    u4 = u2 * u2
    return (u4 * u4) * (u2 * u), most


def coded(value):
    power, most = powered(value)
    return power.astype(bf16), most


def decoded(code, most):
    y = code.astype(f32)
    root = jnp.exp2(jnp.log2(jnp.maximum(jnp.abs(y), 1.2e-38)) * (1.0 / POWER))
    return jnp.where(y < 0, -root, root) * (most * (1.0 / REACH))


def dot(a, b):
    return lax.dot_general(a, b, (((1,), (0,)), ((), ())), preferred_element_type=f32)


def main_kernel(
    x_hbm, g_hbm, sf_hbm, lf_hbm, fh_h, fp_h, fd_h, fph_h, fdn_h, fda_h, bl_h, bf_h, bd_h,
    din, lout, sout, pout,
    x_own, g_own, ahead, back, from_before, from_after, pf, dfil, sf, lf, fh, fp, fd, fph, fdn, fda, bl, bf, bd,
    xs, gs, kf, vf, sp, sd, sh, ohi, olo, hi, lo, sx, fil, dpr, df,
    quart, qbuf, zsrc, zbuf, pbuf1, pbuf2, pbuf3, pone, ptwo, pthree,
    loads, own, halo_s, halo_r, line_s, line_r, z_s, z_r, epi_s, epi_r,
):
    me = lax.axis_index("ctx")
    count = lax.axis_size("ctx")
    tp = lax.axis_index("tp")
    after = {"ctx": lax.rem(me + 1, count)}
    before = {"ctx": lax.rem(me + count - 1, count)}
    core = lax.rem(me, 2)
    x = lax.rem(me // 2, 2)
    z = me // 4
    hx = tp // 4
    y = lax.rem(tp, 4)
    rows = x_hbm.shape[1]
    groups = x_own.shape[0]

    def at(zz, xx, cc, hh, yy):
        return {"ctx": zz * 4 + xx * 2 + cc, "tp": hh * 4 + yy}

    pair = at(z, x, 1 - core, hx, y)
    rings = [at(lax.rem(z + n, 8), x, core, hx, y) for n in range(1, 8)]
    columns = [at(z, x, core, hx, lax.rem(y + n, 4)) for n in range(1, 4)]
    line = [at(z, (x + n // 2) % 2, (core + n) % 2, (hx + n // 4) % 2, y) for n in range(1, 8)]

    def lanes_of(i):
        return pl.ds(pl.multiple_of(i * GROUP, GROUP), GROUP)

    def own_copies(i):
        return (
            pltpu.make_async_copy(x_hbm.at[:, :, lanes_of(i)], x_own.at[i], own.at[0, i]),
            pltpu.make_async_copy(g_hbm.at[:, lanes_of(i)], g_own.at[i], own.at[1, i]),
        )

    def remote(source, target, send, recv, other):
        return pltpu.make_async_remote_copy(
            src_ref=source, dst_ref=target, send_sem=send, recv_sem=recv, device_id=other, device_id_type=MESH
        )

    def halo_copies(i):
        return (
            remote(ahead.at[i], from_before.at[i], halo_s.at[0, i], halo_r.at[0, i], after),
            remote(back.at[i], from_after.at[i], halo_s.at[1, i], halo_r.at[1, i], before),
        )

    sources = (sf_hbm, lf_hbm, fh_h, fp_h, fd_h, fph_h, fdn_h, fda_h, bl_h, bf_h, bd_h)
    targets = (sf, lf, fh, fp, fd, fph, fdn, fda, bl, bf, bd)
    consts = [pltpu.make_async_copy(a, b, loads.at[n]) for n, (a, b) in enumerate(zip(sources, targets))]
    for copy in consts[:1]:
        copy.start()
    for copy in own_copies(0):
        copy.start()
    barrier = pltpu.get_barrier_semaphore()
    for other in [*rings, after, before, *columns, *line]:
        pl.semaphore_signal(barrier, inc=1, device_id=other, device_id_type=MESH)
    for copy in consts[1:5]:
        copy.start()
    for i in range(1, groups):
        for copy in own_copies(i):
            copy.start()
    for copy in consts[5:]:
        copy.start()
    consts[0].wait()
    inner = (me > 0).astype(f32)
    outer = (me < count - 1).astype(f32)

    def lanes_t(t):
        return pl.ds(128 * t, 128)

    def taps(i, t):
        lanes = pl.ds(pl.multiple_of(i * GROUP + 128 * t, 128), 128)
        return lambda s, n: sf[s, n : n + 1, lanes]

    def feature(i, t, s, start, size, tap):
        total = None
        for n in range(7):
            term = xs[i, s, t, pl.ds(start + NEAR - n, size), :] * tap(s, n)
            total = term if total is None else total + term
        return total

    def features(i, t, q_start, kv_start, size, p_slot, p_row, d_slot, d_row, tap, own_rows=False):
        lanes = pl.ds(128 * t, 128)
        p_hi, p_lo = p_slot
        d_hi, d_lo = d_slot
        key = feature(i, t, 1, kv_start, size, tap)
        value = feature(i, t, 2, kv_start, size, tap)
        kf[i, t, pl.ds(kv_start, size), :] = key
        vf[i, t, pl.ds(kv_start, size), :] = value
        product = key * value
        if own_rows:
            pf[t, pl.ds(p_row, size), :] = product
        high, low = split(product)
        p_hi[pl.ds(p_row, size), lanes] = high
        p_lo[pl.ds(p_row, size), lanes] = low
        query = feature(i, t, 0, q_start, size, tap)
        gradient = query * gs[i, t, pl.ds(q_start, size), :]
        if own_rows:
            dfil[t, pl.ds(d_row, size), :] = gradient
        high, low = split(gradient)
        d_hi[pl.ds(d_row, size), lanes] = high
        d_lo[pl.ds(d_row, size), lanes] = low

    def at_slot(slot):
        return hi.at[slot], lo.at[slot]

    def tripled(high, low):
        return jnp.concatenate([high, low, high], axis=0)

    def taken(slot, size):
        return tripled(hi[slot, 0:size, :], lo[slot, 0:size, :])

    def put(slot, start, value):
        high, low = split(value)
        hi[slot, start : start + value.shape[0], :] = high
        lo[slot, start : start + value.shape[0], :] = low

    def near(i):
        for copy in own_copies(i):
            copy.wait()
        for t in range(TILES):
            lanes = lanes_t(t)
            xs[i, 0, t, NEAR : NEAR + 256] = x_own[i, 0, :, lanes].astype(f32)
            for s in (1, 2):
                xs[i, s, t, EDGE : EDGE + 256] = x_own[i, s, :, lanes].astype(f32)
            gs[i, t, 0:256] = g_own[i, :, lanes].astype(f32)
        product = (ohi.at[i, 0], olo.at[i, 0])
        gradient = (ohi.at[i, 1], olo.at[i, 1])
        for t in range(TILES):
            tap = taps(i, t)
            for row in range(0, OWN, CHUNK):
                features(i, t, NEAR + row, EDGE + row, CHUNK, product, row, gradient, row, tap, True)
            lanes = lanes_t(t)
            code, most = coded(pf[t, OWN - FAR : OWN, :])
            ahead[i, 0:FAR, lanes] = code
            for n, parts in enumerate(((jnp.broadcast_to(most, (8, 128)), xs[i, 0, t, 264:272]), (xs[i, 1, t, 392:400], xs[i, 2, t, 392:400]))):
                ahead[i, FAR + NEAR * n : FAR + NEAR * (n + 1), lanes] = jnp.concatenate(parts, axis=0).astype(bf16)
            code, most = coded(dfil[t, 0:FAR, :])
            back[i, 0:FAR, lanes] = code
            back[i, FAR : FAR + NEAR, lanes] = x_own[i, 0, 0:NEAR, lanes]
            back[i, FAR + NEAR : FAR + 2 * NEAR, lanes] = g_own[i, 0:NEAR, lanes]
            back[i, FAR + 2 * NEAR : FAR + 3 * NEAR, lanes] = jnp.concatenate(
                [xs[i, 1, t, EDGE : EDGE + 8], xs[i, 2, t, EDGE : EDGE + 8]], axis=0
            ).astype(bf16)
            back[i, FAR + 3 * NEAR : BACK, lanes] = jnp.broadcast_to(most, (NEAR, 128)).astype(bf16)

    def spectra(i):
        for b in range(8):
            put(2, 16 * b, lf[16 * b : 16 * b + 16, lanes_of(i)])
        sh[i] = dot(fh[...], taken(2, 128))
        sp[i] = dot(fp[...], tripled(ohi[i, 0], olo[i, 0]))
        sd[i] = dot(fd[...], tripled(ohi[i, 1], olo[i, 1]))

    def send_halo(i):
        for copy in halo_copies(i):
            copy.start()

    def local(i, _):
        near(i)
        spectra(i - 1)
        send_halo(i)
        return 0

    near(0)
    pl.semaphore_wait(barrier, 19)
    send_halo(0)
    for copy in consts[1:5]:
        copy.wait()
    lax.fori_loop(1, groups, local, 0)
    spectra(groups - 1)
    for copy in consts[5:]:
        copy.wait()

    mine = core * 2 + x
    trio = [(at(z, (x + n // 2) % 2, (core + n) % 2, hx, y), (core + n) % 2 * 2 + (x + n // 2) % 2) for n in (3, 2, 1)]

    def line_copies(i):
        return [
            remote(quart.at[i, whose], qbuf.at[i, n], line_s.at[i, n], line_r.at[i, n], other)
            for n, (other, whose) in enumerate(trio)
        ]

    def z_copies(first, size):
        here = pl.ds(first, size)
        return [
            remote(
                zsrc.at[lax.rem(z + n + 1, 8), here], zbuf.at[n, here], z_s.at[first, n], z_r.at[first, n], rings[n]
            )
            for n in range(7)
        ]

    def after_line(i):
        for copy in line_copies(i):
            copy.wait()
        total = quart[i, mine] + qbuf[i, 0] + qbuf[i, 1] + qbuf[i, 2]
        long_power, long_most = powered(total[0:64])
        short_power, short_most = powered(total[64:88])
        spot = lax.broadcasted_iota(jnp.int32, (24, 128), 0)
        short_power = jnp.where(spot == 7, long_most, jnp.where(spot == 15, short_most, short_power))
        for n in range(8):
            parts = [long_power[4 * n : 4 * n + 4], long_power[32 + 4 * n : 36 + 4 * n], short_power]
            zsrc[n, i] = jnp.concatenate(parts, axis=0).astype(bf16)

    def group(i, top):
        for copy in halo_copies(i):
            copy.wait_recv()
        for t in range(TILES):
            lanes = lanes_t(t)
            tap = taps(i, t)
            edge = from_before[i, FAR : FAR + NEAR, lanes].astype(f32) * inner
            pmost = edge[0:1]
            xs[i, 0, t, 8:NEAR] = edge[8:NEAR]
            edge = from_before[i, FAR + NEAR : AHEAD, lanes].astype(f32) * inner
            xs[i, 1, t, FAR + 8 : EDGE] = edge[0:8]
            xs[i, 2, t, FAR + 8 : EDGE] = edge[8:NEAR]
            xs[i, 0, t, NEAR + 256 : 2 * NEAR + 256] = from_after[i, FAR : FAR + NEAR, lanes].astype(f32)
            gs[i, t, 256 : 256 + NEAR] = from_after[i, FAR + NEAR : FAR + 2 * NEAR, lanes].astype(f32) * outer
            edge = from_after[i, FAR + 2 * NEAR : FAR + 3 * NEAR, lanes].astype(f32)
            for s in (1, 2):
                xs[i, s, t, EDGE + 256 : EDGE + 264] = edge[8 * s - 8 : 8 * s]
                xs[i, s, t, EDGE + 264 : SIZE] = jnp.zeros((8, 128), f32)
            dmost = from_after[i, FAR + 3 * NEAR : BACK, lanes].astype(f32)[0:1] * outer
            for c in range(0, FAR, 32):
                high, low = split(decoded(from_before[i, c : c + 32, lanes], pmost))
                hi[0, c : c + 32, lanes] = high
                lo[0, c : c + 32, lanes] = low
                high, low = split(decoded(from_after[i, c : c + 32, lanes], dmost))
                hi[1, NEAR + c : NEAR + c + 32, lanes] = high
                lo[1, NEAR + c : NEAR + c + 32, lanes] = low
            features(i, t, 0, FAR, NEAR, at_slot(0), FAR, at_slot(2), 0, tap)
            features(i, t, 256, EDGE + OWN, NEAR, at_slot(0), EDGE, at_slot(1), 0, tap)
        sp[i] = sp[i] + dot(fph[...], taken(0, EDGE + NEAR))
        sd[i] = sd[i] + dot(fdn[...], taken(2, NEAR))
        sx[...] = sd[i] + dot(fda[...], taken(1, EDGE))

        row = lax.broadcasted_iota(jnp.int32, (8, GROUP), 0)
        for b in range(PAIRS):

            def two(ref, b=b):
                return ref[16 * b : 16 * b + 8, :], ref[16 * b + 8 : 16 * b + 16, :]

            pr, pi = two(sp.at[i])
            hr, him = two(sh.at[i])
            dr, di = two(sd.at[i])
            xr, xi = two(sx)

            def pack(same, cross_, re, im, sign, special=b == 0):
                if special:
                    real = re + sign * jnp.where(row == 0, 0.0, same)
                    imag = jnp.where(row == 0, same, im + cross_)
                else:
                    real = re + same if sign > 0 else re - same
                    imag = im + cross_
                return jnp.concatenate([real, imag], axis=0)

            put(0, 16 * b, pack(di * pi, -(di * pr), dr * pr, dr * pi, 1.0))
            put(1, 16 * b, pack(pi * him, pi * hr, pr * hr, pr * him, -1.0))
            put(2, 16 * b, pack(xi * him, xi * hr, xr * hr, -(xr * him), 1.0))

        long_sum = dot(bl[...], taken(0, SIZE))
        for n in range(4):
            for t in range(TILES):
                quart[i, n, 32 * t : 32 * t + 32] = long_sum[32 * n : 32 * n + 32, 128 * t : 128 * t + 128]
        fil[...] = dot(bf[...], taken(1, SIZE))
        dpr[...] = dot(bd[...], taken(2, SIZE))

        for t in range(TILES):
            lanes = pl.ds(128 * t, 128)
            df[0, t, 0:KEEP, :] = gs[i, t, 0:KEEP, :] * fil[:, lanes]
            df[1, t, 0:KEEP, :] = dpr[:, lanes] * vf[i, t, 128 : 128 + KEEP, :]
            df[2, t, 0:KEEP, :] = dpr[:, lanes] * kf[i, t, 128 : 128 + KEEP, :]

        for t in range(TILES):
            short = []
            for s in range(3):
                shift = NEAR if s == 0 else EDGE
                sums = [jnp.zeros((8, 128), f32)] * 7
                for base in range(0, 256, 64):
                    here = df[s, t, pl.ds(base, 64), :]
                    for n in range(7):
                        term = here * xs[i, s, t, pl.ds(base + shift - n, 64), :]
                        sums[n] = sums[n] + jnp.sum(term.reshape(8, 8, 128), axis=0)
                short += [jnp.sum(v, axis=0, keepdims=True) for v in sums] + [jnp.zeros((1, 128), f32)]
            for n in range(2):
                quart[i, 2 * t + n, 64:88] = jnp.concatenate(short, axis=0)
        for copy in line_copies(i):
            copy.start()

        for t in range(TILES):
            lanes = lanes_t(t)
            tap = taps(i, t)
            for s in range(3):
                for base in range(0, 256, 64):
                    total = None
                    for n in range(7):
                        term = df[s, t, pl.ds(base + n, 64), :] * tap(s, n)
                        total = term if total is None else total + term
                    din[i, s, pl.ds(base, 64), lanes] = total
                    top = jnp.maximum(top, jnp.max(jnp.abs(total).reshape(8, 8, 128), axis=0))
        return top

    top = lax.fori_loop(0, groups, group, jnp.zeros((8, 128), f32))

    def spread(source, slots, first, others):
        copies = [remote(source, slots.at[n], epi_s.at[first + n], epi_r.at[first + n], o) for n, o in enumerate(others)]
        for copy in copies:
            copy.start()
        return copies

    def gather(top, copies, slots):
        for copy in copies:
            copy.wait_recv()
        for n in range(len(copies)):
            top = jnp.maximum(top, slots[n])
        return top

    pone[...] = top
    ones = spread(pone, pbuf1, 0, rings)
    zs = [*z_copies(0, groups - 1), *z_copies(groups - 1, 1)]
    for i in range(groups):
        after_line(i)
        if i >= groups - 2:
            for copy in zs[7 * (i - groups + 2) : 7 * (i - groups + 3)]:
                copy.start()
    top = gather(top, ones, pbuf1)
    ptwo[...] = top
    twos = spread(ptwo, pbuf2, 7, line)
    top = gather(top, twos, pbuf2)
    pthree[...] = top
    threes = spread(pthree, pbuf3, 14, columns)
    for copy in zs:
        copy.wait_recv()
    for i in range(groups):
        long_sum, short_sum = 0.0, 0.0
        for n in range(8):
            block = (zsrc[z, i] if n == 7 else zbuf[n, i]).astype(f32)
            long_sum = long_sum + decoded(block[0:8], block[15:16])
            short_sum = short_sum + decoded(block[8:32], block[23:24])
        lout[:, GROUP * i : GROUP * i + 128] = long_sum[0:4]
        lout[:, GROUP * i + 128 : GROUP * (i + 1)] = long_sum[4:8]
        sout[core, i] = short_sum
    last = remote(sout.at[core], sout.at[core], epi_s.at[17], epi_r.at[17], pair)
    last.start()
    pout[...] = gather(top, threes, pbuf3)
    for copy in (*ones, *twos, *threes, *zs):
        copy.wait_send()
    for i in range(groups):
        for copy in halo_copies(i):
            copy.wait_send()
    last.wait()


def main(x3, cotangent, sf, lf):
    _, rows, chan = x3.shape
    consts = [jnp.asarray(c) for c in transforms()]
    groups = chan // GROUP
    anywhere = pl.BlockSpec(memory_space=pl.ANY)
    vmem = pl.BlockSpec(memory_space=pltpu.VMEM)
    V = pltpu.VMEM
    D = pltpu.SemaphoreType.DMA
    return pl.pallas_call(
        main_kernel,
        out_shape=[
            V((groups, 3, rows, GROUP), f32),
            V((4, chan), f32),
            V((2, groups, 24, 128), f32),
            V((8, 128), f32),
        ],
        in_specs=[anywhere] * (4 + len(consts)),
        out_specs=[vmem, vmem, vmem, vmem],
        scratch_shapes=[
            V((groups, 3, rows, GROUP), bf16),
            V((groups, rows, GROUP), bf16),
            V((groups, AHEAD, GROUP), bf16),
            V((groups, BACK, GROUP), bf16),
            V((groups, AHEAD, GROUP), bf16),
            V((groups, BACK, GROUP), bf16),
            V((TILES, OWN, 128), f32),
            V((TILES, OWN, 128), f32),
            V(sf.shape, f32),
            V(lf.shape, f32),
            *[V(c.shape, bf16) for c in consts],
            V((groups, 3, TILES, SIZE, 128), f32),
            V((groups, TILES, SPAN, 128), f32),
            V((groups, TILES, SPAN, 128), f32),
            V((groups, TILES, SPAN, 128), f32),
            V((groups, SIZE, GROUP), f32),
            V((groups, SIZE, GROUP), f32),
            V((groups, SIZE, GROUP), f32),
            V((groups, 2, OWN, GROUP), bf16),
            V((groups, 2, OWN, GROUP), bf16),
            V((3, SIZE, GROUP), bf16),
            V((3, SIZE, GROUP), bf16),
            V((SIZE, GROUP), f32),
            V((KEEP, GROUP), f32),
            V((KEEP, GROUP), f32),
            V((3, TILES, KEEP + 8, 128), f32),
            V((groups, 4, 88, 128), f32),
            V((groups, 3, 88, 128), f32),
            V((8, groups, 32, 128), bf16),
            V((7, groups, 32, 128), bf16),
            V((7, 8, 128), f32),
            V((7, 8, 128), f32),
            V((3, 8, 128), f32),
            V((8, 128), f32),
            V((8, 128), f32),
            V((8, 128), f32),
            D((11,)),
            D((2, groups)),
            D((2, groups)),
            D((2, groups)),
            D((groups, 3)),
            D((groups, 3)),
            D((groups, 7)),
            D((groups, 7)),
            D((18,)),
            D((18,)),
        ],
        compiler_params=pltpu.CompilerParams(
            collective_id=0, has_side_effects=True, vmem_limit_bytes=60 * 1024 * 1024
        ),
        name="gradients",
    )(x3, cotangent, sf, lf, *consts)


STEPS = 2


def scale_kernel(din, lsum, ssum, peak, out_hbm, lout, sout, scale, out, stores):
    groups, streams, rows, _ = din.shape
    step = rows // STEPS
    top = jnp.max(peak[...]) + EPSILON
    factor = FP8_RANGE / top
    copies = []
    for s in range(streams):
        for n in range(STEPS):
            here = pl.ds(n * step, step)
            for i in range(groups):
                out[s, here, GROUP * i : GROUP * (i + 1)] = (din[i, s, here, :] * factor).astype(bf16)
            copies.append(pltpu.make_async_copy(out.at[s, here], out_hbm.at[s, here], stores.at[s * STEPS + n]))
            copies[-1].start()
    scale[0, 0] = top / FP8_RANGE
    lout[...] = lsum[...]
    for c in range(2):
        for i in range(groups):
            lanes = pl.ds(GROUP * i + 128 * c, 128)
            for s in range(streams):
                sout[s, :, lanes] = ssum[c, i, 8 * s : 8 * s + 7]
    for copy in copies:
        copy.wait()


def scaled(din, lsum, ssum, peak):
    groups, _, rows, _ = din.shape
    chan = groups * GROUP
    vmem = pl.BlockSpec(memory_space=pltpu.VMEM)
    anywhere = pl.BlockSpec(memory_space=pl.ANY)
    din, lsum, ssum, peak = [pltpu.with_memory_space_constraint(a, pltpu.VMEM) for a in (din, lsum, ssum, peak)]
    return pl.pallas_call(
        scale_kernel,
        out_shape=[
            jax.ShapeDtypeStruct((3, rows, chan), bf16),
            jax.ShapeDtypeStruct((4, chan), f32),
            jax.ShapeDtypeStruct((3, 7, chan), f32),
            jax.ShapeDtypeStruct((1, 1), f32),
        ],
        in_specs=[vmem, vmem, vmem, vmem],
        out_specs=[anywhere, vmem, vmem, pl.BlockSpec(memory_space=pltpu.SMEM)],
        scratch_shapes=[pltpu.VMEM((3, rows, chan), bf16), pltpu.SemaphoreType.DMA((3 * STEPS,))],
        compiler_params=pltpu.CompilerParams(vmem_limit_bytes=32 * 1024 * 1024),
        name="scaling",
    )(din, lsum, ssum, peak)


def body(projected, cotangent, short_filter, long_filter):
    x3 = projected.transpose(1, 0, 2)
    sf = short_filter.transpose(1, 0, 2)
    out, long_grad, short_grad, scale = scaled(*main(x3, cotangent, sf, long_filter))
    return out.transpose(1, 0, 2), long_grad, short_grad.transpose(1, 0, 2), scale.reshape(())


def solution(mesh):
    placed = (P("ctx", None, "tp"), P("ctx", "tp"), P(None, None, "tp"), P(None, "tp"))
    return jax.shard_map(
        body,
        mesh=mesh,
        in_specs=placed,
        out_specs=(P("ctx", None, "tp"), P("ctx", "tp"), P(None, None, "tp"), P()),
        check_vma=False,
    )
```
